32 devices in a mesh: dp: 8 (over y, x, core), tensor: 4 (over z).
Axes of the slice: x: 2, y: 2, z: 4, core: 2. Of those that a mesh axis runs over, the one named last changes fastest.
Arguments:
- hidden_in: bfloat16 [16, 448, 768], P('dp', 'tensor'), may hold values from -6 to 6
- frames: bfloat16 [16, 1500, 768], P('dp'), may hold values from -6 to 6
- cotangent: bfloat16 [16, 448, 768], P('dp', 'tensor'), may hold values from -6 to 6
- segments: int32 [16, 448], P('dp'), may hold values from 0 to 3, never falling along the last dimension, each value on 1 to 224 neighbouring positions
- stamps: int32 [16, 448], P('dp'), may hold values 0 or 1
- owner_list: int32 [64], replicated, may hold values from 0 to 63, as said below
- master_tiles: float32 [4, 64, 192, 192], P('tensor', 'dp')
- tile_first: float32 [4, 64, 192, 192], P('tensor', 'dp')
- tile_second: float32 [4, 64, 192, 192], P('tensor', 'dp'), as said below
- tile_stats: float32 [4, 64, 2, 192, 192], P('tensor', 'dp'), as said below
- tile_bases: float32 [4, 64, 2, 192, 192], P('tensor', 'dp'), as said below
- master_vectors: float32 [14592], P('dp')
- vector_first: float32 [14592], P('dp')
- vector_second: float32 [14592], P('dp'), as said below
Outputs:
- block_out: float32 [16, 448, 768], P('dp', 'tensor')
- input_grad: float32 [16, 448, 768], P('dp', 'tensor')
- frames_grad: float32 [16, 1500, 768], P('dp', 'tensor')
- new_tiles: float32 [4, 64, 192, 192], P('tensor', 'dp')
- new_tile_first: float32 [4, 64, 192, 192], P('tensor', 'dp')
- new_tile_second: float32 [4, 64, 192, 192], P('tensor', 'dp')
- new_tile_stats: float32 [4, 64, 2, 192, 192], P('tensor', 'dp')
- new_tile_bases: float32 [4, 64, 2, 192, 192], P('tensor', 'dp')
- new_vectors: float32 [14592], P('dp')
- new_vector_first: float32 [14592], P('dp')
- new_vector_second: float32 [14592], P('dp')
The draws below stay inside these ranges and needn't reach their ends.
Inputs may be any that keep to these rules, and one draw needn't show every extreme that they name: `owner_list`: a permutation of 0 to 63. `tile_stats`: every statistics matrix is symmetric positive definite. `tile_bases`: every basis is orthogonal. `tile_second`: positive. `vector_second`: positive.
All inputs are finite; a program needn't handle non-finite values. No bound on the sum of `stamps` on one device may be relied on, other than what follows from the above.
Results may differ from the reference program's by a relative error of at most 0.015.
The reference program's roundings to bfloat16 on the way count: a program that leaves them out, or rounds other values in their place, can miss the bound.
Values may be sent and summed in bfloat16 or wider, within the bound.
No kernel may reach another device: no remote copies, remote signals or barrier semaphores. Data moves between devices by JAX's collectives and lax.ppermute only.
A program may use at most 192 MiB of HBM per device.

```python
import math
import jax
import jax.numpy as jnp
import numpy as np
from jax import lax

D = 768
HEAD = 64
FF = 3072
FRAMES = 1500
SEQ_LEN = 448
STEP = 5
NTILE = 64
SEQS = 16
TOKENS = 7168
TILE = 192
N_TENSOR = 4


def owner_order(key):
    return jax.random.permutation(jax.random.fold_in(key, 11), NTILE).astype(jnp.int32)


def tile_scale():
    return 0.3 * TOKENS ** 0.5


def vector_scale():
    return 0.5 * TOKENS ** 0.5


def draw_owner_list(key, part):
    return owner_order(key)


def draw_master_tiles(key, part):
    tile_ident = jnp.arange(NTILE)
    scale_ident = jnp.where(tile_ident < 24, D ** (-0.5), jnp.where(tile_ident < 32, 4.0 * D ** (-0.5), jnp.where(tile_ident < 48, D ** (-0.5), (4.0 * D) ** (-0.5))))
    scale_place = scale_ident[owner_order(key)]
    noise_key = jax.random.fold_in(key, 12)
    shape = (N_TENSOR, NTILE, TILE, TILE)
    noise = jax.random.normal(noise_key, shape, jnp.float32)
    return noise * scale_place[None, :, None, None]


def draw_tile_first(key, part):
    return jax.random.normal(key, (N_TENSOR, NTILE, TILE, TILE), jnp.float32) * (0.11 * tile_scale())


def draw_tile_second(key, part):
    level = jax.random.uniform(key, (N_TENSOR, NTILE, TILE, TILE), jnp.float32, minval=jnp.log(0.053), maxval=jnp.log(0.21))
    return jnp.exp(level) * tile_scale() ** 2


def draw_tile_stats(key, part):
    shape = (N_TENSOR, NTILE, 2, TILE, TILE)
    level_key = jax.random.fold_in(key, 1)
    diag_key = jax.random.fold_in(key, 2)
    noise_key = jax.random.fold_in(key, 3)
    level = jnp.exp(jax.random.uniform(level_key, (N_TENSOR, NTILE, 2, 1, 1), jnp.float32, minval=0.0, maxval=jnp.log(4.0))) * (0.053 * TILE * tile_scale() ** 2)
    diag_top = 2.0
    diagonal = jnp.exp(jax.random.uniform(diag_key, (N_TENSOR, NTILE, 2, TILE), jnp.float32, minval=0.0, maxval=jnp.log(diag_top)))
    random_part = jax.random.uniform(noise_key, shape, jnp.float32, minval=-1.0, maxval=1.0)
    symmetric = (random_part + jnp.swapaxes(random_part, -1, -2)) * 0.5
    identity = jnp.eye(TILE, dtype=jnp.float32)
    return level * (identity * diagonal[..., None] + symmetric * (0.49 / TILE ** 0.5) * (1.0 - identity))


def draw_tile_bases(key, part):
    shape = (N_TENSOR, NTILE, 2, TILE, TILE)
    spread = 0.6
    random_part = jax.random.normal(key, shape, jnp.float32) * (spread / TILE ** 0.5) + jnp.eye(TILE, dtype=jnp.float32)
    gram_matrix = jnp.einsum('...ki,...kj->...ij', random_part, random_part, precision=lax.Precision.HIGHEST)
    factor = jnp.linalg.cholesky(gram_matrix)
    solved = jax.scipy.linalg.solve_triangular(factor, jnp.swapaxes(random_part, -1, -2), lower=True)
    return jnp.swapaxes(solved, -1, -2)


def draw_master_vectors(key, part):
    length = 19 * D
    row_of = jnp.arange(length) // D
    is_gain = (row_of < 8) & (row_of % 2 == 0)
    gains = 1.0 + jax.random.uniform(jax.random.fold_in(key, 1), (length,), jnp.float32, minval=-0.3, maxval=0.3)
    shifts = jax.random.normal(jax.random.fold_in(key, 2), (length,), jnp.float32) * 0.2
    return jnp.where(is_gain, gains, shifts)


def draw_vector_first(key, part):
    return jax.random.normal(key, (19 * D,), jnp.float32) * (0.11 * vector_scale())


def draw_vector_second(key, part):
    level = jax.random.uniform(key, (19 * D,), jnp.float32, minval=jnp.log(0.053), maxval=jnp.log(0.21))
    return jnp.exp(level) * vector_scale() ** 2


def place_ends(drawn, key, least, largest):
    longest = drawn.shape.index(max(drawn.shape))
    spots = []
    for shift in (0, 1):
        where = [jax.random.randint(jax.random.fold_in(key, axis), (), 0, length) for axis, length in enumerate(drawn.shape)]
        where[longest] = (where[longest] + shift) % drawn.shape[longest]
        spots.append(tuple(where))
    return drawn.at[spots[0]].set(least).at[spots[1]].set(largest)


def shard_levels(stream_key, dims, split, low, high):
    factor_of, own = 1.0, jax.random.fold_in(stream_key, 6)
    for position, shards_of in split:
        draws = jnp.exp(jax.random.uniform(jax.random.fold_in(own, position), (shards_of,), jnp.float32, low / len(split), high / len(split)))
        factor_of = factor_of * jnp.repeat(draws, dims[position] // shards_of).reshape([-1 if axis == position else 1 for axis in range(len(dims))])
    return factor_of


def profile(count, total, limit, slope):
    weights = [(1 << 20) // math.isqrt(rank ** slope) + 1 for rank in range(2, count + 1)]
    spare, counts = total - limit - (count - 1), [1] * (count - 1)
    while spare > 0:
        movable = [i for i in range(count - 1) if counts[i] < limit]
        whole, left = sum([weights[i] for i in movable]), spare
        for i in movable:
            more = min(limit - counts[i], max(1, left * weights[i] // whole), spare)
            counts[i] = counts[i] + more
            spare = spare - more
    return np.array([limit] + counts)


def uneven_parts(key, count, total, most, lean):
    if count == 2:
        one = jax.random.randint(key, (), max(1, total - most), min(most, total - 1) + 1)
        return jnp.stack([one, total - one])
    tallies = jnp.asarray(profile(count, total, most, lean), jnp.int32)
    twos = (count - 1) // 2
    giver, sink = tallies[1:1 + 2 * twos:2], tallies[2:2 + 2 * twos:2]
    room = jnp.minimum(giver - 1, most - sink)
    passed = jax.random.randint(jax.random.fold_in(key, 1), (twos,), 0, 1 << 20) % (room + 1)
    tallies = tallies.at[1:1 + 2 * twos:2].set(giver - passed).at[2:2 + 2 * twos:2].set(sink + passed)
    return tallies[jax.random.permutation(jax.random.fold_in(key, 2), count)]


def bell_draw(key, extent, scale, most, cuts=(), kind=jnp.bfloat16):
    factor_of = shard_levels(key, extent, cuts, -0.22, 0.18) if cuts else 1.0
    drawn = jax.random.normal(key, extent, jnp.float32) * scale * factor_of
    return jnp.minimum(jnp.maximum(drawn, -most), most).astype(kind)


def setup_inputs(seed: int = 0) -> dict:
    streams_of = jax.random.split(jax.random.key(seed), 15)
    hidden_in = bell_draw(streams_of[0], (SEQS, SEQ_LEN, D), 1.0, 6.0, ((0, 8), (1, 4)))
    frames = bell_draw(streams_of[1], (SEQS, FRAMES, D), 1.0, 6.0, ((0, 8),))
    cotangent = bell_draw(streams_of[2], (SEQS, SEQ_LEN, D), 1.0, 6.0, ((0, 8), (1, 4)))
    segments = jax.vmap(lambda own: jnp.searchsorted(jnp.cumsum(uneven_parts(own, 4, SEQ_LEN, SEQ_LEN // 2, 0)), jnp.arange(SEQ_LEN), side="right"))(jax.random.split(streams_of[3], SEQS)).reshape((SEQS, SEQ_LEN)).astype(jnp.int32)
    stamps = place_ends((jax.random.randint(streams_of[4], (SEQS, SEQ_LEN), 0, 8) < 1).astype(jnp.int32), jax.random.fold_in(streams_of[4], 1), 0, 1)
    owner_list = draw_owner_list(jax.random.fold_in(streams_of[14], 71), 0)
    master_tiles = draw_master_tiles(jax.random.fold_in(streams_of[14], 71), 0)
    tile_first = draw_tile_first(jax.random.fold_in(streams_of[14], 71), 0)
    tile_second = draw_tile_second(jax.random.fold_in(streams_of[14], 71), 0)
    tile_stats = draw_tile_stats(jax.random.fold_in(streams_of[14], 71), 0)
    tile_bases = draw_tile_bases(jax.random.fold_in(streams_of[14], 71), 0)
    master_vectors = draw_master_vectors(jax.random.fold_in(streams_of[14], 71), 0)
    vector_first = draw_vector_first(jax.random.fold_in(streams_of[14], 71), 0)
    vector_second = draw_vector_second(jax.random.fold_in(streams_of[14], 71), 0)
    return dict(hidden_in=hidden_in, frames=frames, cotangent=cotangent, segments=segments, stamps=stamps, owner_list=owner_list, master_tiles=master_tiles, tile_first=tile_first, tile_second=tile_second, tile_stats=tile_stats, tile_bases=tile_bases, master_vectors=master_vectors, vector_first=vector_first, vector_second=vector_second)


@jax.custom_vjp
def low(v):
    return lax.optimization_barrier(v.astype(jnp.bfloat16)).astype(jnp.float32)

@jax.custom_vjp
def low_back(v):
    return v

def low_keep(v):
    return (low(v), None)

def low_pass(kept, grad):
    return (grad,)

def back_keep(v):
    return (v, None)

def back_low(kept, grad):
    return (low(grad),)
low.defvjp(low_keep, low_pass)
low_back.defvjp(back_keep, back_low)
highest = lax.Precision.HIGHEST
norm_eps = 1e-05
beta_one = 0.9
beta_two = 0.95
adam_eps = 1e-08
rate_tiles = 0.05
rate_vectors = 0.3
score_scale = 0.125

def rounded(values):
    return low_back(low(values))

def matmul(left_part, right_part):
    return jnp.dot(left_part.astype(jnp.float32), right_part.astype(jnp.float32), precision=highest, preferred_element_type=jnp.float32)

def layer_norm(values, gain, shift):
    centre = lax.optimization_barrier(jnp.mean(values, axis=-1, keepdims=True))
    centred = values - centre
    spread = lax.optimization_barrier(jnp.mean(centred * centred, axis=-1, keepdims=True))
    return centred * lax.rsqrt(spread + norm_eps) * gain + shift

def attend(queries, key_rows, value_rows, segment, stamp_flags, causal):
    length = queries.shape[0]
    key_count = key_rows.shape[0]
    block_rows = min(512, length)
    head_count = queries.shape[1] // HEAD
    key_heads = key_rows.reshape(key_count, head_count, HEAD)
    value_heads = value_rows.reshape(key_count, head_count, HEAD)
    query_blocks = queries.reshape(length // block_rows, block_rows, head_count, HEAD)
    offsets = jnp.arange(length // block_rows, dtype=jnp.int32) * block_rows

    def one_block(inputs):
        query_block, offset = inputs
        scores = low_back(jnp.einsum('qhd,khd->hqk', query_block, key_heads, precision=highest) * score_scale)
        if causal:
            query_pos = offset + jnp.arange(block_rows, dtype=jnp.int32)
            key_pos = jnp.arange(key_count, dtype=jnp.int32)
            query_seg = lax.dynamic_slice_in_dim(segment, offset, block_rows)
            allowed = (key_pos[None, :] <= query_pos[:, None]) & (segment[None, :] == query_seg[:, None]) & ((stamp_flags[None, :] == 0) | (key_pos[None, :] == query_pos[:, None]))
            scores = jnp.where(allowed[None], scores, -1e+30)
        row_max = lax.optimization_barrier(jnp.max(scores, axis=-1, keepdims=True))
        weights = jnp.exp(scores - row_max)
        attention = low(weights / lax.optimization_barrier(jnp.sum(weights, axis=-1, keepdims=True)))
        combined = jnp.einsum('hqk,khd->qhd', attention, value_heads, precision=highest)
        return combined.reshape(block_rows, head_count * HEAD)
    return lax.map(jax.checkpoint(one_block), (query_blocks, offsets)).reshape(length, head_count * HEAD)

def forward(tokens_in, frame_rows, matrices, vectors, segment, stamp_flags):
    query_weight, key_weight, value_weight, cross_query_weight, cross_key_weight, cross_value_weight, output_weight, cross_output_weight, inner_weight, outer_weight = matrices
    normed_one = low(layer_norm(tokens_in, vectors[0], vectors[1]))
    queries = rounded(matmul(normed_one, query_weight) + vectors[11])
    key_rows = rounded(matmul(normed_one, key_weight))
    value_rows = rounded(matmul(normed_one, value_weight) + vectors[12])
    attended = rounded(attend(queries, key_rows, value_rows, segment, stamp_flags, True))
    first_sum = tokens_in + low_back(matmul(attended, output_weight) + vectors[8])
    normed_two = low(layer_norm(first_sum, vectors[2], vectors[3]))
    cross_queries = rounded(matmul(normed_two, cross_query_weight) + vectors[13])
    cross_keys = rounded(matmul(frame_rows, cross_key_weight))
    cross_values = rounded(matmul(frame_rows, cross_value_weight) + vectors[14])
    cross_mixed = rounded(attend(cross_queries, cross_keys, cross_values, segment, stamp_flags, False))
    second_sum = first_sum + low_back(matmul(cross_mixed, cross_output_weight) + vectors[9])
    normed_three = low(layer_norm(second_sum, vectors[4], vectors[5]))
    upward = low_back(matmul(normed_three, inner_weight) + vectors[15:19].reshape(-1))
    active = low(jax.nn.gelu(upward, approximate=False))
    third_sum = second_sum + low_back(matmul(active, outer_weight) + vectors[10])
    return layer_norm(third_sum, vectors[6], vectors[7])

def tile_shapes(tile_side, model_width, hidden_units):
    return [(model_width, tile_side)] * 6 + [(tile_side, model_width)] * 2 + [(model_width, hidden_units), (hidden_units, model_width)]

def from_tiles(tiles, row_count, col_count):
    tile_side = tiles.shape[-1]
    return tiles.reshape(row_count // tile_side, col_count // tile_side, tile_side, tile_side).transpose(0, 2, 1, 3).reshape(row_count, col_count)

def to_tiles(matrix, tile_side):
    row_count, col_count = matrix.shape
    return matrix.reshape(row_count // tile_side, tile_side, col_count // tile_side, tile_side).transpose(0, 2, 1, 3).reshape(-1, tile_side, tile_side)

def local_matrices(tiles, model_width, hidden_units):
    tile_side = tiles.shape[-1]
    result = []
    offset = 0
    for row_count, col_count in tile_shapes(tile_side, model_width, hidden_units):
        number = row_count // tile_side * (col_count // tile_side)
        result.append(from_tiles(tiles[offset:offset + number], row_count, col_count))
        offset += number
    return result

def rotate(basis_left, middle, basis_right):
    inner = jnp.einsum('nji,njk->nik', basis_left, middle, precision=highest)
    return jnp.einsum('nij,njk->nik', inner, basis_right, precision=highest)

def orthonormal(matrix):
    gram_matrix = jnp.einsum('nki,nkj->nij', matrix, matrix, precision=highest)
    factor = jnp.linalg.cholesky(gram_matrix)
    solved = jax.scipy.linalg.solve_triangular(factor, jnp.swapaxes(matrix, -1, -2), lower=True)
    return jnp.swapaxes(solved, -1, -2)

def soap_update(gradient, master, first, second, statistics, bases):
    basis_left = bases[:, 0]
    basis_right = bases[:, 1]
    new_first = beta_one * first + (1.0 - beta_one) * gradient
    rotated = rotate(basis_left, gradient, basis_right)
    new_second = beta_two * second + (1.0 - beta_two) * rotated * rotated
    moment_rot = rotate(basis_left, new_first, basis_right) / (1.0 - beta_one ** STEP)
    normal_step = moment_rot / (jnp.sqrt(new_second / (1.0 - beta_two ** STEP)) + adam_eps)
    back_left = jnp.einsum('nij,njk->nik', basis_left, normal_step, precision=highest)
    update = jnp.einsum('nij,nkj->nik', back_left, basis_right, precision=highest)
    new_master = master - rate_tiles * update
    stats_left = beta_two * statistics[:, 0] + (1.0 - beta_two) * jnp.einsum('nij,nkj->nik', gradient, gradient, precision=highest)
    stats_right = beta_two * statistics[:, 1] + (1.0 - beta_two) * jnp.einsum('nji,njk->nik', gradient, gradient, precision=highest)
    new_left = orthonormal(jnp.einsum('nij,njk->nik', stats_left, basis_left, precision=highest))
    new_right = orthonormal(jnp.einsum('nij,njk->nik', stats_right, basis_right, precision=highest))
    return (new_first, new_second, new_master, jnp.stack([stats_left, stats_right], axis=1), jnp.stack([new_left, new_right], axis=1))

def reference(hidden_in, frames, cotangent, segments, stamps, owner_list, master_tiles, tile_first, tile_second, tile_stats, tile_bases, master_vectors, vector_first, vector_second):
    tile_side = master_tiles.shape[-1]
    hidden_units = FF // N_TENSOR
    low_tiles = lax.optimization_barrier(master_tiles.astype(jnp.bfloat16)).astype(jnp.float32)
    inverse = jnp.zeros((NTILE,), jnp.int32).at[owner_list].set(jnp.arange(NTILE, dtype=jnp.int32))
    by_ident = low_tiles[:, inverse]
    per_rank = [local_matrices(by_ident[tensor_rank], D, hidden_units) for tensor_rank in range(N_TENSOR)]
    join_axes = [1] * 6 + [0] * 2 + [1, 0]
    matrices = [jnp.concatenate([per_rank[tensor_rank][matrix_slot] for tensor_rank in range(N_TENSOR)], axis=join_axes[matrix_slot]) for matrix_slot in range(10)]
    vectors = lax.optimization_barrier(master_vectors.astype(jnp.bfloat16)).astype(jnp.float32).reshape(19, D)

    def per_sequence(carry, inputs):
        tokens_in, frame_rows, grad_out, segment, stamp_flags = inputs

        def run_layer(token_rows, frame_block, weight_list, vector_rows):
            return forward(token_rows, frame_block, weight_list, vector_rows, segment, stamp_flags)
        output, pullback = jax.vjp(run_layer, tokens_in, frame_rows, matrices, vectors)
        grad_tokens, grad_frames, grad_mats, grad_vecs = pullback(grad_out)
        summed = (jax.tree.map(jnp.add, carry[0], grad_mats), carry[1] + grad_vecs)
        return (summed, (output, grad_tokens, grad_frames))
    start_carry = ([jnp.zeros_like(matrix) for matrix in matrices], jnp.zeros_like(vectors))
    (grad_mats, grad_vecs), (outputs, grad_tokens, grad_frames) = lax.scan(per_sequence, start_carry, (hidden_in.astype(jnp.float32), frames.astype(jnp.float32), cotangent.astype(jnp.float32), segments, stamps))
    rank_tiles = []
    for tensor_rank in range(N_TENSOR):
        pieces = []
        for matrix_slot in range(10):
            full_grad = grad_mats[matrix_slot]
            shard_len = full_grad.shape[join_axes[matrix_slot]] // N_TENSOR
            shard_grad = lax.slice_in_dim(full_grad, tensor_rank * shard_len, (tensor_rank + 1) * shard_len, axis=join_axes[matrix_slot])
            pieces.append(to_tiles(shard_grad, tile_side))
        rank_tiles.append(jnp.concatenate(pieces, axis=0))
    grad_tiles = jnp.stack(rank_tiles)[:, owner_list]
    count_all = N_TENSOR * NTILE
    flat_shape = (count_all, tile_side, tile_side)
    pair_shape = (count_all, 2, tile_side, tile_side)
    new_first, new_second, new_master, new_stats, new_bases = soap_update(grad_tiles.reshape(flat_shape), master_tiles.reshape(flat_shape), tile_first.reshape(flat_shape), tile_second.reshape(flat_shape), tile_stats.reshape(pair_shape), tile_bases.reshape(pair_shape))
    vector_grad = grad_vecs.reshape(-1)
    new_vector_first = beta_one * vector_first + (1.0 - beta_one) * vector_grad
    new_vector_second = beta_two * vector_second + (1.0 - beta_two) * vector_grad * vector_grad
    new_vectors = master_vectors - rate_vectors * (new_vector_first / (1.0 - beta_one ** STEP)) / (jnp.sqrt(new_vector_second / (1.0 - beta_two ** STEP)) + adam_eps)
    tile_shape = (N_TENSOR, NTILE, tile_side, tile_side)
    stack_shape = (N_TENSOR, NTILE, 2, tile_side, tile_side)
    return (outputs, grad_tokens, grad_frames, new_master.reshape(tile_shape), new_first.reshape(tile_shape), new_second.reshape(tile_shape), new_stats.reshape(stack_shape), new_bases.reshape(stack_shape), new_vectors, new_vector_first, new_vector_second)
```

```python
import functools

import jax
import jax.numpy as jnp
from jax import lax
from jax.experimental import pallas as pl
from jax.experimental.pallas import tpu as pltpu
from jax.sharding import PartitionSpec as P

HEAD = 64
FF = 3072
STEP = 5


highest = lax.Precision.HIGHEST
norm_eps = 1e-05
beta_one = 0.9
beta_two = 0.95
adam_eps = 1e-08
rate_tiles = 0.05
rate_vectors = 0.3
score_scale = 0.125


def product(left_part, right_part):
    return jnp.dot(left_part, right_part, preferred_element_type=jnp.float32)


def times_transpose(left_part, right_part):
    return jnp.einsum("rn,kn->rk", left_part, right_part, preferred_element_type=jnp.float32)


def weight_grad(inputs, grads):
    return jnp.einsum("rk,rn->kn", inputs, grads, preferred_element_type=jnp.float32)


def flatten_rows(values):
    return values.reshape(-1, values.shape[-1])


def normalize(values, gain, shift):
    centre = jnp.mean(values, axis=-1, keepdims=True)
    centred = values - centre
    inverse = lax.rsqrt(jnp.mean(centred * centred, axis=-1, keepdims=True) + norm_eps)
    return centred * inverse * gain + shift


def normalize_back(values, gain, grads):
    centre = jnp.mean(values, axis=-1, keepdims=True)
    centred = values - centre
    inverse = lax.rsqrt(jnp.mean(centred * centred, axis=-1, keepdims=True) + norm_eps)
    unit_rows = centred * inverse
    scaled = grads * gain
    result = inverse * (
        scaled
        - jnp.mean(scaled, axis=-1, keepdims=True)
        - unit_rows * jnp.mean(scaled * unit_rows, axis=-1, keepdims=True)
    )
    return (result, jnp.sum(grads * unit_rows, axis=(0, 1)), jnp.sum(grads, axis=(0, 1)))


def tile_shapes(tile_side, model_width, hidden_units):
    return (
        [(model_width, tile_side)] * 6
        + [(tile_side, model_width)] * 2
        + [(model_width, hidden_units), (hidden_units, model_width)]
    )


def from_tiles(tiles, row_count, col_count):
    tile_side = tiles.shape[-1]
    return (
        tiles.reshape(row_count // tile_side, col_count // tile_side, tile_side, tile_side)
        .transpose(0, 2, 1, 3)
        .reshape(row_count, col_count)
    )


def to_tiles(matrix, tile_side):
    row_count, col_count = matrix.shape
    return (
        matrix.reshape(row_count // tile_side, tile_side, col_count // tile_side, tile_side)
        .transpose(0, 2, 1, 3)
        .reshape(-1, tile_side, tile_side)
    )


def local_matrices(tiles, model_width, hidden_units):
    tile_side = tiles.shape[-1]
    result = []
    offset = 0
    for row_count, col_count in tile_shapes(tile_side, model_width, hidden_units):
        number = row_count // tile_side * (col_count // tile_side)
        result.append(from_tiles(tiles[offset : offset + number], row_count, col_count))
        offset += number
    return result


def block_scores(query_block, key_heads, mask_rule, sequence, offset, block_rows):
    scores = (
        jnp.einsum("qhd,khd->hqk", query_block, key_heads, preferred_element_type=jnp.float32)
        * score_scale
    )
    if mask_rule is None:
        return scores
    return jnp.where(mask_rule(sequence, offset, block_rows)[None], scores, -1e30)


def attend_forward(queries, key_rows, value_rows, mask_rule):
    seq_count, length, span_width = queries.shape
    head_count = span_width // HEAD
    block_rows = min(512, length)
    per_sequence = length // block_rows

    def one_block(position):
        sequence = position // per_sequence
        offset = position % per_sequence * block_rows
        query_block = queries[sequence].reshape(block_rows, head_count, HEAD)
        key_heads = key_rows[sequence].reshape(-1, head_count, HEAD)
        value_heads = value_rows[sequence].reshape(-1, head_count, HEAD)
        scores = block_scores(query_block, key_heads, mask_rule, sequence, offset, block_rows)
        row_max = jnp.max(scores, axis=-1, keepdims=True)
        weights = jnp.exp(scores - row_max)
        row_total = jnp.sum(weights, axis=-1, keepdims=True)
        attention = (weights / row_total).astype(jnp.bfloat16)
        combined = jnp.einsum(
            "hqk,khd->qhd", attention, value_heads, preferred_element_type=jnp.float32
        )
        return (
            combined.reshape(block_rows, span_width).astype(jnp.bfloat16),
            (row_max + jnp.log(row_total))[..., 0],
        )

    combined, log_totals = lax.map(one_block, jnp.arange(seq_count * per_sequence, dtype=jnp.int32))
    return (combined, log_totals)


def attend_backward(queries, key_rows, value_rows, grad_out, log_totals, mask_rule):
    seq_count, length, span_width = queries.shape
    head_count = span_width // HEAD
    block_rows = min(512, length)
    per_sequence = length // block_rows
    key_count = key_rows.shape[1]

    def one_block(position):
        sequence = position // per_sequence
        offset = position % per_sequence * block_rows
        query_block = queries[sequence].reshape(block_rows, head_count, HEAD)
        grad_block = grad_out[sequence].reshape(block_rows, head_count, HEAD)
        key_heads = key_rows[sequence].reshape(-1, head_count, HEAD)
        value_heads = value_rows[sequence].reshape(-1, head_count, HEAD)
        scores = block_scores(query_block, key_heads, mask_rule, sequence, offset, block_rows)
        attention = jnp.exp(scores - log_totals[position][..., None])
        grad_attention = jnp.einsum(
            "qhd,khd->hqk", grad_block, value_heads, preferred_element_type=jnp.float32
        )
        row_dot = jnp.sum(attention * grad_attention, axis=-1, keepdims=True)
        grad_scores = (attention * (grad_attention - row_dot)).astype(jnp.bfloat16)
        grad_query = (
            jnp.einsum("hqk,khd->qhd", grad_scores, key_heads, preferred_element_type=jnp.float32)
            * score_scale
        )
        grad_key = (
            jnp.einsum("hqk,qhd->khd", grad_scores, query_block, preferred_element_type=jnp.float32)
            * score_scale
        )
        grad_value = jnp.einsum(
            "hqk,qhd->khd",
            attention.astype(jnp.bfloat16),
            grad_block,
            preferred_element_type=jnp.float32,
        )
        return (
            grad_query.reshape(block_rows, span_width).astype(jnp.bfloat16),
            grad_key.reshape(-1, span_width),
            grad_value.reshape(-1, span_width),
        )

    grad_query, grad_key, grad_value = lax.map(
        one_block, jnp.arange(seq_count * per_sequence, dtype=jnp.int32)
    )
    grad_key = (
        grad_key.reshape(seq_count, per_sequence, key_count, span_width)
        .sum(axis=1)
        .astype(jnp.bfloat16)
    )
    grad_value = (
        grad_value.reshape(seq_count, per_sequence, key_count, span_width)
        .sum(axis=1)
        .astype(jnp.bfloat16)
    )
    return (grad_query, grad_key, grad_value)


HI = lax.Precision.HIGHEST

def split2(a):
    hi = a.astype(jnp.bfloat16)
    lo = (a - hi.astype(jnp.float32)).astype(jnp.bfloat16)
    return hi, lo

def bdot(a, b, dims):
    return lax.dot_general(a, b, (dims, ((), ())), preferred_element_type=jnp.float32)

NN = ((1,), (0,)); TN = ((0,), (0,)); NT = ((1,), (1,))

def dot3(a, b, dims):
    (ah, al), (bh, bl) = a, b
    return bdot(ah, bh, dims) + (bdot(ah, bl, dims) + bdot(al, bh, dims))

def dothi(a, b, dims):
    return lax.dot_general(a, b, (dims, ((), ())), precision=HI, preferred_element_type=jnp.float32)

def soap_pre_kernel(first, stats, bases, rot_first, stats_rot):
    ql, qr = split2(bases[0, 0]), split2(bases[0, 1])
    inner = split2(dot3(ql, split2(first[0]), TN))
    rot_first[0] = dot3(inner, qr, NN)
    stats_rot[0, 0] = dot3(split2(stats[0, 0]), ql, NN)
    stats_rot[0, 1] = dot3(split2(stats[0, 1]), qr, NN)

def soap_main_kernel(grad, master, first, second, stats, bases, rot_first, stats_rot,
                     new_master, new_first, new_second, new_stats, turned, grams):
    g32 = grad[0].astype(jnp.float32)
    g, ql, qr = split2(g32), split2(bases[0, 0]), split2(bases[0, 1])
    new_first[0] = beta_one * first[0] + (1.0 - beta_one) * g32
    part_left = split2(dot3(ql, g, TN))
    rotated = dot3(part_left, qr, NN)
    fresh = beta_two * second[0] + (1.0 - beta_two) * rotated * rotated
    new_second[0] = fresh
    moment = (beta_one * rot_first[0] + (1.0 - beta_one) * rotated) / (1.0 - beta_one**STEP)
    step = moment / (jnp.sqrt(fresh / (1.0 - beta_two**STEP)) + adam_eps)
    back = split2(dot3(ql, split2(step), NN))
    new_master[0] = master[0] - rate_tiles * dot3(back, qr, NT)
    new_stats[0, 0] = beta_two * stats[0, 0] + (1.0 - beta_two) * dot3(g, g, NT)
    new_stats[0, 1] = beta_two * stats[0, 1] + (1.0 - beta_two) * dot3(g, g, TN)
    part_right = split2(dot3(g, qr, NN))
    for side, term in ((0, dot3(g, part_left, NT)), (1, dot3(g, part_right, TN))):
        side_turned = beta_two * stats_rot[0, side] + (1.0 - beta_two) * term
        turned[0, side] = side_turned
        halves = split2(side_turned)
        grams[0, side] = dot3(halves, halves, TN)

def chol_kernel(turned, grams, out, work, inv, fac, *, block):
    count, side = work.shape[0], work.shape[1]
    row = lax.broadcasted_iota(jnp.int32, (side, side), 0)
    col = lax.broadcasted_iota(jnp.int32, (side, side), 1)
    eye = (row == col).astype(jnp.float32)
    for m in range(count):
        work[m] = grams[m]
        inv[m] = eye
    brow = lax.broadcasted_iota(jnp.int32, (count, block, 2 * block), 1)
    bcol = lax.broadcasted_iota(jnp.int32, (count, block, 2 * block), 2)
    aug_eye = ((bcol - block) == brow).astype(jnp.float32)
    for k in range(side // block):
        lo = k * block
        diag = work[:, lo : lo + block, lo : lo + block]
        w = jnp.concatenate([diag, jnp.zeros_like(diag)], axis=2) + aug_eye
        for j in range(block - 1):
            piv = w[:, j : j + 1, :]
            ratio = w[:, :, j : j + 1] / w[:, j : j + 1, j : j + 1]
            w = w - jnp.where(brow > j, ratio * piv, 0.0)
        d = jnp.sum(jnp.where(brow == bcol, w, 0.0), axis=2, keepdims=True)
        fac[...] = w[:, :, block:] * lax.rsqrt(d)

        def one(m, _):
            x = fac[m]
            y = dothi(x, work[m, lo : lo + block, :], NN)
            z = dothi(x, inv[m, lo : lo + block, :], NN)
            inv[m, lo : lo + block, :] = z
            if lo + block < side:
                rest = side - lo - block
                ys = split2(y)
                upd = dothi(y, y, TN)
                updx = dothi(y, z, TN)
                work[m, lo + block :, :] = work[m, lo + block :, :] - upd[lo + block :, :]
                inv[m, lo + block :, :] = inv[m, lo + block :, :] - updx[lo + block :, :]
            return 0
        lax.fori_loop(0, count, one, 0)

    def last(m, _):
        out[m] = dothi(turned[m], inv[m], NT)
        return 0
    lax.fori_loop(0, count, last, 0)

def tile_spec(side):
    return pl.BlockSpec((1, side, side), lambda i: (i, 0, 0))
def pair_spec(side):
    return pl.BlockSpec((1, 2, side, side), lambda i: (i, 0, 0, 0))

def soap_pre(first, stats, bases):
    n, side = first.shape[0], first.shape[1]
    t, p = tile_spec(side), pair_spec(side)
    return pl.pallas_call(soap_pre_kernel, grid=(n,), in_specs=[t, p, p], out_specs=[t, p],
        out_shape=[jax.ShapeDtypeStruct(first.shape, jnp.float32), jax.ShapeDtypeStruct(stats.shape, jnp.float32)],
        name="soap_pre")(first, stats, bases)

def soap_main(grad, master, first, second, stats, bases, rot_first, stats_rot):
    n, side = first.shape[0], first.shape[1]
    t, p = tile_spec(side), pair_spec(side)
    f = jnp.float32
    ts, ps = jax.ShapeDtypeStruct(first.shape, f), jax.ShapeDtypeStruct(stats.shape, f)
    return pl.pallas_call(soap_main_kernel, grid=(n,), in_specs=[t, t, t, t, p, p, t, p],
        out_specs=[t, t, t, p, p, p], out_shape=[ts, ts, ts, ps, ps, ps], name="soap_main")(
        grad, master, first, second, stats, bases, rot_first, stats_rot)

def chol_bases(turned, grams, block=32):
    n, _, side, _ = turned.shape
    shape = (2 * n, side, side)
    out = pl.pallas_call(functools.partial(chol_kernel, block=block),
        out_shape=jax.ShapeDtypeStruct(shape, jnp.float32),
        scratch_shapes=[pltpu.VMEM(shape, jnp.float32), pltpu.VMEM(shape, jnp.float32), pltpu.VMEM((2*n, block, block), jnp.float32)],
        compiler_params=pltpu.CompilerParams(vmem_limit_bytes=48 * 2**20), name="chol_bases")(
        turned.reshape(shape), grams.reshape(shape))
    return out.reshape(turned.shape)

def soap(gradient, master, first, second, statistics, bases, block=32):
    rot_first, stats_rot = soap_pre(first, statistics, bases)
    nm, nf, ns, nst, turned, grams = soap_main(gradient, master, first, second, statistics, bases, rot_first, stats_rot)
    return nf, ns, nm, nst, chol_bases(turned, grams, block)


def permute_kernel(order, source, result):
    result[...] = source[...]


def permute_tiles(tiles, order):
    count, side = tiles.shape[0], tiles.shape[-1]
    return pl.pallas_call(
        permute_kernel,
        grid_spec=pltpu.PrefetchScalarGridSpec(
            num_scalar_prefetch=1,
            grid=(count,),
            in_specs=[pl.BlockSpec((1, side, side), lambda i, order: (order[i], 0, 0))],
            out_specs=pl.BlockSpec((1, side, side), lambda i, order: (i, 0, 0)),
        ),
        out_shape=jax.ShapeDtypeStruct(tiles.shape, tiles.dtype),
        name="permute_tiles",
    )(order, tiles)


def shards(
    hidden_in,
    frames,
    cotangent,
    segments,
    stamps,
    owner_list,
    master_tiles,
    tile_first,
    tile_second,
    tile_stats,
    tile_bases,
    master_vectors,
    vector_first,
    vector_second,
):
    tensor_count = lax.axis_size("tensor")
    tensor_rank = lax.axis_index("tensor")
    seq_count, local_rows, model_width = hidden_in.shape
    full_rows = local_rows * tensor_count
    tile_side = master_tiles.shape[-1]
    hidden_units = FF // tensor_count
    tile_count = owner_list.shape[0]
    inverse = (
        jnp.zeros((tile_count,), jnp.int32)
        .at[owner_list]
        .set(jnp.arange(tile_count, dtype=jnp.int32))
    )
    gathered = lax.all_gather(master_tiles[0].astype(jnp.bfloat16), "dp", axis=0, tiled=True)
    by_ident = permute_tiles(gathered, inverse)
    (
        query_weight,
        key_weight,
        value_weight,
        cross_query_weight,
        cross_key_weight,
        cross_value_weight,
        output_weight,
        cross_output_weight,
        inner_weight,
        outer_weight,
    ) = local_matrices(by_ident, model_width, hidden_units)
    vectors = (
        lax.all_gather(master_vectors.astype(jnp.bfloat16), "dp", axis=0, tiled=True)
        .astype(jnp.float32)
        .reshape(19, model_width)
    )
    head_bias = lax.dynamic_slice_in_dim(vectors[11:15], tensor_rank * tile_side, tile_side, 1)
    inner_bias = lax.dynamic_index_in_dim(vectors[15:19], tensor_rank, 0, keepdims=False)

    def causal_mask(sequence, offset, block_rows):
        segment = segments[sequence]
        stamp_flags = stamps[sequence]
        query_pos = offset + jnp.arange(block_rows, dtype=jnp.int32)
        key_pos = jnp.arange(segment.shape[0], dtype=jnp.int32)
        return (
            (key_pos[None, :] <= query_pos[:, None])
            & (segment[None, :] == segment[:, None])
            & ((stamp_flags[None, :] == 0) | (key_pos[None, :] == query_pos[:, None]))
        )

    def spread(values):
        return lax.all_gather(values, "tensor", axis=1, tiled=True)

    def enter_branch(values):
        return spread(values)

    def leave_branch(partial_sum):
        return lax.psum_scatter(partial_sum, "tensor", scatter_dimension=1, tiled=True)

    def frame_projection():
        frame_flat = flatten_rows(frames)
        key_part = (
            product(frame_flat, cross_key_weight)
            .astype(jnp.bfloat16)
            .reshape(seq_count, -1, tile_side)
        )
        value_part = (
            (product(frame_flat, cross_value_weight) + head_bias[3])
            .astype(jnp.bfloat16)
            .reshape(seq_count, -1, tile_side)
        )
        return (key_part, value_part)

    residual = hidden_in.astype(jnp.float32)
    top_grad = cotangent.astype(jnp.float32)
    shared_share = jnp.float32(1.0)
    wide_shape = (seq_count, full_rows, model_width)
    normed_one = enter_branch(normalize(residual, vectors[0], vectors[1]).astype(jnp.bfloat16))
    normed_flat = flatten_rows(normed_one)
    queries = (
        (product(normed_flat, query_weight) + head_bias[0])
        .astype(jnp.bfloat16)
        .reshape(seq_count, full_rows, tile_side)
    )
    key_rows = (
        product(normed_flat, key_weight)
        .astype(jnp.bfloat16)
        .reshape(seq_count, full_rows, tile_side)
    )
    value_rows = (
        (product(normed_flat, value_weight) + head_bias[1])
        .astype(jnp.bfloat16)
        .reshape(seq_count, full_rows, tile_side)
    )
    attended, log_self = attend_forward(queries, key_rows, value_rows, causal_mask)
    first_sum = (
        residual
        + leave_branch(product(flatten_rows(attended), output_weight).reshape(wide_shape))
        + vectors[8]
    )
    normed_two = enter_branch(normalize(first_sum, vectors[2], vectors[3]).astype(jnp.bfloat16))
    cross_queries = (
        (product(flatten_rows(normed_two), cross_query_weight) + head_bias[2])
        .astype(jnp.bfloat16)
        .reshape(seq_count, full_rows, tile_side)
    )
    cross_keys, cross_values = frame_projection()
    cross_mixed, log_cross = attend_forward(cross_queries, cross_keys, cross_values, None)
    second_sum = (
        first_sum
        + leave_branch(product(flatten_rows(cross_mixed), cross_output_weight).reshape(wide_shape))
        + vectors[9]
    )
    normed_three = enter_branch(normalize(second_sum, vectors[4], vectors[5]).astype(jnp.bfloat16))
    upward = product(flatten_rows(normed_three), inner_weight) + inner_bias
    active = jax.nn.gelu(upward, approximate=False).astype(jnp.bfloat16)
    third_sum = (
        second_sum + leave_branch(product(active, outer_weight).reshape(wide_shape)) + vectors[10]
    )
    block_out = normalize(third_sum, vectors[6], vectors[7])
    grad_third, final_gain_grad, final_shift_grad = normalize_back(third_sum, vectors[6], top_grad)
    branch_three = grad_third.astype(jnp.bfloat16)
    full_three = flatten_rows(enter_branch(branch_three))
    outer_bias_grad = jnp.sum(branch_three.astype(jnp.float32), axis=(0, 1))
    outer_weight_grad = weight_grad(active, full_three)
    grad_active = times_transpose(full_three, outer_weight)
    _, gelu_back = jax.vjp(lambda inner_value: jax.nn.gelu(inner_value, approximate=False), upward)
    grad_up = gelu_back(grad_active)[0].astype(jnp.bfloat16)
    inner_bias_grad = jnp.sum(grad_up.astype(jnp.float32), axis=0)
    inner_weight_grad = weight_grad(flatten_rows(normed_three), grad_up)
    grad_normed_three = leave_branch(times_transpose(grad_up, inner_weight).reshape(wide_shape))
    back_three, inner_gain_grad, inner_shift_grad = normalize_back(
        second_sum, vectors[4], grad_normed_three
    )
    grad_second = grad_third + back_three
    branch_two = grad_second.astype(jnp.bfloat16)
    full_two = flatten_rows(enter_branch(branch_two))
    cross_out_bias_grad = jnp.sum(branch_two.astype(jnp.float32), axis=(0, 1))
    cross_output_grad = weight_grad(flatten_rows(cross_mixed), full_two)
    grad_cross_mixed = (
        times_transpose(full_two, cross_output_weight)
        .astype(jnp.bfloat16)
        .reshape(seq_count, full_rows, tile_side)
    )
    keys_back, values_back = frame_projection()
    grad_cross_query, grad_cross_key, grad_cross_value = attend_backward(
        cross_queries, keys_back, values_back, grad_cross_mixed, log_cross, None
    )
    cross_query_bias_grad = jnp.sum(grad_cross_query.astype(jnp.float32), axis=(0, 1))
    cross_value_bias_grad = jnp.sum(grad_cross_value.astype(jnp.float32), axis=(0, 1))
    frame_flat = flatten_rows(frames)
    cross_query_grad = weight_grad(flatten_rows(normed_two), flatten_rows(grad_cross_query))
    cross_key_grad = weight_grad(frame_flat, flatten_rows(grad_cross_key))
    cross_value_grad = weight_grad(frame_flat, flatten_rows(grad_cross_value))
    part_normed_two = times_transpose(flatten_rows(grad_cross_query), cross_query_weight).reshape(
        wide_shape
    )
    part_frames = (
        times_transpose(flatten_rows(grad_cross_key), cross_key_weight)
        + times_transpose(flatten_rows(grad_cross_value), cross_value_weight)
    ).reshape(seq_count, -1, model_width)
    grad_normed_two, frames_grad = (
        lax.psum_scatter(part_normed_two, "tensor", scatter_dimension=1, tiled=True),
        lax.psum_scatter(part_frames, "tensor", scatter_dimension=1, tiled=True),
    )
    back_two, cross_gain_grad, cross_shift_grad = normalize_back(
        first_sum, vectors[2], grad_normed_two
    )
    grad_first = grad_second + back_two
    branch_one = grad_first.astype(jnp.bfloat16)
    full_one = flatten_rows(enter_branch(branch_one))
    self_out_bias_grad = jnp.sum(branch_one.astype(jnp.float32), axis=(0, 1))
    output_weight_grad = weight_grad(flatten_rows(attended), full_one)
    grad_attended = (
        times_transpose(full_one, output_weight)
        .astype(jnp.bfloat16)
        .reshape(seq_count, full_rows, tile_side)
    )
    grad_query, grad_key, grad_value = attend_backward(
        queries, key_rows, value_rows, grad_attended, log_self, causal_mask
    )
    query_bias_grad = jnp.sum(grad_query.astype(jnp.float32), axis=(0, 1))
    value_bias_grad = jnp.sum(grad_value.astype(jnp.float32), axis=(0, 1))
    query_weight_grad = weight_grad(normed_flat, flatten_rows(grad_query))
    key_weight_grad = weight_grad(normed_flat, flatten_rows(grad_key))
    value_weight_grad = weight_grad(normed_flat, flatten_rows(grad_value))
    part_normed_one = (
        times_transpose(flatten_rows(grad_query), query_weight)
        + times_transpose(flatten_rows(grad_key), key_weight)
        + times_transpose(flatten_rows(grad_value), value_weight)
    ).reshape(wide_shape)
    grad_normed_one = leave_branch(part_normed_one)
    back_one, self_gain_grad, self_shift_grad = normalize_back(
        residual, vectors[0], grad_normed_one
    )
    input_grad = grad_first + back_one
    weight_grads = [
        query_weight_grad,
        key_weight_grad,
        value_weight_grad,
        cross_query_grad,
        cross_key_grad,
        cross_value_grad,
        output_weight_grad,
        cross_output_grad,
        inner_weight_grad,
        outer_weight_grad,
    ]
    tile_terms = jnp.concatenate(
        [to_tiles(grad_item, tile_side) for grad_item in weight_grads], axis=0
    )
    tile_terms = permute_tiles(tile_terms, owner_list)
    owned_grads = lax.psum_scatter(tile_terms, "dp", scatter_dimension=0, tiled=True)
    shared_rows = (
        jnp.stack(
            [
                self_gain_grad,
                self_shift_grad,
                cross_gain_grad,
                cross_shift_grad,
                inner_gain_grad,
                inner_shift_grad,
                final_gain_grad,
                final_shift_grad,
                self_out_bias_grad,
                cross_out_bias_grad,
                outer_bias_grad,
            ]
        )
        * shared_share
    )
    head_rows = lax.dynamic_update_slice(
        jnp.zeros((4, model_width), jnp.float32),
        jnp.stack([query_bias_grad, value_bias_grad, cross_query_bias_grad, cross_value_bias_grad]),
        (0, tensor_rank * tile_side),
    )
    inner_rows = lax.dynamic_update_slice(
        jnp.zeros((4, model_width), jnp.float32), inner_bias_grad[None], (tensor_rank, 0)
    )
    vector_terms = jnp.concatenate([shared_rows, head_rows, inner_rows], axis=0).reshape(-1)
    owned_vector_terms = lax.psum_scatter(vector_terms, "dp", scatter_dimension=0, tiled=True)
    vector_grad = lax.psum(owned_vector_terms, "tensor")
    new_first, new_second, new_master, new_stats, new_bases = soap(
        owned_grads, master_tiles[0], tile_first[0], tile_second[0], tile_stats[0], tile_bases[0]
    )
    new_vector_first = beta_one * vector_first + (1.0 - beta_one) * vector_grad
    new_vector_second = beta_two * vector_second + (1.0 - beta_two) * vector_grad * vector_grad
    new_vectors = master_vectors - rate_vectors * (new_vector_first / (1.0 - beta_one**STEP)) / (
        jnp.sqrt(new_vector_second / (1.0 - beta_two**STEP)) + adam_eps
    )
    return (
        block_out,
        input_grad,
        frames_grad,
        new_master[None],
        new_first[None],
        new_second[None],
        new_stats[None],
        new_bases[None],
        new_vectors,
        new_vector_first,
        new_vector_second,
    )


def solution(mesh):
    in_specs = (
        P("dp", "tensor", None),
        P("dp", None, None),
        P("dp", "tensor", None),
        P("dp", None),
        P("dp", None),
        P(),
        P("tensor", "dp", None, None),
        P("tensor", "dp", None, None),
        P("tensor", "dp", None, None),
        P("tensor", "dp", None, None, None),
        P("tensor", "dp", None, None, None),
        P("dp"),
        P("dp"),
        P("dp"),
    )
    out_specs = (
        P("dp", "tensor", None),
        P("dp", "tensor", None),
        P("dp", "tensor", None),
        P("tensor", "dp", None, None),
        P("tensor", "dp", None, None),
        P("tensor", "dp", None, None),
        P("tensor", "dp", None, None, None),
        P("tensor", "dp", None, None, None),
        P("dp"),
        P("dp"),
        P("dp"),
    )
    return jax.shard_map(shards, mesh=mesh, in_specs=in_specs, out_specs=out_specs, check_vma=False)
```

```python
import functools

import jax
import jax.numpy as jnp
from jax import lax
from jax.experimental import pallas as pl
from jax.experimental.pallas import tpu as pltpu
from jax.sharding import PartitionSpec as P

HEAD = 64
FF = 3072
STEP = 5
LANES = 128
SLOT = 256
VM = 56 * 2**20
HI = lax.Precision.HIGHEST

norm_eps = 1e-05
beta_one = 0.9
beta_two = 0.95
adam_eps = 1e-08
rate_tiles = 0.05
rate_vectors = 0.3
score_scale = 0.125


def split2(a):
    hi = a.astype(jnp.bfloat16)
    lo = (a - hi.astype(jnp.float32)).astype(jnp.bfloat16)
    return hi, lo

def bdot(a, b, dims):
    return lax.dot_general(a, b, (dims, ((), ())), preferred_element_type=jnp.float32)

NN = ((1,), (0,)); TN = ((0,), (0,)); NT = ((1,), (1,))

def dot3(a, b, dims):
    (ah, al), (bh, bl) = a, b
    return bdot(ah, bh, dims) + (bdot(ah, bl, dims) + bdot(al, bh, dims))

def dothi(a, b, dims):
    return lax.dot_general(a, b, (dims, ((), ())), precision=HI, preferred_element_type=jnp.float32)

def soap_pre_kernel(first, stats, bases, rot_first, stats_rot):
    ql, qr = split2(bases[0, 0]), split2(bases[0, 1])
    inner = split2(dot3(ql, split2(first[0]), TN))
    rot_first[0] = dot3(inner, qr, NN)
    stats_rot[0, 0] = dot3(split2(stats[0, 0]), ql, NN)
    stats_rot[0, 1] = dot3(split2(stats[0, 1]), qr, NN)

def soap_main_kernel(grad, master, first, second, stats, bases, rot_first, stats_rot,
                     new_master, new_first, new_second, new_stats, turned, grams):
    g32 = grad[0].astype(jnp.float32)
    g, ql, qr = split2(g32), split2(bases[0, 0]), split2(bases[0, 1])
    new_first[0] = beta_one * first[0] + (1.0 - beta_one) * g32
    part_left = split2(dot3(ql, g, TN))
    rotated = dot3(part_left, qr, NN)
    fresh = beta_two * second[0] + (1.0 - beta_two) * rotated * rotated
    new_second[0] = fresh
    moment = (beta_one * rot_first[0] + (1.0 - beta_one) * rotated) / (1.0 - beta_one**STEP)
    step = moment / (jnp.sqrt(fresh / (1.0 - beta_two**STEP)) + adam_eps)
    back = split2(dot3(ql, split2(step), NN))
    new_master[0] = master[0] - rate_tiles * dot3(back, qr, NT)
    new_stats[0, 0] = beta_two * stats[0, 0] + (1.0 - beta_two) * dot3(g, g, NT)
    new_stats[0, 1] = beta_two * stats[0, 1] + (1.0 - beta_two) * dot3(g, g, TN)
    part_right = split2(dot3(g, qr, NN))
    for side, term in ((0, dot3(g, part_left, NT)), (1, dot3(g, part_right, TN))):
        side_turned = beta_two * stats_rot[0, side] + (1.0 - beta_two) * term
        turned[0, side] = side_turned
        halves = split2(side_turned)
        grams[0, side] = dot3(halves, halves, TN)

def chol_kernel(turned, grams, out, work, inv, fac, *, block):
    count, side = work.shape[0], work.shape[1]
    row = lax.broadcasted_iota(jnp.int32, (side, side), 0)
    col = lax.broadcasted_iota(jnp.int32, (side, side), 1)
    eye = (row == col).astype(jnp.float32)
    for m in range(count):
        work[m] = grams[m]
        inv[m] = eye
    brow = lax.broadcasted_iota(jnp.int32, (count, block, 2 * block), 1)
    bcol = lax.broadcasted_iota(jnp.int32, (count, block, 2 * block), 2)
    aug_eye = ((bcol - block) == brow).astype(jnp.float32)
    for k in range(side // block):
        lo = k * block
        diag = work[:, lo : lo + block, lo : lo + block]
        w = jnp.concatenate([diag, jnp.zeros_like(diag)], axis=2) + aug_eye
        for j in range(block - 1):
            piv = w[:, j : j + 1, :]
            ratio = w[:, :, j : j + 1] / w[:, j : j + 1, j : j + 1]
            w = w - jnp.where(brow > j, ratio * piv, 0.0)
        d = jnp.sum(jnp.where(brow == bcol, w, 0.0), axis=2, keepdims=True)
        fac[...] = w[:, :, block:] * lax.rsqrt(d)

        def one(m, _):
            x = fac[m]
            y = dothi(x, work[m, lo : lo + block, :], NN)
            z = dothi(x, inv[m, lo : lo + block, :], NN)
            inv[m, lo : lo + block, :] = z
            if lo + block < side:
                rest = side - lo - block
                ys = split2(y)
                upd = dothi(y, y, TN)
                updx = dothi(y, z, TN)
                work[m, lo + block :, :] = work[m, lo + block :, :] - upd[lo + block :, :]
                inv[m, lo + block :, :] = inv[m, lo + block :, :] - updx[lo + block :, :]
            return 0
        lax.fori_loop(0, count, one, 0)

    def last(m, _):
        out[m] = dothi(turned[m], inv[m], NT)
        return 0
    lax.fori_loop(0, count, last, 0)

def tile_spec(side):
    return pl.BlockSpec((1, side, side), lambda i: (i, 0, 0))
def pair_spec(side):
    return pl.BlockSpec((1, 2, side, side), lambda i: (i, 0, 0, 0))

def soap_pre(first, stats, bases):
    n, side = first.shape[0], first.shape[1]
    t, p = tile_spec(side), pair_spec(side)
    return pl.pallas_call(soap_pre_kernel, grid=(n,), in_specs=[t, p, p], out_specs=[t, p],
        out_shape=[jax.ShapeDtypeStruct(first.shape, jnp.float32), jax.ShapeDtypeStruct(stats.shape, jnp.float32)],
        name="soap_pre")(first, stats, bases)

def soap_main(grad, master, first, second, stats, bases, rot_first, stats_rot):
    n, side = first.shape[0], first.shape[1]
    t, p = tile_spec(side), pair_spec(side)
    f = jnp.float32
    ts, ps = jax.ShapeDtypeStruct(first.shape, f), jax.ShapeDtypeStruct(stats.shape, f)
    return pl.pallas_call(soap_main_kernel, grid=(n,), in_specs=[t, t, t, t, p, p, t, p],
        out_specs=[t, t, t, p, p, p], out_shape=[ts, ts, ts, ps, ps, ps], name="soap_main")(
        grad, master, first, second, stats, bases, rot_first, stats_rot)

def chol_bases(turned, grams, block=32):
    n, _, side, _ = turned.shape
    shape = (2 * n, side, side)
    out = pl.pallas_call(functools.partial(chol_kernel, block=block),
        out_shape=jax.ShapeDtypeStruct(shape, jnp.float32),
        scratch_shapes=[pltpu.VMEM(shape, jnp.float32), pltpu.VMEM(shape, jnp.float32), pltpu.VMEM((2*n, block, block), jnp.float32)],
        compiler_params=pltpu.CompilerParams(vmem_limit_bytes=48 * 2**20), name="chol_bases")(
        turned.reshape(shape), grams.reshape(shape))
    return out.reshape(turned.shape)

def soap(gradient, master, first, second, statistics, bases, block=32):
    rot_first, stats_rot = soap_pre(first, statistics, bases)
    nm, nf, ns, nst, turned, grams = soap_main(gradient, master, first, second, statistics, bases, rot_first, stats_rot)
    return nf, ns, nm, nst, chol_bases(turned, grams, block)


def head_pick(shape, head):
    lane = lax.broadcasted_iota(jnp.int32, shape, len(shape) - 1)
    return (lane >= HEAD) if head % 2 else (lane < HEAD)


def forward_heads(query, key, value, allowed, heads):
    blocks = []
    for first in range(0, heads, 2):
        span = slice(first * HEAD, first * HEAD + LANES)
        query_block, key_block, value_block = query[:, span], key[:, span], value[:, span]
        made = None
        for head in range(first, min(first + 2, heads)):
            own_query = jnp.where(head_pick(query_block.shape, head), query_block, jnp.zeros_like(query_block))
            scores = bdot(own_query, key_block, NT) * score_scale
            if allowed is not None:
                scores = jnp.where(allowed, scores, -1e30)
            weights = jnp.exp(scores - jnp.max(scores, axis=1, keepdims=True)).astype(jnp.bfloat16)
            own_value = jnp.where(head_pick(value_block.shape, head), value_block, jnp.ones_like(value_block))
            both = bdot(weights, own_value, NN)
            mixed = both / pltpu.roll(both, HEAD, 1)
            pick = head_pick(mixed.shape, head)
            made = jnp.where(pick, mixed, 0.0 if made is None else made)
        blocks.append(made.astype(jnp.bfloat16))
    return jnp.concatenate(blocks, axis=1)


def cross_forward_kernel(query, key, value, out, *, heads):
    out[0] = forward_heads(query[0], key[0], value[0], None, heads)


def self_forward_kernel(query, key, value, seg_col, seg_row, stamp_row, out, *, heads):
    rows = query.shape[1]
    at = lax.broadcasted_iota(jnp.int32, (rows, rows), 0)
    key_at = lax.broadcasted_iota(jnp.int32, (rows, rows), 1)
    allowed = (key_at <= at) & (seg_col[0] == seg_row[0]) & ((stamp_row[0] == 0) | (key_at == at))
    out[0] = forward_heads(query[0], key[0], value[0], allowed, heads)


def backward_head(query_block, key_block, key_turned, value_block, grad_block, mixed_block, allowed, head):
    pick = head_pick(query_block.shape, head)
    own_query = jnp.where(pick, query_block, jnp.zeros_like(query_block))
    own_grad = jnp.where(pick, grad_block, jnp.zeros_like(grad_block))
    scores = bdot(key_block, own_query, NT) * score_scale
    if allowed is not None:
        scores = jnp.where(allowed, scores, -1e30)
    weights = jnp.exp(scores - jnp.max(scores, axis=0, keepdims=True))
    probs = weights * (1.0 / jnp.sum(weights, axis=0, keepdims=True))
    grad_probs = bdot(value_block, own_grad, NT)
    row_dot = jnp.sum(probs * grad_probs, axis=0, keepdims=True)
    grad_scores = (probs * (grad_probs - row_dot)).astype(jnp.bfloat16)
    return probs.astype(jnp.bfloat16), grad_scores, bdot(key_turned, grad_scores, NN)


def backward_heads(query, key, value, grad, allowed, heads, probs_ref, scores_ref):
    blocks = []
    for first in range(0, heads, 2):
        span = slice(first * HEAD, first * HEAD + LANES)
        query_block, key_block, value_block, grad_block = query[:, span], key[:, span], value[:, span], grad[:, span]
        key_turned = key_block.T
        made = None
        for head in range(first, min(first + 2, heads)):
            probs, grad_scores, turned = backward_head(query_block, key_block, key_turned, value_block, grad_block, None, allowed, head)
            probs_ref[head] = probs
            scores_ref[head] = grad_scores
            row = lax.broadcasted_iota(jnp.int32, turned.shape, 0)
            pick = (row >= HEAD) if head % 2 else (row < HEAD)
            made = jnp.where(pick, turned, 0.0 if made is None else made)
        blocks.append((made.T * score_scale).astype(jnp.bfloat16))
    return jnp.concatenate(blocks, axis=1)


def key_value_grads(query, grad, heads, probs_ref, scores_ref):
    keys, values = [], []
    for first in range(0, heads, 2):
        span = slice(first * HEAD, first * HEAD + LANES)
        made_key = made_value = None
        for head in range(first, min(first + 2, heads)):
            grad_key = bdot(scores_ref[head], query[:, span], NN) * score_scale
            grad_value = bdot(probs_ref[head], grad[:, span], NN)
            pick = head_pick(grad_key.shape, head)
            made_key = jnp.where(pick, grad_key, 0.0 if made_key is None else made_key)
            made_value = jnp.where(pick, grad_value, 0.0 if made_value is None else made_value)
        keys.append(made_key.astype(jnp.bfloat16))
        values.append(made_value.astype(jnp.bfloat16))
    return jnp.concatenate(keys, axis=1), jnp.concatenate(values, axis=1)


def cross_backward_kernel(rank, query, key, value, grad, grad_query, grad_key, grad_value, probs_ref, scores_ref, *, heads):
    grad_query[0] = backward_heads(query[0], key[0], value[0], grad[0], None, heads, probs_ref, scores_ref)

    @pl.when(pl.program_id(1) == rank[0])
    def _():
        made = key_value_grads(query[0], grad[0], heads, probs_ref, scores_ref)
        grad_key[0], grad_value[0] = made


def self_backward_kernel(rank, query, key, value, grad, seg_col, seg_row, stamp_col, out, probs_ref, scores_ref, *, heads):
    rows = query.shape[1]
    key_at = lax.broadcasted_iota(jnp.int32, (rows, rows), 0)
    at = lax.broadcasted_iota(jnp.int32, (rows, rows), 1)
    allowed = (key_at <= at) & (seg_col[0] == seg_row[0]) & ((stamp_col[0] == 0) | (key_at == at))
    grad_query = backward_heads(query[0], key[0], value[0], grad[0], allowed, heads, probs_ref, scores_ref)
    grad_key, grad_value = key_value_grads(query[0], grad[0], heads, probs_ref, scores_ref)
    out[0] = jnp.concatenate([grad_query, grad_key, grad_value], axis=1)


def slot_spec(rows, offset):
    return pl.BlockSpec((1, rows, SLOT), lambda b, r: (b, 0, offset + r))


def self_forward(qkv, seg_col, seg_row, stamp_row, ranks, heads):
    seqs, rows, _ = qkv.shape
    col = pl.BlockSpec((1, rows, 1), lambda b, r: (b, 0, 0))
    row = pl.BlockSpec((1, 1, rows), lambda b, r: (b, 0, 0))
    return pl.pallas_call(
        functools.partial(self_forward_kernel, heads=heads),
        grid=(seqs, ranks),
        in_specs=[slot_spec(rows, 0), slot_spec(rows, ranks), slot_spec(rows, 2 * ranks), col, row, row],
        out_specs=slot_spec(rows, 0),
        out_shape=jax.ShapeDtypeStruct((seqs, rows, ranks * SLOT), jnp.bfloat16),
        compiler_params=pltpu.CompilerParams(vmem_limit_bytes=VM),
        name="self_forward",
    )(qkv, qkv, qkv, seg_col, seg_row, stamp_row)


def cross_forward(queries, keys_values, ranks, heads):
    seqs, rows, _ = queries.shape
    frames = keys_values.shape[1]
    return pl.pallas_call(
        functools.partial(cross_forward_kernel, heads=heads),
        grid=(seqs, ranks),
        in_specs=[slot_spec(rows, 0), slot_spec(frames, 0), slot_spec(frames, ranks)],
        out_specs=slot_spec(rows, 0),
        out_shape=jax.ShapeDtypeStruct((seqs, rows, ranks * SLOT), jnp.bfloat16),
        compiler_params=pltpu.CompilerParams(vmem_limit_bytes=VM),
        name="cross_forward",
    )(queries, keys_values, keys_values)


def ranked_spec(rows, offset):
    return pl.BlockSpec((1, rows, SLOT), lambda b, r, rank: (b, 0, offset + r))


def cross_backward(rank, queries, keys_values, grads, ranks, heads):
    seqs, rows, _ = queries.shape
    frames = keys_values.shape[1]
    kept = pl.BlockSpec((1, frames, SLOT), lambda b, r, rank: (b, 0, 0))
    bf = jnp.bfloat16
    return pl.pallas_call(
        functools.partial(cross_backward_kernel, heads=heads),
        grid_spec=pltpu.PrefetchScalarGridSpec(
            num_scalar_prefetch=1,
            grid=(seqs, ranks),
            in_specs=[ranked_spec(rows, 0), ranked_spec(frames, 0), ranked_spec(frames, ranks), ranked_spec(rows, 0)],
            out_specs=[ranked_spec(rows, 0), kept, kept],
            scratch_shapes=[pltpu.VMEM((heads, frames, rows), bf), pltpu.VMEM((heads, frames, rows), bf)],
        ),
        out_shape=[
            jax.ShapeDtypeStruct((seqs, rows, ranks * SLOT), bf),
            jax.ShapeDtypeStruct((seqs, frames, SLOT), bf),
            jax.ShapeDtypeStruct((seqs, frames, SLOT), bf),
        ],
        compiler_params=pltpu.CompilerParams(vmem_limit_bytes=VM),
        name="cross_backward",
    )(rank, queries, keys_values, keys_values, grads)


def self_backward(rank, qkv, grads, seg_col, seg_row, stamp_col, ranks, heads):
    seqs, rows, _ = qkv.shape
    bf = jnp.bfloat16
    own = lambda offset: pl.BlockSpec((1, rows, SLOT), lambda b, rank: (b, 0, offset + rank[0]))
    col = pl.BlockSpec((1, rows, 1), lambda b, rank: (b, 0, 0))
    row = pl.BlockSpec((1, 1, rows), lambda b, rank: (b, 0, 0))
    return pl.pallas_call(
        functools.partial(self_backward_kernel, heads=heads),
        grid_spec=pltpu.PrefetchScalarGridSpec(
            num_scalar_prefetch=1,
            grid=(seqs,),
            in_specs=[own(0), own(ranks), own(2 * ranks), own(0), col, row, col],
            out_specs=pl.BlockSpec((1, rows, 3 * SLOT), lambda b, rank: (b, 0, 0)),
            scratch_shapes=[pltpu.VMEM((heads, rows, rows), bf), pltpu.VMEM((heads, rows, rows), bf)],
        ),
        out_shape=jax.ShapeDtypeStruct((seqs, rows, 3 * SLOT), bf),
        compiler_params=pltpu.CompilerParams(vmem_limit_bytes=VM),
        name="self_backward",
    )(rank, qkv, qkv, qkv, grads, seg_col, seg_row, stamp_col)


def tile_sources():
    steps = []
    for base in (0, 4, 8, 16, 20, 12):
        for pair in range(2):
            steps.append([(pair * 2 + i // 4, base + i % 4) for i in range(8)])
    for base in (24, 28):
        for pair in range(2):
            steps.append([(pair * 2 + i // 4, base + i % 4) for i in range(8)])
    for half in range(2):
        for rank in range(4):
            steps.append([(rank, 32 + (half * 2 + i // 4) * 4 + i % 4) for i in range(8)])
    for rank in range(4):
        for half in range(2):
            steps.append([(rank, 48 + (half * 2 + i // 4) * 4 + i % 4) for i in range(8)])
    return steps


def assemble_kernel(table, *refs):
    tiles, (o_qkv, o_ckv, o_cq, o_wo, o_co, o_in, o_out) = refs[:8], refs[8:]
    step = pl.program_id(0)
    side = tiles[0].shape[1]

    def columns(out):
        gap = jnp.zeros((side, SLOT - side), jnp.bfloat16)
        for i in range(8):
            wide = jnp.concatenate([tiles[i][0], gap], axis=1)
            out[(i % 4) * side : (i % 4 + 1) * side, (i // 4) * SLOT : (i // 4 + 1) * SLOT] = wide

    def joined(half):
        return jnp.concatenate([tiles[half * 4 + i][0] for i in range(4)], axis=1)

    def padded_rows(out):
        for half in range(2):
            out[half * SLOT : half * SLOT + side, :] = joined(half)
            out[half * SLOT + side : (half + 1) * SLOT, :] = jnp.zeros((SLOT - side, 4 * side), jnp.bfloat16)

    def rows(out):
        for half in range(2):
            out[half * side : (half + 1) * side, :] = joined(half)

    for low, high, fill, out in (
        (0, 6, columns, o_qkv),
        (6, 10, columns, o_ckv),
        (10, 12, columns, o_cq),
        (12, 14, padded_rows, o_wo),
        (14, 16, padded_rows, o_co),
        (16, 24, rows, o_in),
        (24, 32, rows, o_out),
    ):
        pl.when((step >= low) & (step < high))(functools.partial(fill, out))


def assemble(table, tiles):
    side = tiles.shape[-1]
    width = 4 * side

    def tile_at(i):
        return pl.BlockSpec((1, side, side), lambda s, table: (table[s * 8 + i], 0, 0))

    def within(low, count):
        return lambda s: jnp.clip(s - low, 0, count - 1)

    a, b, c, d, e, f, g = [within(*x) for x in ((0, 6), (6, 4), (10, 2), (12, 2), (14, 2), (16, 8), (24, 8))]
    bf = jnp.bfloat16
    return pl.pallas_call(
        assemble_kernel,
        grid_spec=pltpu.PrefetchScalarGridSpec(
            num_scalar_prefetch=1,
            grid=(32,),
            in_specs=[tile_at(i) for i in range(8)],
            out_specs=[
                pl.BlockSpec((width, 2 * SLOT), lambda s, table: (0, a(s))),
                pl.BlockSpec((width, 2 * SLOT), lambda s, table: (0, b(s))),
                pl.BlockSpec((width, 2 * SLOT), lambda s, table: (0, c(s))),
                pl.BlockSpec((2 * SLOT, width), lambda s, table: (d(s), 0)),
                pl.BlockSpec((2 * SLOT, width), lambda s, table: (e(s), 0)),
                pl.BlockSpec((2 * side, width), lambda s, table: (f(s) // 4, f(s) % 4)),
                pl.BlockSpec((2 * side, width), lambda s, table: (g(s), 0)),
            ],
        ),
        out_shape=[
            jax.ShapeDtypeStruct((width, 12 * SLOT), bf),
            jax.ShapeDtypeStruct((width, 8 * SLOT), bf),
            jax.ShapeDtypeStruct((width, 4 * SLOT), bf),
            jax.ShapeDtypeStruct((4 * SLOT, width), bf),
            jax.ShapeDtypeStruct((4 * SLOT, width), bf),
            jax.ShapeDtypeStruct((width, 4 * width), bf),
            jax.ShapeDtypeStruct((4 * width, width), bf),
        ],
        compiler_params=pltpu.CompilerParams(vmem_limit_bytes=VM),
        name="assemble",
    )(table, *([tiles] * 8))


def weight_grads_kernel(
    rank, place, n1, dqkv, n2, dcq, frames, dk, dv, attended, b1, mixed, b2, n3, grad_up, active, b3, out
):
    side = out.shape[1]

    def slots(made, bases):
        for m, base in enumerate(bases):
            for i in range(4):
                out[place[base + i]] = made[i * side : (i + 1) * side, m * SLOT : m * SLOT + side].astype(jnp.bfloat16)

    def grid_of(made, base, rows):
        for i in range(rows):
            for j in range(4):
                tile = made[i * side : (i + 1) * side, j * side : (j + 1) * side]
                out[place[base + i * 4 + j]] = tile.astype(jnp.bfloat16)

    slots(bdot(n1[...], dqkv[...], TN), (0, 4, 8))
    slots(bdot(n2[...], dcq[...], TN), (12,))
    slots(bdot(frames[0], dk[0], TN) + bdot(frames[1], dk[1], TN), (16,))
    slots(bdot(frames[0], dv[0], TN) + bdot(frames[1], dv[1], TN), (20,))
    grid_of(bdot(attended[...], b1[...], TN), 24, 1)
    grid_of(bdot(mixed[...], b2[...], TN), 28, 1)
    grid_of(bdot(n3[...], grad_up[...], TN), 32, 4)
    grid_of(bdot(active[...], b3[...], TN), 48, 4)


def weight_grads(rank, place, side, n1, dqkv, n2, dcq, frames, dk, dv, attended, b1, mixed, b2, n3, grad_up, active, b3):
    def whole(x):
        return pl.BlockSpec(x.shape, lambda i, rank, place: (0,) * x.ndim)

    def own(x, width):
        return pl.BlockSpec((x.shape[0], width), lambda i, rank, place: (0, rank[0]))

    shape = (place.shape[0], side, side)
    return pl.pallas_call(
        weight_grads_kernel,
        grid_spec=pltpu.PrefetchScalarGridSpec(
            num_scalar_prefetch=2,
            grid=(1,),
            in_specs=[
                whole(n1), whole(dqkv), whole(n2), own(dcq, SLOT), whole(frames), whole(dk), whole(dv),
                own(attended, SLOT), whole(b1), own(mixed, SLOT), whole(b2), whole(n3),
                own(grad_up, 4 * side), own(active, 4 * side), whole(b3),
            ],
            out_specs=pl.BlockSpec(shape, lambda i, rank, place: (0, 0, 0)),
        ),
        out_shape=jax.ShapeDtypeStruct(shape, jnp.bfloat16),
        compiler_params=pltpu.CompilerParams(vmem_limit_bytes=60 * 2**20),
        name="weight_grads",
    )(rank, place, n1, dqkv, n2, dcq, frames, dk, dv, attended, b1, mixed, b2, n3, grad_up, active, b3)


def frames_kernel(frames, weight, bias, out):
    out[0] = (bdot(frames[0], weight[...], NN) + bias[...]).astype(jnp.bfloat16)


def frame_projection(frames, weight, bias):
    seqs, count, width = frames.shape
    total = weight.shape[1]
    return pl.pallas_call(
        frames_kernel,
        grid=(seqs, total // 512),
        in_specs=[
            pl.BlockSpec((1, count, width), lambda b, c: (b, 0, 0)),
            pl.BlockSpec((width, 512), lambda b, c: (0, c)),
            pl.BlockSpec((1, 512), lambda b, c: (0, c)),
        ],
        out_specs=pl.BlockSpec((1, count, 512), lambda b, c: (b, 0, c)),
        out_shape=jax.ShapeDtypeStruct((seqs, count, total), jnp.bfloat16),
        compiler_params=pltpu.CompilerParams(vmem_limit_bytes=VM),
        name="frame_projection",
    )(frames, weight, bias[None])


def frames_back_kernel(rank, dk, dv, key_weight, value_weight, out, *, parts):
    made = bdot(dk[0], key_weight[...], NT) + bdot(dv[0], value_weight[...], NT)
    share = made.shape[0] // parts
    for part in range(parts):
        piece = made[part * share : (part + 1) * share]
        out[part, 0] = jnp.concatenate([piece, jnp.zeros((out.shape[2] - share, piece.shape[1]), jnp.float32)], axis=0).astype(jnp.bfloat16)


def frames_back(rank, dk, dv, weight, parts):
    seqs, count, slot = dk.shape
    width = weight.shape[0]
    padded = -(-(count // parts) // 16) * 16
    own = pl.BlockSpec((1, count, slot), lambda b, rank: (b, 0, 0))
    return pl.pallas_call(
        functools.partial(frames_back_kernel, parts=parts),
        grid_spec=pltpu.PrefetchScalarGridSpec(
            num_scalar_prefetch=1,
            grid=(seqs,),
            in_specs=[
                own, own,
                pl.BlockSpec((width, slot), lambda b, rank: (0, rank[0])),
                pl.BlockSpec((width, slot), lambda b, rank: (0, parts + rank[0])),
            ],
            out_specs=pl.BlockSpec((parts, 1, padded, width), lambda b, rank: (0, b, 0, 0)),
        ),
        out_shape=jax.ShapeDtypeStruct((parts, seqs, padded, width), jnp.bfloat16),
        compiler_params=pltpu.CompilerParams(vmem_limit_bytes=VM),
        name="frames_back",
    )(rank, dk, dv, weight, weight)


def product(left_part, right_part):
    return jnp.dot(left_part, right_part, preferred_element_type=jnp.float32)


def times_transpose(left_part, right_part):
    return lax.dot_general(left_part, right_part, (NT, ((), ())), preferred_element_type=jnp.float32)


def unit_rows(values):
    centre = jnp.mean(values, axis=-1, keepdims=True)
    centred = values - centre
    inverse = lax.rsqrt(jnp.mean(centred * centred, axis=-1, keepdims=True) + norm_eps)
    return centred * inverse, inverse


def normalize(values, gain, shift):
    return unit_rows(values)[0] * gain + shift


def normalize_back(values, gain, grads):
    unit, inverse = unit_rows(values)
    scaled = grads * gain
    result = inverse * (
        scaled
        - jnp.mean(scaled, axis=-1, keepdims=True)
        - unit * jnp.mean(scaled * unit, axis=-1, keepdims=True)
    )
    return result, jnp.sum(grads * unit, axis=0), jnp.sum(grads, axis=0)


def gelu_pair(value):
    size = jnp.abs(value) * 0.7071067811865476
    bell = jnp.exp(-size * size)
    t = 1.0 / (1.0 + 0.3275911 * size)
    poly = t * (0.254829592 + t * (-0.284496736 + t * (1.421413741 + t * (-1.453152027 + t * 1.061405429))))
    tail = 0.5 * poly * bell
    level = jnp.where(value >= 0, 1.0 - tail, tail)
    return value * level, level + value * bell * 0.3989422804014327


def spread_heads(rows, ranks):
    lead = rows.shape[0]
    side = rows.shape[1] // ranks
    return jnp.pad(rows.reshape(lead, ranks, side), ((0, 0), (0, 0), (0, SLOT - side))).reshape(lead, ranks * SLOT)


def shards(
    hidden_in, frames, cotangent, segments, stamps, owner_list, master_tiles, tile_first, tile_second,
    tile_stats, tile_bases, master_vectors, vector_first, vector_second,
):
    f32, bf16 = jnp.float32, jnp.bfloat16
    ranks, groups = lax.axis_size("tensor"), lax.axis_size("dp")
    rank, group = lax.axis_index("tensor"), lax.axis_index("dp")
    seqs, local_rows, width = hidden_in.shape
    rows = local_rows * ranks
    tokens = seqs * rows
    own_tiles, side = master_tiles.shape[1], master_tiles.shape[-1]
    heads = side // HEAD
    rank_ref = rank.astype(jnp.int32)[None]

    both = lax.all_gather(jnp.stack([hidden_in, cotangent]), "tensor", axis=2, tiled=True)
    hidden = both[0].reshape(tokens, width).astype(f32)
    top_grad = both[1].reshape(tokens, width).astype(f32)
    gathered = lax.all_gather(master_tiles[0].astype(bf16), ("dp", "tensor"), axis=0, tiled=True)
    vectors = lax.all_gather(master_vectors.astype(bf16), "dp", axis=0, tiled=True).astype(f32).reshape(19, width)

    count = owner_list.shape[0]
    position = jnp.arange(count, dtype=jnp.int32)
    place = jnp.sum(jnp.where(owner_list[None, :] == position[:, None], position[None, :], 0), axis=1)
    steps = tile_sources()
    source_rank = jnp.array([r for step in steps for r, _ in step], jnp.int32)
    source_ident = jnp.array([t for step in steps for _, t in step], jnp.int32)
    found = jnp.sum(jnp.where(owner_list[None, :] == source_ident[:, None], position[None, :], 0), axis=1)
    table = (found // own_tiles * ranks + source_rank) * own_tiles + found % own_tiles
    w_qkv, c_kv, c_q, w_o, c_o, w_in, w_out = assemble(table, gathered)

    head_bias = spread_heads(vectors[11:15], ranks)
    none = jnp.zeros_like(head_bias[0])
    inner_bias = vectors[15:19].reshape(-1)
    seg_col, seg_row = segments[:, :, None], segments[:, None, :]
    stamp_col, stamp_row = stamps[:, :, None], stamps[:, None, :]

    def split(values):
        return values.reshape(seqs, rows, values.shape[-1])

    def flat(values):
        return values.reshape(tokens, values.shape[-1])

    def own_rows(values):
        return lax.dynamic_slice_in_dim(split(values), rank * local_rows, local_rows, axis=1)

    keys_values = frame_projection(frames, c_kv, jnp.concatenate([none, head_bias[3]]))
    n1 = normalize(hidden, vectors[0], vectors[1]).astype(bf16)
    qkv = split((product(n1, w_qkv) + jnp.concatenate([head_bias[0], none, head_bias[1]])).astype(bf16))
    attended = flat(self_forward(qkv, seg_col, seg_row, stamp_row, ranks, heads))
    first_sum = hidden + product(attended, w_o) + vectors[8]
    n2 = normalize(first_sum, vectors[2], vectors[3]).astype(bf16)
    cross_queries = split((product(n2, c_q) + head_bias[2]).astype(bf16))
    mixed = flat(cross_forward(cross_queries, keys_values, ranks, heads))
    second_sum = first_sum + product(mixed, c_o) + vectors[9]
    n3 = normalize(second_sum, vectors[4], vectors[5]).astype(bf16)
    active, slope = gelu_pair(product(n3, w_in) + inner_bias)
    active, slope = active.astype(bf16), slope.astype(bf16)
    third_sum = second_sum + product(active, w_out) + vectors[10]
    block_out = own_rows(normalize(third_sum, vectors[6], vectors[7]))

    grad_third, gain_final, shift_final = normalize_back(third_sum, vectors[6], top_grad)
    b3 = grad_third.astype(bf16)
    grad_up = (times_transpose(b3, w_out) * slope.astype(f32)).astype(bf16)
    back, gain_three, shift_three = normalize_back(second_sum, vectors[4], times_transpose(grad_up, w_in))
    grad_second = grad_third + back
    b2 = grad_second.astype(bf16)
    grad_mixed = split(times_transpose(b2, c_o).astype(bf16))
    dcq, dk, dv = cross_backward(rank_ref, cross_queries, keys_values, grad_mixed, ranks, heads)
    dcq = flat(dcq)
    frames_part = frames_back(rank_ref, dk, dv, c_kv, ranks)
    frames_sum = lax.psum_scatter(
        frames_part.reshape(ranks * seqs, frames_part.shape[2], width), "tensor", scatter_dimension=0, tiled=True
    )
    frames_grad = frames_sum[:, : frames.shape[1] // ranks].astype(f32)
    back, gain_two, shift_two = normalize_back(first_sum, vectors[2], times_transpose(dcq, c_q))
    grad_first = grad_second + back
    b1 = grad_first.astype(bf16)
    grad_attended = split(times_transpose(b1, w_o).astype(bf16))
    dqkv = flat(self_backward(rank_ref, qkv, grad_attended, seg_col, seg_row, stamp_col, ranks, heads))

    own_weight = lax.dynamic_slice_in_dim(w_qkv.reshape(width, 3, ranks * SLOT), rank * SLOT, SLOT, axis=2)
    part_one = times_transpose(dqkv, own_weight.reshape(width, 3 * SLOT))
    unit_one, _ = unit_rows(hidden)
    gain_one, shift_one = jnp.sum(part_one * unit_one, axis=0), jnp.sum(part_one, axis=0)
    grad_one = lax.psum_scatter(split(part_one.astype(bf16)), "tensor", scatter_dimension=1, tiled=True).astype(f32)
    back, _, _ = normalize_back(
        hidden_in.astype(f32).reshape(-1, width), vectors[0], grad_one.reshape(-1, width)
    )
    input_grad = own_rows(grad_first) + back.reshape(hidden_in.shape)

    tile_terms = weight_grads(
        rank_ref, place, side, n1, dqkv, n2, dcq, frames, dk, dv, attended, b1, mixed, b2, n3, grad_up, active, b3
    )
    owned_grads = lax.psum_scatter(tile_terms, "dp", scatter_dimension=0, tiled=True)

    def total(values):
        return jnp.sum(values.astype(f32), axis=tuple(range(values.ndim - 1)))

    same = jnp.stack(
        [gain_two, shift_two, gain_three, shift_three, gain_final, shift_final, total(b1), total(b2), total(b3)]
    )
    query_sum = total(dcq).reshape(ranks, SLOT)[:, :side].reshape(1, width)
    up_sum = total(grad_up).reshape(4, width)
    even = 1.0 / ranks
    dqkv_sum = total(dqkv)
    own_sums = jnp.stack([dqkv_sum[:side], dqkv_sum[2 * SLOT : 2 * SLOT + side], total(dv)[:side]])
    own_sums = lax.dynamic_update_slice(jnp.zeros((3, width), f32), own_sums, (0, rank * side))
    vector_terms = jnp.concatenate(
        [gain_one[None], shift_one[None], same * even, own_sums[:2], query_sum * even, own_sums[2:], up_sum * even]
    )
    vector_sums = lax.psum(vector_terms.reshape(-1), ("dp", "tensor"))
    length = master_vectors.shape[0]
    vector_grad = lax.dynamic_slice_in_dim(vector_sums, group * length, length)

    new_first, new_second, new_master, new_stats, new_bases = soap(
        owned_grads, master_tiles[0], tile_first[0], tile_second[0], tile_stats[0], tile_bases[0]
    )
    new_vector_first = beta_one * vector_first + (1.0 - beta_one) * vector_grad
    new_vector_second = beta_two * vector_second + (1.0 - beta_two) * vector_grad * vector_grad
    new_vectors = master_vectors - rate_vectors * (new_vector_first / (1.0 - beta_one**STEP)) / (
        jnp.sqrt(new_vector_second / (1.0 - beta_two**STEP)) + adam_eps
    )
    return (
        block_out, input_grad, frames_grad, new_master[None], new_first[None], new_second[None],
        new_stats[None], new_bases[None], new_vectors, new_vector_first, new_vector_second,
    )


def solution(mesh):
    rows, seqs, tiles, pairs = (
        P("dp", "tensor", None), P("dp", None), P("tensor", "dp", None, None), P("tensor", "dp", None, None, None)
    )
    line = P("dp")
    in_specs = (
        rows, P("dp", None, None), rows, seqs, seqs, P(), tiles, tiles, tiles, pairs, pairs, line, line, line
    )
    out_specs = (rows, rows, rows, tiles, tiles, tiles, pairs, pairs, line, line, line)
    return jax.shard_map(shards, mesh=mesh, in_specs=in_specs, out_specs=out_specs, check_vma=False)
```

```python
import functools

import jax
import jax.numpy as jnp
from jax import lax
from jax.experimental import pallas as pl
from jax.experimental.pallas import tpu as pltpu
from jax.sharding import PartitionSpec as P

HEAD = 64
FF = 3072
STEP = 5
LANES = 128
SLOT = 256
VM = 56 * 2**20
HI = lax.Precision.HIGHEST

norm_eps = 1e-05
beta_one = 0.9
beta_two = 0.95
adam_eps = 1e-08
rate_tiles = 0.05
rate_vectors = 0.3
score_scale = 0.125


def split2(a):
    hi = a.astype(jnp.bfloat16)
    lo = (a - hi.astype(jnp.float32)).astype(jnp.bfloat16)
    return hi, lo

def bdot(a, b, dims):
    return lax.dot_general(a, b, (dims, ((), ())), preferred_element_type=jnp.float32)

NN = ((1,), (0,)); TN = ((0,), (0,)); NT = ((1,), (1,))

def dot3(a, b, dims):
    (ah, al), (bh, bl) = a, b
    return bdot(ah, bh, dims) + (bdot(ah, bl, dims) + bdot(al, bh, dims))

def dothi(a, b, dims):
    return lax.dot_general(a, b, (dims, ((), ())), precision=HI, preferred_element_type=jnp.float32)

def soap_pre_kernel(first, stats, bases, rot_first, stats_rot):
    ql, qr = split2(bases[0, 0]), split2(bases[0, 1])
    inner = split2(dot3(ql, split2(first[0]), TN))
    rot_first[0] = dot3(inner, qr, NN)
    stats_rot[0, 0] = dot3(split2(stats[0, 0]), ql, NN)
    stats_rot[0, 1] = dot3(split2(stats[0, 1]), qr, NN)

def soap_main_kernel(grad, master, first, second, stats, bases, rot_first, stats_rot,
                     new_master, new_first, new_second, new_stats, turned, grams):
    g32 = grad[0].astype(jnp.float32)
    g, ql, qr = split2(g32), split2(bases[0, 0]), split2(bases[0, 1])
    new_first[0] = beta_one * first[0] + (1.0 - beta_one) * g32
    part_left = split2(dot3(ql, g, TN))
    rotated = dot3(part_left, qr, NN)
    fresh = beta_two * second[0] + (1.0 - beta_two) * rotated * rotated
    new_second[0] = fresh
    moment = (beta_one * rot_first[0] + (1.0 - beta_one) * rotated) / (1.0 - beta_one**STEP)
    step = moment / (jnp.sqrt(fresh / (1.0 - beta_two**STEP)) + adam_eps)
    back = split2(dot3(ql, split2(step), NN))
    new_master[0] = master[0] - rate_tiles * dot3(back, qr, NT)
    new_stats[0, 0] = beta_two * stats[0, 0] + (1.0 - beta_two) * dot3(g, g, NT)
    new_stats[0, 1] = beta_two * stats[0, 1] + (1.0 - beta_two) * dot3(g, g, TN)
    part_right = split2(dot3(g, qr, NN))
    for side, term in ((0, dot3(g, part_left, NT)), (1, dot3(g, part_right, TN))):
        side_turned = beta_two * stats_rot[0, side] + (1.0 - beta_two) * term
        turned[0, side] = side_turned
        halves = split2(side_turned)
        grams[0, side] = dot3(halves, halves, TN)

def chol_kernel(turned, grams, out, work, fac, *, block, unroll, passes):
    count, side = work.shape[0], work.shape[1]
    wide = work.shape[2] // 2
    for m in range(count):
        work[m, :, :side] = grams[m]
        work[m, :, side:wide] = jnp.zeros((side, wide - side), jnp.float32)
        work[m, :, wide : wide + side] = turned[m].T
        work[m, :, wide + side :] = jnp.zeros((side, wide - side), jnp.float32)
    brow = lax.broadcasted_iota(jnp.int32, (count, block, 2 * block), 1)
    bcol = lax.broadcasted_iota(jnp.int32, (count, block, 2 * block), 2)
    aug_eye = ((bcol - block) == brow).astype(jnp.float32)
    for k in range(side // block):
        lo, hi = k * block, (k + 1) * block
        diag = work[:, lo:hi, lo:hi]
        w = jnp.concatenate([diag, jnp.zeros_like(diag)], axis=2) + aug_eye
        for j in range(block - 1):
            piv = w[:, j : j + 1, :]
            ratio = w[:, :, j : j + 1] / w[:, j : j + 1, j : j + 1]
            w = w - jnp.where(brow > j, ratio * piv, 0.0)
        d = jnp.sum(jnp.where(brow == bcol, w, 0.0), axis=2, keepdims=True)
        fac[...] = w[:, :, block:] * lax.rsqrt(d)

        def several(i, _):
            for u in range(unroll):
                m = i * unroll + u
                if passes == 6:
                    y = dothi(fac[m], work[m, lo:hi, :], NN)
                else:
                    y = dot3(split2(fac[m]), split2(work[m, lo:hi, :]), NN)
                work[m, lo:hi, :] = y
                if hi < side:
                    turn = y[:, :side].T[hi:]
                    if passes == 6:
                        step = dothi(turn, y, NN)
                    else:
                        step = dot3(split2(turn), split2(y), NN)
                    work[m, hi:, :] = work[m, hi:, :] - step
            return 0
        lax.fori_loop(0, count // unroll, several, 0)
    for m in range(count):
        out[m] = work[m, :, wide : wide + side].T

def tile_spec(side):
    return pl.BlockSpec((1, side, side), lambda i: (i, 0, 0))
def pair_spec(side):
    return pl.BlockSpec((1, 2, side, side), lambda i: (i, 0, 0, 0))

def soap_pre(first, stats, bases):
    n, side = first.shape[0], first.shape[1]
    t, p = tile_spec(side), pair_spec(side)
    return pl.pallas_call(soap_pre_kernel, grid=(n,), in_specs=[t, p, p], out_specs=[t, p],
        out_shape=[jax.ShapeDtypeStruct(first.shape, jnp.float32), jax.ShapeDtypeStruct(stats.shape, jnp.float32)],
        name="soap_pre")(first, stats, bases)

def soap_main(grad, master, first, second, stats, bases, rot_first, stats_rot):
    n, side = first.shape[0], first.shape[1]
    t, p = tile_spec(side), pair_spec(side)
    f = jnp.float32
    ts, ps = jax.ShapeDtypeStruct(first.shape, f), jax.ShapeDtypeStruct(stats.shape, f)
    return pl.pallas_call(soap_main_kernel, grid=(n,), in_specs=[t, t, t, t, p, p, t, p],
        out_specs=[t, t, t, p, p, p], out_shape=[ts, ts, ts, ps, ps, ps], name="soap_main")(
        grad, master, first, second, stats, bases, rot_first, stats_rot)

def chol_bases(turned, grams, block=64, unroll=4, passes=3):
    n, _, side, _ = turned.shape
    shape = (2 * n, side, side)
    unroll = min(unroll, 2 * n)
    out = pl.pallas_call(functools.partial(chol_kernel, block=block, unroll=unroll, passes=passes),
        out_shape=jax.ShapeDtypeStruct(shape, jnp.float32),
        scratch_shapes=[pltpu.VMEM((2 * n, side, 512), jnp.float32), pltpu.VMEM((2*n, block, block), jnp.float32)],
        compiler_params=pltpu.CompilerParams(vmem_limit_bytes=48 * 2**20), name="chol_bases")(
        turned.reshape(shape), grams.reshape(shape))
    return out.reshape(turned.shape)


def soap(gradient, master, first, second, statistics, bases):
    rot_first, stats_rot = soap_pre(first, statistics, bases)
    nm, nf, ns, nst, turned, grams = soap_main(gradient, master, first, second, statistics, bases, rot_first, stats_rot)
    return nf, ns, nm, nst, chol_bases(turned, grams)


def head_pick(shape, head):
    lane = lax.broadcasted_iota(jnp.int32, shape, len(shape) - 1)
    return (lane >= HEAD) if head % 2 else (lane < HEAD)


def forward_heads(query, key, value, allowed, heads, chunk):
    rows = query.shape[0]
    units = [(low, head) for low in range(0, rows, chunk) for head in range(heads)]
    spans = [slice(head // 2 * LANES, head // 2 * LANES + LANES) for head in range(heads)]
    own_values = []
    for head in range(heads):
        block = value[:, spans[head]]
        own_values.append(jnp.where(head_pick(block.shape, head), block, jnp.ones_like(block)))

    def scores_of(unit):
        low, head = unit
        block = query[low : low + chunk, spans[head]]
        own = jnp.where(head_pick(block.shape, head), block, jnp.zeros_like(block)) * jnp.bfloat16(score_scale)
        return bdot(own, key[:, spans[head]], NT)

    done, logs = {}, {}
    ahead = scores_of(units[0])
    for i, (low, head) in enumerate(units):
        scores = ahead
        if i + 1 < len(units):
            ahead = scores_of(units[i + 1])
        if allowed is not None:
            scores = jnp.where(allowed[low : low + chunk], scores, -1e30)
        top = jnp.max(scores, axis=1, keepdims=True)
        weights = jnp.exp(scores - top).astype(jnp.bfloat16)
        both = bdot(weights, own_values[head], NN)
        turned = pltpu.roll(both, HEAD, 1)
        pick = head_pick(both.shape, head)
        done[low, head] = both / turned
        logs[low, head] = top + jnp.log(jnp.where(pick, turned, both))
    columns, lines = [], []
    for low in range(0, rows, chunk):
        blocks = []
        lane = lax.broadcasted_iota(jnp.int32, (chunk, LANES), 1)
        line = jnp.zeros((chunk, LANES), jnp.float32)
        for first in range(0, heads, 2):
            other = done[low, first + 1] if first + 1 < heads else 0.0
            blocks.append(jnp.where(lane < HEAD, done[low, first], other).astype(jnp.bfloat16))
        for head in range(heads):
            line = jnp.where(lane == head, logs[low, head], line)
        columns.append(jnp.concatenate(blocks, axis=1))
        lines.append(line)
    return jnp.concatenate(columns, axis=0), jnp.concatenate(lines, axis=0).T[:8]


def cross_forward_kernel(query, key, value, out, logs, *, heads, chunk):
    out[0], logs[0, 0] = forward_heads(query[0], key[0], value[0], None, heads, chunk)


def self_forward_kernel(query, key, value, seg_col, seg_row, stamp_row, out, logs, *, heads, chunk):
    rows = query.shape[1]
    at = lax.broadcasted_iota(jnp.int32, (rows, rows), 0)
    key_at = lax.broadcasted_iota(jnp.int32, (rows, rows), 1)
    allowed = (key_at <= at) & (seg_col[0] == seg_row[0]) & ((stamp_row[0] == 0) | (key_at == at))
    out[0], logs[0, 0] = forward_heads(query[0], key[0], value[0], allowed, heads, chunk)


def backward_heads(query, key, value, grad, mixed, logs, allowed, heads, chunk, probs_ref, scores_ref):
    keys = key.shape[0]
    spans = [slice(head // 2 * LANES, head // 2 * LANES + LANES) for head in range(heads)]
    products = (grad.astype(jnp.float32) * mixed.astype(jnp.float32)).T
    own_query, own_grad, turned, dots, total = [], [], [], [], [None] * heads
    for head in range(heads):
        pick = head_pick((query.shape[0], LANES), head)
        zero = jnp.zeros((query.shape[0], LANES), jnp.bfloat16)
        own_query.append(jnp.where(pick, query[:, spans[head]], zero) * jnp.bfloat16(score_scale))
        own_grad.append(jnp.where(pick, grad[:, spans[head]], zero))
        dots.append(jnp.sum(products[head * HEAD : (head + 1) * HEAD], axis=0, keepdims=True))
        if head % 2 == 0:
            turned.append(key[:, spans[head]].T)
    units = [(low, head) for low in range(0, keys, chunk) for head in range(heads)]

    def products_of(unit):
        low, head = unit
        high = min(low + chunk, keys)
        return bdot(key[low:high, spans[head]], own_query[head], NT), bdot(value[low:high, spans[head]], own_grad[head], NT)

    ahead = products_of(units[0])
    for i, (low, head) in enumerate(units):
        high = min(low + chunk, keys)
        scores, grad_probs = ahead
        if i + 1 < len(units):
            ahead = products_of(units[i + 1])
        if allowed is not None:
            scores = jnp.where(allowed[low:high], scores, -1e30)
        probs = jnp.exp(scores - logs[head : head + 1])
        grad_scores = (probs * (grad_probs - dots[head])).astype(jnp.bfloat16)
        probs_ref[head, low:high] = probs.astype(jnp.bfloat16)
        scores_ref[head, low:high] = grad_scores
        half = head % 2 * HEAD
        term = bdot(turned[head // 2][half : half + HEAD, low:high], grad_scores, NN)
        total[head] = term if total[head] is None else total[head] + term
    if heads % 2:
        total.append(jnp.zeros_like(total[0]))
    return (jnp.concatenate(total, axis=0).T * score_scale).astype(jnp.bfloat16)


def key_value_grads(query, grad, heads, probs_ref, scores_ref):
    keys, values = [], []
    for first in range(0, heads, 2):
        span = slice(first * HEAD, first * HEAD + LANES)
        made_key = made_value = None
        for head in range(first, min(first + 2, heads)):
            grad_key = bdot(scores_ref[head], query[:, span], NN) * score_scale
            grad_value = bdot(probs_ref[head], grad[:, span], NN)
            pick = head_pick(grad_key.shape, head)
            made_key = jnp.where(pick, grad_key, 0.0 if made_key is None else made_key)
            made_value = jnp.where(pick, grad_value, 0.0 if made_value is None else made_value)
        keys.append(made_key.astype(jnp.bfloat16))
        values.append(made_value.astype(jnp.bfloat16))
    return jnp.concatenate(keys, axis=1), jnp.concatenate(values, axis=1)


def cross_backward_kernel(
    rank, query, key, value, grad, mixed, logs, grad_query, grad_key, grad_value, probs_ref, scores_ref, *, heads, chunk
):
    grad_query[0] = backward_heads(
        query[0], key[0], value[0], grad[0], mixed[0], logs[0, 0], None, heads, chunk, probs_ref, scores_ref
    )

    @pl.when(pl.program_id(1) == rank[0])
    def _():
        made = key_value_grads(query[0], grad[0], heads, probs_ref, scores_ref)
        grad_key[0], grad_value[0] = made


def self_backward_kernel(
    rank, query, key, value, grad, mixed, logs, seg_col, seg_row, stamp_col, out, probs_ref, scores_ref, *, heads, chunk
):
    rows = query.shape[1]
    key_at = lax.broadcasted_iota(jnp.int32, (rows, rows), 0)
    at = lax.broadcasted_iota(jnp.int32, (rows, rows), 1)
    allowed = (key_at <= at) & (seg_col[0] == seg_row[0]) & ((stamp_col[0] == 0) | (key_at == at))
    grad_query = backward_heads(
        query[0], key[0], value[0], grad[0], mixed[0], logs[0, 0], allowed, heads, chunk, probs_ref, scores_ref
    )
    grad_key, grad_value = key_value_grads(query[0], grad[0], heads, probs_ref, scores_ref)
    out[0] = jnp.concatenate([grad_query, grad_key, grad_value], axis=1)


def slot_spec(rows, offset):
    return pl.BlockSpec((1, rows, SLOT), lambda b, r: (b, 0, offset + r))


def self_forward(qkv, seg_col, seg_row, stamp_row, ranks, heads, chunk=448):
    seqs, rows, _ = qkv.shape
    col = pl.BlockSpec((1, rows, 1), lambda b, r: (b, 0, 0))
    row = pl.BlockSpec((1, 1, rows), lambda b, r: (b, 0, 0))
    return pl.pallas_call(
        functools.partial(self_forward_kernel, heads=heads, chunk=chunk),
        grid=(seqs, ranks),
        in_specs=[slot_spec(rows, 0), slot_spec(rows, ranks), slot_spec(rows, 2 * ranks), col, row, row],
        out_specs=[slot_spec(rows, 0), pl.BlockSpec((1, 1, 8, rows), lambda b, r: (b, r, 0, 0))],
        out_shape=[
            jax.ShapeDtypeStruct((seqs, rows, ranks * SLOT), jnp.bfloat16),
            jax.ShapeDtypeStruct((seqs, ranks, 8, rows), jnp.float32),
        ],
        compiler_params=pltpu.CompilerParams(vmem_limit_bytes=VM),
        name="self_forward",
    )(qkv, qkv, qkv, seg_col, seg_row, stamp_row)


def cross_forward(queries, keys_values, ranks, heads, chunk=448):
    seqs, rows, _ = queries.shape
    frames = keys_values.shape[1]
    return pl.pallas_call(
        functools.partial(cross_forward_kernel, heads=heads, chunk=chunk),
        grid=(seqs, ranks),
        in_specs=[slot_spec(rows, 0), slot_spec(frames, 0), slot_spec(frames, ranks)],
        out_specs=[slot_spec(rows, 0), pl.BlockSpec((1, 1, 8, rows), lambda b, r: (b, r, 0, 0))],
        out_shape=[
            jax.ShapeDtypeStruct((seqs, rows, ranks * SLOT), jnp.bfloat16),
            jax.ShapeDtypeStruct((seqs, ranks, 8, rows), jnp.float32),
        ],
        compiler_params=pltpu.CompilerParams(vmem_limit_bytes=VM),
        name="cross_forward",
    )(queries, keys_values, keys_values)


def ranked_spec(rows, offset):
    return pl.BlockSpec((1, rows, SLOT), lambda b, r, rank: (b, 0, offset + r))


def cross_backward(rank, queries, keys_values, grads, mixed, logs, ranks, heads, chunk=512):
    seqs, rows, _ = queries.shape
    frames = keys_values.shape[1]
    kept = pl.BlockSpec((1, frames, SLOT), lambda b, r, rank: (b, 0, 0))
    bf = jnp.bfloat16
    return pl.pallas_call(
        functools.partial(cross_backward_kernel, heads=heads, chunk=chunk),
        grid_spec=pltpu.PrefetchScalarGridSpec(
            num_scalar_prefetch=1,
            grid=(seqs, ranks),
            in_specs=[
                ranked_spec(rows, 0), ranked_spec(frames, 0), ranked_spec(frames, ranks), ranked_spec(rows, 0), ranked_spec(rows, 0),
                pl.BlockSpec((1, 1, 8, rows), lambda b, r, rank: (b, r, 0, 0)),
            ],
            out_specs=[ranked_spec(rows, 0), kept, kept],
            scratch_shapes=[pltpu.VMEM((heads, frames, rows), bf), pltpu.VMEM((heads, frames, rows), bf)],
        ),
        out_shape=[
            jax.ShapeDtypeStruct((seqs, rows, ranks * SLOT), bf),
            jax.ShapeDtypeStruct((seqs, frames, SLOT), bf),
            jax.ShapeDtypeStruct((seqs, frames, SLOT), bf),
        ],
        compiler_params=pltpu.CompilerParams(vmem_limit_bytes=VM),
        name="cross_backward",
    )(rank, queries, keys_values, keys_values, grads, mixed, logs)


def self_backward(rank, qkv, grads, mixed, logs, seg_col, seg_row, stamp_col, ranks, heads, chunk=224):
    seqs, rows, _ = qkv.shape
    bf = jnp.bfloat16
    own = lambda offset: pl.BlockSpec((1, rows, SLOT), lambda b, rank: (b, 0, offset + rank[0]))
    col = pl.BlockSpec((1, rows, 1), lambda b, rank: (b, 0, 0))
    row = pl.BlockSpec((1, 1, rows), lambda b, rank: (b, 0, 0))
    return pl.pallas_call(
        functools.partial(self_backward_kernel, heads=heads, chunk=chunk),
        grid_spec=pltpu.PrefetchScalarGridSpec(
            num_scalar_prefetch=1,
            grid=(seqs,),
            in_specs=[
                own(0), own(ranks), own(2 * ranks), own(0), own(0),
                pl.BlockSpec((1, 1, 8, rows), lambda b, rank: (b, rank[0], 0, 0)), col, row, col,
            ],
            out_specs=pl.BlockSpec((1, rows, 3 * SLOT), lambda b, rank: (b, 0, 0)),
            scratch_shapes=[pltpu.VMEM((heads, rows, rows), bf), pltpu.VMEM((heads, rows, rows), bf)],
        ),
        out_shape=jax.ShapeDtypeStruct((seqs, rows, 3 * SLOT), bf),
        compiler_params=pltpu.CompilerParams(vmem_limit_bytes=VM),
        name="self_backward",
    )(rank, qkv, qkv, qkv, grads, mixed, logs, seg_col, seg_row, stamp_col)


def pack_kernel(tiles, line, out):
    side = tiles.shape[1]
    half, extra = side // 2, side - LANES
    for i in range(tiles.shape[0]):
        tile = tiles[i].astype(jnp.bfloat16)
        low = i * (side + half)
        out[low : low + side] = tile[:, :LANES]
        out[low + side : low + side + half] = jnp.concatenate([tile[:half, LANES:], tile[half:, LANES:]], axis=1)
    out[out.shape[0] - line.shape[0] :] = line[...].astype(jnp.bfloat16)


def pack(tiles, line):
    count, side, _ = tiles.shape
    rows = count * (side + side // 2) + line.shape[0]
    return pl.pallas_call(
        pack_kernel, out_shape=jax.ShapeDtypeStruct((rows, LANES), jnp.bfloat16), name="pack"
    )(tiles, line)


def gather_plane(held, flips, axis):
    cut = held.shape[1] // 32 * 16
    across = lax.ppermute(held, axis, flips(2))
    along = lax.ppermute(held, axis, flips(4))
    corner_low = lax.ppermute(across[:, :cut], axis, flips(4))
    corner_high = lax.ppermute(along[:, cut:], axis, flips(2))
    even = jnp.concatenate([held, across, along, jnp.concatenate([corner_low, corner_high], axis=1)], axis=0)
    return even, lax.ppermute(even, axis, flips(1))


def gather_blocks(block, ranks, groups):
    if ranks == 4 and groups == 8:
        flips = lambda bits: [(i, i ^ bits) for i in range(groups)]
        turn = lambda step: [(i, (i + step) % ranks) for i in range(ranks)]
        one, three, two = [lax.ppermute(block, "tensor", turn(step)) for step in (1, 3, 2)]
        arrays, where = [], []
        for step, held in ((0, block), (1, one), (3, three), (2, two)):
            for parity, array in enumerate(gather_plane(held[None], flips, "dp")):
                arrays.append(array)
                where.append([(step, 2 * k + parity) for k in range(4)])
        return arrays, where, two
    return [lax.all_gather(block, ("dp", "tensor"), axis=0)], None, None


def assemble_kernel(target, *refs, sources, own_tiles, tile_rows):
    ins, outs = refs[:sources], refs[sources : sources + 7]
    staging, (f_qkv, f_ckv, f_cq, f_wo, f_co, f_in, f_out), arrived, sent = refs[sources + 7], refs[sources + 8 : -2], refs[-2], refs[-1]
    side = tile_rows * 2 // 3
    half = side // 2
    at = 0
    for source in ins:
        blocks = source.shape[0]

        def fetch(k, _, source=source, at=at):
            for slot in range(own_tiles):
                pltpu.make_async_copy(
                    source.at[k, pl.ds(slot * tile_rows, tile_rows)],
                    staging.at[target[at + k * own_tiles + slot]],
                    arrived,
                ).start()
            return 0

        lax.fori_loop(0, blocks, fetch, 0)
        at += blocks * own_tiles
    pltpu.make_async_copy(staging, staging, arrived).wait()

    def parts(rank, ident):
        packed = staging.at[rank * 64 + ident]
        low = packed[side:]
        return packed[:side], jnp.concatenate([low[:, : side - LANES], low[:, side - LANES :]], axis=0)

    def columns(out, base, offset):
        for rank in range(4):
            for i in range(4):
                main, rest = parts(rank, base + i)
                rest = jnp.concatenate([rest, jnp.zeros((side, SLOT - side), jnp.bfloat16)], axis=1)
                out[i * side : (i + 1) * side, offset + rank * SLOT : offset + (rank + 1) * SLOT] = jnp.concatenate([main, rest], axis=1)

    def joined(rank, base):
        pieces = []
        for i in range(4):
            pieces.extend(parts(rank, base + i))
        return jnp.concatenate(pieces, axis=1)

    def padded_rows(out, base):
        for rank in range(4):
            out[rank * SLOT : rank * SLOT + side, :] = joined(rank, base)
            out[rank * SLOT + side : (rank + 1) * SLOT, :] = jnp.zeros((SLOT - side, 4 * side), jnp.bfloat16)

    copies = []

    def send(i, held):
        copy = pltpu.make_async_copy(held, outs[i], sent.at[i])
        copy.start()
        copies.append(copy)

    for m, base in enumerate((0, 4, 8)):
        columns(f_qkv, base, m * 4 * SLOT)
    send(0, f_qkv)
    for m, base in enumerate((16, 20)):
        columns(f_ckv, base, m * 4 * SLOT)
    send(1, f_ckv)
    columns(f_cq, 12, 0)
    send(2, f_cq)
    padded_rows(f_wo, 24)
    send(3, f_wo)
    padded_rows(f_co, 28)
    send(4, f_co)
    for rank in range(4):
        for i in range(4):
            f_in[i * side : (i + 1) * side, rank * 4 * side : (rank + 1) * 4 * side] = joined(rank, 32 + 4 * i)
    send(5, f_in)
    for rank in range(4):
        for i in range(4):
            f_out[(rank * 4 + i) * side : (rank * 4 + i + 1) * side, :] = joined(rank, 48 + 4 * i)
    send(6, f_out)
    for copy in copies:
        copy.wait()


def assemble(target, arrays, own_tiles, side):
    width = 4 * side
    tile_rows = side + side // 2
    bf = jnp.bfloat16
    shapes = [
        (width, 12 * SLOT), (width, 8 * SLOT), (width, 4 * SLOT), (4 * SLOT, width), (4 * SLOT, width),
        (width, 4 * width), (4 * width, width),
    ]
    anywhere = pl.BlockSpec(memory_space=pl.ANY)
    return pl.pallas_call(
        functools.partial(assemble_kernel, sources=len(arrays), own_tiles=own_tiles, tile_rows=tile_rows),
        grid_spec=pltpu.PrefetchScalarGridSpec(
            num_scalar_prefetch=1,
            grid=(1,),
            in_specs=[anywhere] * len(arrays),
            out_specs=[anywhere] * 7,
            scratch_shapes=[pltpu.VMEM((256, tile_rows, LANES), bf)]
            + [pltpu.VMEM(shape, bf) for shape in shapes]
            + [pltpu.SemaphoreType.DMA, pltpu.SemaphoreType.DMA((7,))],
        ),
        out_shape=[jax.ShapeDtypeStruct(shape, bf) for shape in shapes],
        compiler_params=pltpu.CompilerParams(vmem_limit_bytes=56 * 2**20),
        name="assemble",
    )(target, *arrays)


def weight_grads_kernel(
    rank, place, n1, dqkv, n2, dcq, frames, dk, dv, attended, b1, mixed, b2, n3, grad_up, active, b3, out
):
    side = out.shape[1]

    def slots(made, bases):
        for m, base in enumerate(bases):
            for i in range(4):
                out[place[base + i]] = made[i * side : (i + 1) * side, m * SLOT : m * SLOT + side].astype(jnp.bfloat16)

    def grid_of(made, base, rows):
        for i in range(rows):
            for j in range(4):
                tile = made[i * side : (i + 1) * side, j * side : (j + 1) * side]
                out[place[base + i * 4 + j]] = tile.astype(jnp.bfloat16)

    slots(bdot(n1[...], dqkv[...], TN), (0, 4, 8))
    slots(bdot(n2[...], dcq[...], TN), (12,))
    slots(bdot(frames[0], dk[0], TN) + bdot(frames[1], dk[1], TN), (16,))
    slots(bdot(frames[0], dv[0], TN) + bdot(frames[1], dv[1], TN), (20,))
    grid_of(bdot(attended[...], b1[...], TN), 24, 1)
    grid_of(bdot(mixed[...], b2[...], TN), 28, 1)
    grid_of(bdot(n3[...], grad_up[...], TN), 32, 4)
    grid_of(bdot(active[...], b3[...], TN), 48, 4)


def weight_grads(rank, place, side, n1, dqkv, n2, dcq, frames, dk, dv, attended, b1, mixed, b2, n3, grad_up, active, b3):
    def whole(x):
        return pl.BlockSpec(x.shape, lambda i, rank, place: (0,) * x.ndim)

    def own(x, width):
        return pl.BlockSpec((x.shape[0], width), lambda i, rank, place: (0, rank[0]))

    shape = (place.shape[0], side, side)
    return pl.pallas_call(
        weight_grads_kernel,
        grid_spec=pltpu.PrefetchScalarGridSpec(
            num_scalar_prefetch=2,
            grid=(1,),
            in_specs=[
                whole(n1), whole(dqkv), whole(n2), own(dcq, SLOT), whole(frames), whole(dk), whole(dv),
                own(attended, SLOT), whole(b1), own(mixed, SLOT), whole(b2), whole(n3),
                own(grad_up, 4 * side), own(active, 4 * side), whole(b3),
            ],
            out_specs=pl.BlockSpec(shape, lambda i, rank, place: (0, 0, 0)),
        ),
        out_shape=jax.ShapeDtypeStruct(shape, jnp.bfloat16),
        compiler_params=pltpu.CompilerParams(vmem_limit_bytes=60 * 2**20),
        name="weight_grads",
    )(rank, place, n1, dqkv, n2, dcq, frames, dk, dv, attended, b1, mixed, b2, n3, grad_up, active, b3)


def frames_kernel(frames, weight, bias, out):
    out[0] = (bdot(frames[0], weight[...], NN) + bias[...]).astype(jnp.bfloat16)


def frame_projection(frames, weight, bias):
    seqs, count, width = frames.shape
    total = weight.shape[1]
    return pl.pallas_call(
        frames_kernel,
        grid=(seqs, total // 512),
        in_specs=[
            pl.BlockSpec((1, count, width), lambda b, c: (b, 0, 0)),
            pl.BlockSpec((width, 512), lambda b, c: (0, c)),
            pl.BlockSpec((1, 512), lambda b, c: (0, c)),
        ],
        out_specs=pl.BlockSpec((1, count, 512), lambda b, c: (b, 0, c)),
        out_shape=jax.ShapeDtypeStruct((seqs, count, total), jnp.bfloat16),
        compiler_params=pltpu.CompilerParams(vmem_limit_bytes=VM),
        name="frame_projection",
    )(frames, weight, bias[None])


def frames_back_kernel(rank, dk, dv, key_weight, value_weight, out, *, parts):
    made = bdot(dk[0], key_weight[...], NT) + bdot(dv[0], value_weight[...], NT)
    share = made.shape[0] // parts
    for part in range(parts):
        piece = made[part * share : (part + 1) * share]
        out[part, 0] = jnp.concatenate([piece, jnp.zeros((out.shape[2] - share, piece.shape[1]), jnp.float32)], axis=0).astype(jnp.bfloat16)


def frames_back(rank, dk, dv, weight, parts):
    seqs, count, slot = dk.shape
    width = weight.shape[0]
    padded = -(-(count // parts) // 16) * 16
    own = pl.BlockSpec((1, count, slot), lambda b, rank: (b, 0, 0))
    return pl.pallas_call(
        functools.partial(frames_back_kernel, parts=parts),
        grid_spec=pltpu.PrefetchScalarGridSpec(
            num_scalar_prefetch=1,
            grid=(seqs,),
            in_specs=[
                own, own,
                pl.BlockSpec((width, slot), lambda b, rank: (0, rank[0])),
                pl.BlockSpec((width, slot), lambda b, rank: (0, parts + rank[0])),
            ],
            out_specs=pl.BlockSpec((parts, 1, padded, width), lambda b, rank: (0, b, 0, 0)),
        ),
        out_shape=jax.ShapeDtypeStruct((parts, seqs, padded, width), jnp.bfloat16),
        compiler_params=pltpu.CompilerParams(vmem_limit_bytes=VM),
        name="frames_back",
    )(rank, dk, dv, weight, weight)


def product(left_part, right_part):
    return jnp.dot(left_part, right_part, preferred_element_type=jnp.float32)


def times_transpose(left_part, right_part):
    return lax.dot_general(left_part, right_part, (NT, ((), ())), preferred_element_type=jnp.float32)


def unit_rows(values):
    centre = jnp.mean(values, axis=-1, keepdims=True)
    centred = values - centre
    inverse = lax.rsqrt(jnp.mean(centred * centred, axis=-1, keepdims=True) + norm_eps)
    return centred * inverse, inverse


def normalize(values, gain, shift):
    return unit_rows(values)[0] * gain + shift


def normalize_back(values, gain, grads):
    unit, inverse = unit_rows(values)
    scaled = grads * gain
    result = inverse * (
        scaled
        - jnp.mean(scaled, axis=-1, keepdims=True)
        - unit * jnp.mean(scaled * unit, axis=-1, keepdims=True)
    )
    return result, jnp.sum(grads * unit, axis=0), jnp.sum(grads, axis=0)


def gelu_pair(value):
    size = jnp.abs(value) * 0.7071067811865476
    bell = jnp.exp(-size * size)
    t = 1.0 / (1.0 + 0.3275911 * size)
    poly = t * (0.254829592 + t * (-0.284496736 + t * (1.421413741 + t * (-1.453152027 + t * 1.061405429))))
    tail = 0.5 * poly * bell
    level = jnp.where(value >= 0, 1.0 - tail, tail)
    return value * level, level + value * bell * 0.3989422804014327


def spread_heads(rows, ranks):
    lead = rows.shape[0]
    side = rows.shape[1] // ranks
    return jnp.pad(rows.reshape(lead, ranks, side), ((0, 0), (0, 0), (0, SLOT - side))).reshape(lead, ranks * SLOT)


def shards(
    hidden_in, frames, cotangent, segments, stamps, owner_list, master_tiles, tile_first, tile_second,
    tile_stats, tile_bases, master_vectors, vector_first, vector_second,
):
    f32, bf16 = jnp.float32, jnp.bfloat16
    ranks, groups = lax.axis_size("tensor"), lax.axis_size("dp")
    rank, group = lax.axis_index("tensor"), lax.axis_index("dp")
    seqs, local_rows, width = hidden_in.shape
    rows = local_rows * ranks
    tokens = seqs * rows
    own_tiles, side = master_tiles.shape[1], master_tiles.shape[-1]
    heads = side // HEAD
    rank_ref = rank.astype(jnp.int32)[None]

    length = master_vectors.shape[0]
    line_rows = -(-length // (16 * LANES)) * 16
    line = jnp.pad(master_vectors, (0, line_rows * LANES - length)).reshape(line_rows, LANES)
    block = pack(master_tiles[0], line)
    arrays, where, last = gather_blocks(block, ranks, groups)
    if where is None:
        source_rank = jnp.tile(jnp.arange(ranks, dtype=jnp.int32), groups)
        source_group = jnp.repeat(jnp.arange(groups, dtype=jnp.int32), ranks)
        lines = arrays[0].reshape(groups, ranks, -1, LANES)[:, 0, -line_rows:].reshape(groups, -1)[:, :length]
    else:
        steps = jnp.array([step for array in where for step, _ in array], jnp.int32)
        bits = jnp.array([bit for array in where for _, bit in array], jnp.int32)
        source_rank = (rank - steps) % ranks
        source_group = group ^ bits
        lines = jnp.concatenate([array[:, -line_rows:] for array in arrays[:2]], axis=0).reshape(groups, -1)[:, :length]
        spots = source_group[:groups]
        order = jnp.arange(groups, dtype=jnp.int32)
        lines = jnp.sum(jnp.where((spots[None] == order[:, None])[:, :, None], lines[None].astype(f32), 0.0), axis=1)
    vectors = lines.astype(f32).reshape(19, width)

    count = owner_list.shape[0]
    position = jnp.arange(count, dtype=jnp.int32)
    place = jnp.sum(jnp.where(owner_list[None, :] == position[:, None], position[None, :], 0), axis=1)
    spot = (source_group[:, None] * own_tiles + jnp.arange(own_tiles, dtype=jnp.int32)[None]).reshape(-1)
    ident = jnp.sum(jnp.where(spot[:, None] == position[None, :], owner_list[None, :], 0), axis=1)
    target = jnp.repeat(source_rank, own_tiles) * count + ident
    w_qkv, c_kv, c_q, w_o, c_o, w_in, w_out = assemble(target, arrays, own_tiles, side)

    rows_in = jnp.stack([hidden_in, cotangent])
    if where is not None:
        rows_in, _ = lax.optimization_barrier((rows_in, last))
    both = lax.all_gather(rows_in, "tensor", axis=2, tiled=True)
    hidden = both[0].reshape(tokens, width).astype(f32)
    top_grad = both[1].reshape(tokens, width).astype(f32)

    head_bias = spread_heads(vectors[11:15], ranks)
    none = jnp.zeros_like(head_bias[0])
    inner_bias = vectors[15:19].reshape(-1)
    seg_col, seg_row = segments[:, :, None], segments[:, None, :]
    stamp_col, stamp_row = stamps[:, :, None], stamps[:, None, :]

    def split(values):
        return values.reshape(seqs, rows, values.shape[-1])

    def flat(values):
        return values.reshape(tokens, values.shape[-1])

    def own_rows(values):
        return lax.dynamic_slice_in_dim(split(values), rank * local_rows, local_rows, axis=1)

    keys_values = frame_projection(frames, c_kv, jnp.concatenate([none, head_bias[3]]))
    n1 = normalize(hidden, vectors[0], vectors[1]).astype(bf16)
    qkv = split((product(n1, w_qkv) + jnp.concatenate([head_bias[0], none, head_bias[1]])).astype(bf16))
    attended, self_logs = self_forward(qkv, seg_col, seg_row, stamp_row, ranks, heads)
    attended = flat(attended)
    first_sum = hidden + product(attended, w_o) + vectors[8]
    n2 = normalize(first_sum, vectors[2], vectors[3]).astype(bf16)
    cross_queries = split((product(n2, c_q) + head_bias[2]).astype(bf16))
    mixed, cross_logs = cross_forward(cross_queries, keys_values, ranks, heads)
    mixed = flat(mixed)
    second_sum = first_sum + product(mixed, c_o) + vectors[9]
    n3 = normalize(second_sum, vectors[4], vectors[5]).astype(bf16)
    active, slope = gelu_pair(product(n3, w_in) + inner_bias)
    active, slope = active.astype(bf16), slope.astype(bf16)
    third_sum = second_sum + product(active, w_out) + vectors[10]
    block_out = own_rows(normalize(third_sum, vectors[6], vectors[7]))

    grad_third, gain_final, shift_final = normalize_back(third_sum, vectors[6], top_grad)
    b3 = grad_third.astype(bf16)
    grad_up = (times_transpose(b3, w_out) * slope.astype(f32)).astype(bf16)
    back, gain_three, shift_three = normalize_back(second_sum, vectors[4], times_transpose(grad_up, w_in))
    grad_second = grad_third + back
    b2 = grad_second.astype(bf16)
    grad_mixed = split(times_transpose(b2, c_o).astype(bf16))
    dcq, dk, dv = cross_backward(
        rank_ref, cross_queries, keys_values, grad_mixed, split(mixed), cross_logs, ranks, heads
    )
    dcq = flat(dcq)
    frames_part = frames_back(rank_ref, dk, dv, c_kv, ranks)
    frames_sum = lax.psum_scatter(
        frames_part.reshape(ranks * seqs, frames_part.shape[2], width), "tensor", scatter_dimension=0, tiled=True
    )
    frames_grad = frames_sum[:, : frames.shape[1] // ranks].astype(f32)
    back, gain_two, shift_two = normalize_back(first_sum, vectors[2], times_transpose(dcq, c_q))
    grad_first = grad_second + back
    b1 = grad_first.astype(bf16)
    grad_attended = split(times_transpose(b1, w_o).astype(bf16))
    dqkv = flat(
        self_backward(
            rank_ref, qkv, grad_attended, split(attended), self_logs, seg_col, seg_row, stamp_col, ranks, heads
        )
    )

    own_weight = lax.dynamic_slice_in_dim(w_qkv.reshape(width, 3, ranks * SLOT), rank * SLOT, SLOT, axis=2)
    part_one = times_transpose(dqkv, own_weight.reshape(width, 3 * SLOT))
    unit_one, _ = unit_rows(hidden)
    gain_one, shift_one = jnp.sum(part_one * unit_one, axis=0), jnp.sum(part_one, axis=0)
    grad_one = lax.psum_scatter(split(part_one.astype(bf16)), "tensor", scatter_dimension=1, tiled=True).astype(f32)
    back, _, _ = normalize_back(
        hidden_in.astype(f32).reshape(-1, width), vectors[0], grad_one.reshape(-1, width)
    )
    input_grad = own_rows(grad_first) + back.reshape(hidden_in.shape)

    tile_terms = weight_grads(
        rank_ref, place, side, n1, dqkv, n2, dcq, frames, dk, dv, attended, b1, mixed, b2, n3, grad_up, active, b3
    )
    owned_grads = lax.psum_scatter(tile_terms, "dp", scatter_dimension=0, tiled=True)

    def total(values):
        return jnp.sum(values.astype(f32), axis=tuple(range(values.ndim - 1)))

    same = jnp.stack(
        [gain_two, shift_two, gain_three, shift_three, gain_final, shift_final, total(b1), total(b2), total(b3)]
    )
    query_sum = total(dcq).reshape(ranks, SLOT)[:, :side].reshape(1, width)
    up_sum = total(grad_up).reshape(4, width)
    even = 1.0 / ranks
    dqkv_sum = total(dqkv)
    own_sums = jnp.stack([dqkv_sum[:side], dqkv_sum[2 * SLOT : 2 * SLOT + side], total(dv)[:side]])
    own_sums = lax.dynamic_update_slice(jnp.zeros((3, width), f32), own_sums, (0, rank * side))
    vector_terms = jnp.concatenate(
        [gain_one[None], shift_one[None], same * even, own_sums[:2], query_sum * even, own_sums[2:], up_sum * even]
    )
    vector_sums = lax.psum(vector_terms.reshape(-1), ("dp", "tensor"))
    vector_grad = lax.dynamic_slice_in_dim(vector_sums, group * length, length)

    new_first, new_second, new_master, new_stats, new_bases = soap(
        owned_grads, master_tiles[0], tile_first[0], tile_second[0], tile_stats[0], tile_bases[0]
    )
    new_vector_first = beta_one * vector_first + (1.0 - beta_one) * vector_grad
    new_vector_second = beta_two * vector_second + (1.0 - beta_two) * vector_grad * vector_grad
    new_vectors = master_vectors - rate_vectors * (new_vector_first / (1.0 - beta_one**STEP)) / (
        jnp.sqrt(new_vector_second / (1.0 - beta_two**STEP)) + adam_eps
    )
    return (
        block_out, input_grad, frames_grad, new_master[None], new_first[None], new_second[None],
        new_stats[None], new_bases[None], new_vectors, new_vector_first, new_vector_second,
    )


def solution(mesh):
    rows, seqs, tiles, pairs = (
        P("dp", "tensor", None), P("dp", None), P("tensor", "dp", None, None), P("tensor", "dp", None, None, None)
    )
    line = P("dp")
    in_specs = (
        rows, P("dp", None, None), rows, seqs, seqs, P(), tiles, tiles, tiles, pairs, pairs, line, line, line
    )
    out_specs = (rows, rows, rows, tiles, tiles, tiles, pairs, pairs, line, line, line)
    return jax.shard_map(shards, mesh=mesh, in_specs=in_specs, out_specs=out_specs, check_vma=False)
```

```python
import functools

import jax
import jax.numpy as jnp
from jax import lax
from jax.experimental import pallas as pl
from jax.experimental.pallas import tpu as pltpu
from jax.experimental.layout import Layout, with_layout_constraint
from jax.sharding import PartitionSpec as P

HEAD = 64
FF = 3072
STEP = 5
LANES = 128
SLOT = 256
VM = 56 * 2**20
HI = lax.Precision.HIGHEST

norm_eps = 1e-05
beta_one = 0.9
beta_two = 0.95
adam_eps = 1e-08
rate_tiles = 0.05
rate_vectors = 0.3
score_scale = 0.125


def split2(a):
    hi = a.astype(jnp.bfloat16)
    lo = (a - hi.astype(jnp.float32)).astype(jnp.bfloat16)
    return hi, lo

def bdot(a, b, dims):
    return lax.dot_general(a, b, (dims, ((), ())), preferred_element_type=jnp.float32)

NN = ((1,), (0,)); TN = ((0,), (0,)); NT = ((1,), (1,))

def dot3(a, b, dims):
    (ah, al), (bh, bl) = a, b
    return bdot(ah, bh, dims) + (bdot(ah, bl, dims) + bdot(al, bh, dims))

def dothi(a, b, dims):
    return lax.dot_general(a, b, (dims, ((), ())), precision=HI, preferred_element_type=jnp.float32)

def soap_pre_kernel(first, stats, bases, rot_first, stats_rot):
    ql, qr = split2(bases[0, 0]), split2(bases[0, 1])
    inner = split2(dot3(ql, split2(first[0]), TN))
    rot_first[0] = dot3(inner, qr, NN)
    stats_rot[0, 0] = dot3(split2(stats[0, 0]), ql, NN)
    stats_rot[0, 1] = dot3(split2(stats[0, 1]), qr, NN)

def soap_main_kernel(grad, master, first, second, stats, bases, rot_first, stats_rot,
                     new_master, new_first, new_second, new_stats, turned, grams):
    side = master.shape[1]
    rest = grad[side:]
    rest = jnp.concatenate([rest[:, : side - LANES], rest[:, side - LANES :]], axis=0)
    g32 = jnp.concatenate([grad[:side], rest], axis=1)
    g, ql, qr = split2(g32), split2(bases[0, 0]), split2(bases[0, 1])
    new_first[0] = beta_one * first[0] + (1.0 - beta_one) * g32
    part_left = split2(dot3(ql, g, TN))
    rotated = dot3(part_left, qr, NN)
    fresh = beta_two * second[0] + (1.0 - beta_two) * rotated * rotated
    new_second[0] = fresh
    moment = (beta_one * rot_first[0] + (1.0 - beta_one) * rotated) / (1.0 - beta_one**STEP)
    step = moment / (jnp.sqrt(fresh / (1.0 - beta_two**STEP)) + adam_eps)
    back = split2(dot3(ql, split2(step), NN))
    new_master[0] = master[0] - rate_tiles * dot3(back, qr, NT)
    new_stats[0, 0] = beta_two * stats[0, 0] + (1.0 - beta_two) * dot3(g, g, NT)
    new_stats[0, 1] = beta_two * stats[0, 1] + (1.0 - beta_two) * dot3(g, g, TN)
    part_right = split2(dot3(g, qr, NN))
    for side, term in ((0, dot3(g, part_left, NT)), (1, dot3(g, part_right, TN))):
        side_turned = beta_two * stats_rot[0, side] + (1.0 - beta_two) * term
        turned[0, side] = side_turned
        halves = split2(side_turned)
        grams[0, side] = dot3(halves, halves, TN)

def chol_kernel(turned, grams, out, work, fac, *, block, unroll, passes):
    count, side = work.shape[0], work.shape[1]
    wide = work.shape[2] // 2
    for m in range(count):
        work[m, :, :side] = grams[m]
        work[m, :, side:wide] = jnp.zeros((side, wide - side), jnp.float32)
        work[m, :, wide : wide + side] = turned[m].T
        work[m, :, wide + side :] = jnp.zeros((side, wide - side), jnp.float32)
    brow = lax.broadcasted_iota(jnp.int32, (count, block, 2 * block), 1)
    bcol = lax.broadcasted_iota(jnp.int32, (count, block, 2 * block), 2)
    aug_eye = ((bcol - block) == brow).astype(jnp.float32)
    for k in range(side // block):
        lo, hi = k * block, (k + 1) * block
        diag = work[:, lo:hi, lo:hi]
        w = jnp.concatenate([diag, jnp.zeros_like(diag)], axis=2) + aug_eye
        for j in range(block - 1):
            piv = w[:, j : j + 1, :]
            ratio = w[:, :, j : j + 1] / w[:, j : j + 1, j : j + 1]
            w = w - jnp.where(brow > j, ratio * piv, 0.0)
        d = jnp.sum(jnp.where(brow == bcol, w, 0.0), axis=2, keepdims=True)
        fac[...] = w[:, :, block:] * lax.rsqrt(d)

        def several(i, _):
            for u in range(unroll):
                m = i * unroll + u
                if passes == 6:
                    y = dothi(fac[m], work[m, lo:hi, :], NN)
                else:
                    y = dot3(split2(fac[m]), split2(work[m, lo:hi, :]), NN)
                work[m, lo:hi, :] = y
                if hi < side:
                    turn = y[:, :side].T[hi:]
                    if passes == 6:
                        step = dothi(turn, y, NN)
                    else:
                        step = dot3(split2(turn), split2(y), NN)
                    work[m, hi:, :] = work[m, hi:, :] - step
            return 0
        lax.fori_loop(0, count // unroll, several, 0)
    for m in range(count):
        out[m] = work[m, :, wide : wide + side].T

def tile_spec(side):
    return pl.BlockSpec((1, side, side), lambda i: (i, 0, 0))
def pair_spec(side):
    return pl.BlockSpec((1, 2, side, side), lambda i: (i, 0, 0, 0))

def soap_pre(first, stats, bases):
    n, side = first.shape[0], first.shape[1]
    t, p = tile_spec(side), pair_spec(side)
    return pl.pallas_call(soap_pre_kernel, grid=(n,), in_specs=[t, p, p], out_specs=[t, p],
        out_shape=[jax.ShapeDtypeStruct(first.shape, jnp.float32), jax.ShapeDtypeStruct(stats.shape, jnp.float32)],
        name="soap_pre")(first, stats, bases)

def soap_main(grad, master, first, second, stats, bases, rot_first, stats_rot):
    n, side = first.shape[0], first.shape[1]
    t, p = tile_spec(side), pair_spec(side)
    f = jnp.float32
    ts, ps = jax.ShapeDtypeStruct(first.shape, f), jax.ShapeDtypeStruct(stats.shape, f)
    return pl.pallas_call(soap_main_kernel, grid=(n,), in_specs=[pl.BlockSpec((side + side // 2, LANES), lambda i: (i, 0)), t, t, t, p, p, t, p],
        out_specs=[t, t, t, p, p, p], out_shape=[ts, ts, ts, ps, ps, ps], name="soap_main")(
        grad, master, first, second, stats, bases, rot_first, stats_rot)

def chol_bases(turned, grams, block=64, unroll=4, passes=3):
    n, _, side, _ = turned.shape
    shape = (2 * n, side, side)
    unroll = min(unroll, 2 * n)
    out = pl.pallas_call(functools.partial(chol_kernel, block=block, unroll=unroll, passes=passes),
        out_shape=jax.ShapeDtypeStruct(shape, jnp.float32),
        scratch_shapes=[pltpu.VMEM((2 * n, side, 512), jnp.float32), pltpu.VMEM((2*n, block, block), jnp.float32)],
        compiler_params=pltpu.CompilerParams(vmem_limit_bytes=48 * 2**20), name="chol_bases")(
        turned.reshape(shape), grams.reshape(shape))
    return out.reshape(turned.shape)


def soap(gradient, master, first, second, statistics, bases, rot_first, stats_rot):
    nm, nf, ns, nst, turned, grams = soap_main(gradient, master, first, second, statistics, bases, rot_first, stats_rot)
    return nf, ns, nm, nst, chol_bases(turned, grams)


def head_pick(shape, head):
    lane = lax.broadcasted_iota(jnp.int32, shape, len(shape) - 1)
    return (lane >= HEAD) if head % 2 else (lane < HEAD)


def forward_heads(query, key, value, allowed, heads, chunk):
    rows = query.shape[0]
    units = [(low, head) for low in range(0, rows, chunk) for head in range(heads)]
    spans = [slice(head // 2 * LANES, head // 2 * LANES + LANES) for head in range(heads)]
    own_values = []
    for head in range(heads):
        block = value[:, spans[head]]
        own_values.append(jnp.where(head_pick(block.shape, head), block, jnp.ones_like(block)))

    def scores_of(unit):
        low, head = unit
        block = query[low : low + chunk, spans[head]]
        own = jnp.where(head_pick(block.shape, head), block, jnp.zeros_like(block)) * jnp.bfloat16(score_scale)
        return bdot(own, key[:, spans[head]], NT)

    done, logs = {}, {}
    ahead = scores_of(units[0])
    for i, (low, head) in enumerate(units):
        scores = ahead
        if i + 1 < len(units):
            ahead = scores_of(units[i + 1])
        if allowed is not None:
            scores = jnp.where(allowed[low : low + chunk], scores, -1e30)
        top = jnp.max(scores, axis=1, keepdims=True)
        weights = jnp.exp(scores - top).astype(jnp.bfloat16)
        both = bdot(weights, own_values[head], NN)
        turned = pltpu.roll(both, HEAD, 1)
        pick = head_pick(both.shape, head)
        done[low, head] = both / turned
        logs[low, head] = top + jnp.log(jnp.where(pick, turned, both))
    columns, lines = [], []
    for low in range(0, rows, chunk):
        blocks = []
        lane = lax.broadcasted_iota(jnp.int32, (chunk, LANES), 1)
        line = jnp.zeros((chunk, LANES), jnp.float32)
        for first in range(0, heads, 2):
            other = done[low, first + 1] if first + 1 < heads else 0.0
            blocks.append(jnp.where(lane < HEAD, done[low, first], other).astype(jnp.bfloat16))
        for head in range(heads):
            line = jnp.where(lane == head, logs[low, head], line)
        columns.append(jnp.concatenate(blocks, axis=1))
        lines.append(line)
    return jnp.concatenate(columns, axis=0), jnp.concatenate(lines, axis=0).T[:8]


def cross_forward_kernel(query, key, value, out, logs, *, heads, chunk):
    out[0], logs[0, 0] = forward_heads(query[0], key[0], value[0], None, heads, chunk)


def self_forward_kernel(query, key, value, seg_col, seg_row, stamp_row, out, logs, *, heads, chunk):
    rows = query.shape[1]
    at = lax.broadcasted_iota(jnp.int32, (rows, rows), 0)
    key_at = lax.broadcasted_iota(jnp.int32, (rows, rows), 1)
    allowed = (key_at <= at) & (seg_col[0] == seg_row[0]) & ((stamp_row[0] == 0) | (key_at == at))
    out[0], logs[0, 0] = forward_heads(query[0], key[0], value[0], allowed, heads, chunk)


def backward_heads(query, key, value, grad, mixed, logs, allowed, heads, chunk, probs_ref, scores_ref):
    keys = key.shape[0]
    spans = [slice(head // 2 * LANES, head // 2 * LANES + LANES) for head in range(heads)]
    products = (grad.astype(jnp.float32) * mixed.astype(jnp.float32)).T
    own_query, own_grad, turned, dots, total = [], [], [], [], [None] * heads
    for head in range(heads):
        pick = head_pick((query.shape[0], LANES), head)
        zero = jnp.zeros((query.shape[0], LANES), jnp.bfloat16)
        own_query.append(jnp.where(pick, query[:, spans[head]], zero) * jnp.bfloat16(score_scale))
        own_grad.append(jnp.where(pick, grad[:, spans[head]], zero))
        dots.append(jnp.sum(products[head * HEAD : (head + 1) * HEAD], axis=0, keepdims=True))
        if head % 2 == 0:
            turned.append(key[:, spans[head]].T)
    units = [(low, head) for low in range(0, keys, chunk) for head in range(heads)]

    def products_of(unit):
        low, head = unit
        high = min(low + chunk, keys)
        return bdot(key[low:high, spans[head]], own_query[head], NT), bdot(value[low:high, spans[head]], own_grad[head], NT)

    ahead = products_of(units[0])
    for i, (low, head) in enumerate(units):
        high = min(low + chunk, keys)
        scores, grad_probs = ahead
        if i + 1 < len(units):
            ahead = products_of(units[i + 1])
        if allowed is not None:
            scores = jnp.where(allowed[low:high], scores, -1e30)
        probs = jnp.exp(scores - logs[head : head + 1])
        grad_scores = (probs * (grad_probs - dots[head])).astype(jnp.bfloat16)
        probs_ref[head, low:high] = probs.astype(jnp.bfloat16)
        scores_ref[head, low:high] = grad_scores
        half = head % 2 * HEAD
        term = bdot(turned[head // 2][half : half + HEAD, low:high], grad_scores, NN)
        total[head] = term if total[head] is None else total[head] + term
    if heads % 2:
        total.append(jnp.zeros_like(total[0]))
    return (jnp.concatenate(total, axis=0).T * score_scale).astype(jnp.bfloat16)


def key_value_grads(query, grad, heads, probs_ref, scores_ref):
    keys, values = [], []
    for first in range(0, heads, 2):
        span = slice(first * HEAD, first * HEAD + LANES)
        made_key = made_value = None
        for head in range(first, min(first + 2, heads)):
            grad_key = bdot(scores_ref[head], query[:, span], NN) * score_scale
            grad_value = bdot(probs_ref[head], grad[:, span], NN)
            pick = head_pick(grad_key.shape, head)
            made_key = jnp.where(pick, grad_key, 0.0 if made_key is None else made_key)
            made_value = jnp.where(pick, grad_value, 0.0 if made_value is None else made_value)
        keys.append(made_key.astype(jnp.bfloat16))
        values.append(made_value.astype(jnp.bfloat16))
    return jnp.concatenate(keys, axis=1), jnp.concatenate(values, axis=1)


def cross_backward_kernel(
    rank, query, key, value, grad, mixed, logs, grad_query, grad_key, grad_value, probs_ref, scores_ref, *, heads, chunk
):
    grad_query[0] = backward_heads(
        query[0], key[0], value[0], grad[0], mixed[0], logs[0, 0], None, heads, chunk, probs_ref, scores_ref
    )

    @pl.when(pl.program_id(1) == rank[0])
    def _():
        made = key_value_grads(query[0], grad[0], heads, probs_ref, scores_ref)
        grad_key[0], grad_value[0] = made


def self_backward_kernel(
    rank, query, key, value, grad, mixed, logs, seg_col, seg_row, stamp_col, out, probs_ref, scores_ref, *, heads, chunk
):
    rows = query.shape[1]
    key_at = lax.broadcasted_iota(jnp.int32, (rows, rows), 0)
    at = lax.broadcasted_iota(jnp.int32, (rows, rows), 1)
    allowed = (key_at <= at) & (seg_col[0] == seg_row[0]) & ((stamp_col[0] == 0) | (key_at == at))
    grad_query = backward_heads(
        query[0], key[0], value[0], grad[0], mixed[0], logs[0, 0], allowed, heads, chunk, probs_ref, scores_ref
    )
    grad_key, grad_value = key_value_grads(query[0], grad[0], heads, probs_ref, scores_ref)
    out[0] = jnp.concatenate([grad_query, grad_key, grad_value], axis=1)


def slot_spec(rows, offset):
    return pl.BlockSpec((1, rows, SLOT), lambda b, r: (b, 0, offset + r))


def self_forward(qkv, seg_col, seg_row, stamp_row, ranks, heads, chunk=448):
    seqs, rows, _ = qkv.shape
    col = pl.BlockSpec((1, rows, 1), lambda b, r: (b, 0, 0))
    row = pl.BlockSpec((1, 1, rows), lambda b, r: (b, 0, 0))
    return pl.pallas_call(
        functools.partial(self_forward_kernel, heads=heads, chunk=chunk),
        grid=(seqs, ranks),
        in_specs=[slot_spec(rows, 0), slot_spec(rows, ranks), slot_spec(rows, 2 * ranks), col, row, row],
        out_specs=[slot_spec(rows, 0), pl.BlockSpec((1, 1, 8, rows), lambda b, r: (b, r, 0, 0))],
        out_shape=[
            jax.ShapeDtypeStruct((seqs, rows, ranks * SLOT), jnp.bfloat16),
            jax.ShapeDtypeStruct((seqs, ranks, 8, rows), jnp.float32),
        ],
        compiler_params=pltpu.CompilerParams(vmem_limit_bytes=VM),
        name="self_forward",
    )(qkv, qkv, qkv, seg_col, seg_row, stamp_row)


def cross_forward(queries, keys_values, ranks, heads, chunk=448):
    seqs, rows, _ = queries.shape
    frames = keys_values.shape[1]
    return pl.pallas_call(
        functools.partial(cross_forward_kernel, heads=heads, chunk=chunk),
        grid=(seqs, ranks),
        in_specs=[slot_spec(rows, 0), slot_spec(frames, 0), slot_spec(frames, ranks)],
        out_specs=[slot_spec(rows, 0), pl.BlockSpec((1, 1, 8, rows), lambda b, r: (b, r, 0, 0))],
        out_shape=[
            jax.ShapeDtypeStruct((seqs, rows, ranks * SLOT), jnp.bfloat16),
            jax.ShapeDtypeStruct((seqs, ranks, 8, rows), jnp.float32),
        ],
        compiler_params=pltpu.CompilerParams(vmem_limit_bytes=VM),
        name="cross_forward",
    )(queries, keys_values, keys_values)


def ranked_spec(rows, offset):
    return pl.BlockSpec((1, rows, SLOT), lambda b, r, rank: (b, 0, offset + r))


def cross_backward(rank, queries, keys_values, grads, mixed, logs, ranks, heads, chunk=512):
    seqs, rows, _ = queries.shape
    frames = keys_values.shape[1]
    kept = pl.BlockSpec((1, frames, SLOT), lambda b, r, rank: (b, 0, 0))
    bf = jnp.bfloat16
    return pl.pallas_call(
        functools.partial(cross_backward_kernel, heads=heads, chunk=chunk),
        grid_spec=pltpu.PrefetchScalarGridSpec(
            num_scalar_prefetch=1,
            grid=(seqs, ranks),
            in_specs=[
                ranked_spec(rows, 0), ranked_spec(frames, 0), ranked_spec(frames, ranks), ranked_spec(rows, 0), ranked_spec(rows, 0),
                pl.BlockSpec((1, 1, 8, rows), lambda b, r, rank: (b, r, 0, 0)),
            ],
            out_specs=[ranked_spec(rows, 0), kept, kept],
            scratch_shapes=[pltpu.VMEM((heads, frames, rows), bf), pltpu.VMEM((heads, frames, rows), bf)],
        ),
        out_shape=[
            jax.ShapeDtypeStruct((seqs, rows, ranks * SLOT), bf),
            jax.ShapeDtypeStruct((seqs, frames, SLOT), bf),
            jax.ShapeDtypeStruct((seqs, frames, SLOT), bf),
        ],
        compiler_params=pltpu.CompilerParams(vmem_limit_bytes=VM),
        name="cross_backward",
    )(rank, queries, keys_values, keys_values, grads, mixed, logs)


def self_backward(rank, qkv, grads, mixed, logs, seg_col, seg_row, stamp_col, ranks, heads, chunk=224):
    seqs, rows, _ = qkv.shape
    bf = jnp.bfloat16
    own = lambda offset: pl.BlockSpec((1, rows, SLOT), lambda b, rank: (b, 0, offset + rank[0]))
    col = pl.BlockSpec((1, rows, 1), lambda b, rank: (b, 0, 0))
    row = pl.BlockSpec((1, 1, rows), lambda b, rank: (b, 0, 0))
    return pl.pallas_call(
        functools.partial(self_backward_kernel, heads=heads, chunk=chunk),
        grid_spec=pltpu.PrefetchScalarGridSpec(
            num_scalar_prefetch=1,
            grid=(seqs,),
            in_specs=[
                own(0), own(ranks), own(2 * ranks), own(0), own(0),
                pl.BlockSpec((1, 1, 8, rows), lambda b, rank: (b, rank[0], 0, 0)), col, row, col,
            ],
            out_specs=pl.BlockSpec((1, rows, 3 * SLOT), lambda b, rank: (b, 0, 0)),
            scratch_shapes=[pltpu.VMEM((heads, rows, rows), bf), pltpu.VMEM((heads, rows, rows), bf)],
        ),
        out_shape=jax.ShapeDtypeStruct((seqs, rows, 3 * SLOT), bf),
        compiler_params=pltpu.CompilerParams(vmem_limit_bytes=VM),
        name="self_backward",
    )(rank, qkv, qkv, qkv, grads, mixed, logs, seg_col, seg_row, stamp_col)


def pack_kernel(tiles, line, out):
    side = tiles.shape[1]
    half, extra = side // 2, side - LANES
    for i in range(tiles.shape[0]):
        tile = tiles[i].astype(jnp.bfloat16)
        low = i * (side + half)
        out[low : low + side] = tile[:, :LANES]
        out[low + side : low + side + half] = jnp.concatenate([tile[:half, LANES:], tile[half:, LANES:]], axis=1)
    out[out.shape[0] - line.shape[0] :] = line[...].astype(jnp.bfloat16)


def pack(tiles, line):
    count, side, _ = tiles.shape
    rows = count * (side + side // 2) + line.shape[0]
    return pl.pallas_call(
        pack_kernel, out_shape=jax.ShapeDtypeStruct((rows, LANES), jnp.bfloat16), name="pack"
    )(tiles, line)


def gather_blocks(block, ranks, groups, ready):
    if ranks != 4 or groups != 8:
        return [lax.all_gather(block, ("dp", "tensor"), axis=0)], None, None, ready

    def flip(values, bits):
        return lax.ppermute(values, "dp", [(i, i ^ bits) for i in range(groups)])

    def turn(values, step):
        return lax.ppermute(values, "tensor", [(i, (i + step) % ranks) for i in range(ranks)])

    cut = block.shape[0] // 32 * 16
    one, three = turn(block, 1), turn(block, 3)
    held = block[None]
    sides = flip(held, 2), flip(held, 4)
    later, _ = lax.optimization_barrier((block, sides))
    two = turn(later, 2)
    units, before = [(0, held, sides)], sides
    for step, values in ((1, one), (3, three), (2, two)):
        if step == 1:
            values, ready = lax.optimization_barrier((values, ready))
        held, _ = lax.optimization_barrier((values[None], before))
        before = flip(held, 2), flip(held, 4)
        units.append((step, held, before))
    arrays, where = [], []
    for step, held, (across, along) in units:
        low, high = flip(across[:, :cut], 4), flip(along[:, cut:], 2)
        even = jnp.concatenate([held, across, along, jnp.concatenate([low, high], axis=1)], axis=0)
        for parity, array in enumerate((even, flip(even, 1))):
            arrays.append(array)
            where.append([(step, 2 * k + parity) for k in range(4)])
    return arrays, where, two, ready


def assemble_kernel(target, *refs, sources, own_tiles, tile_rows):
    ins, outs = refs[:sources], refs[sources : sources + 7]
    staging, (f_qkv, f_ckv, f_cq, f_wo, f_co, f_in, f_out), arrived, sent = refs[sources + 7], refs[sources + 8 : -2], refs[-2], refs[-1]
    side = tile_rows * 2 // 3
    half = side // 2
    at = 0
    for source in ins:
        blocks = source.shape[0]

        def fetch(k, _, source=source, at=at):
            for slot in range(own_tiles):
                pltpu.make_async_copy(
                    source.at[k, pl.ds(slot * tile_rows, tile_rows)],
                    staging.at[target[at + k * own_tiles + slot]],
                    arrived,
                ).start()
            return 0

        lax.fori_loop(0, blocks, fetch, 0)
        at += blocks * own_tiles
    pltpu.make_async_copy(staging, staging, arrived).wait()

    def parts(rank, ident):
        packed = staging.at[rank * 64 + ident]
        low = packed[side:]
        return packed[:side], jnp.concatenate([low[:, : side - LANES], low[:, side - LANES :]], axis=0)

    def columns(out, base, offset):
        for rank in range(4):
            for i in range(4):
                main, rest = parts(rank, base + i)
                rest = jnp.concatenate([rest, jnp.zeros((side, SLOT - side), jnp.bfloat16)], axis=1)
                out[i * side : (i + 1) * side, offset + rank * SLOT : offset + (rank + 1) * SLOT] = jnp.concatenate([main, rest], axis=1)

    def joined(rank, base):
        pieces = []
        for i in range(4):
            pieces.extend(parts(rank, base + i))
        return jnp.concatenate(pieces, axis=1)

    def padded_rows(out, base):
        for rank in range(4):
            out[rank * SLOT : rank * SLOT + side, :] = joined(rank, base)
            out[rank * SLOT + side : (rank + 1) * SLOT, :] = jnp.zeros((SLOT - side, 4 * side), jnp.bfloat16)

    copies = []

    def send(i, held):
        copy = pltpu.make_async_copy(held, outs[i], sent.at[i])
        copy.start()
        copies.append(copy)

    for m, base in enumerate((0, 4, 8)):
        columns(f_qkv, base, m * 4 * SLOT)
    send(0, f_qkv)
    for m, base in enumerate((16, 20)):
        columns(f_ckv, base, m * 4 * SLOT)
    send(1, f_ckv)
    columns(f_cq, 12, 0)
    send(2, f_cq)
    padded_rows(f_wo, 24)
    send(3, f_wo)
    padded_rows(f_co, 28)
    send(4, f_co)
    for rank in range(4):
        for i in range(4):
            f_in[i * side : (i + 1) * side, rank * 4 * side : (rank + 1) * 4 * side] = joined(rank, 32 + 4 * i)
    send(5, f_in)
    for rank in range(4):
        for i in range(4):
            f_out[(rank * 4 + i) * side : (rank * 4 + i + 1) * side, :] = joined(rank, 48 + 4 * i)
    send(6, f_out)
    for copy in copies:
        copy.wait()


def assemble(target, arrays, own_tiles, side):
    width = 4 * side
    tile_rows = side + side // 2
    bf = jnp.bfloat16
    shapes = [
        (width, 12 * SLOT), (width, 8 * SLOT), (width, 4 * SLOT), (4 * SLOT, width), (4 * SLOT, width),
        (width, 4 * width), (4 * width, width),
    ]
    anywhere = pl.BlockSpec(memory_space=pl.ANY)
    return pl.pallas_call(
        functools.partial(assemble_kernel, sources=len(arrays), own_tiles=own_tiles, tile_rows=tile_rows),
        grid_spec=pltpu.PrefetchScalarGridSpec(
            num_scalar_prefetch=1,
            grid=(1,),
            in_specs=[anywhere] * len(arrays),
            out_specs=[anywhere] * 7,
            scratch_shapes=[pltpu.VMEM((256, tile_rows, LANES), bf)]
            + [pltpu.VMEM(shape, bf) for shape in shapes]
            + [pltpu.SemaphoreType.DMA, pltpu.SemaphoreType.DMA((7,))],
        ),
        out_shape=[jax.ShapeDtypeStruct(shape, bf) for shape in shapes],
        compiler_params=pltpu.CompilerParams(vmem_limit_bytes=56 * 2**20),
        name="assemble",
    )(target, *arrays)


def weight_grads_kernel(
    rank, slot, sub, n1, dqkv, n2, dcq, frames, dk, dv, attended, b1, mixed, b2, n3, grad_up, active, b3, lines, out, *, side
):
    half = side // 2
    tile_rows = side + half

    def keep(tile, ident):
        tile = tile.astype(jnp.bfloat16)
        at = pl.multiple_of(sub[ident] * tile_rows, 32)
        out[slot[ident], pl.ds(at, side)] = tile[:, :LANES]
        rest = tile[:, LANES:]
        out[slot[ident], pl.ds(at + side, half)] = jnp.concatenate([rest[:half], rest[half:]], axis=1)

    def slots(made, bases):
        for m, base in enumerate(bases):
            for i in range(4):
                keep(made[i * side : (i + 1) * side, m * SLOT : m * SLOT + side], base + i)

    def grid_of(made, base, rows):
        for i in range(rows):
            for j in range(4):
                keep(made[i * side : (i + 1) * side, j * side : (j + 1) * side], base + i * 4 + j)

    slots(bdot(n1[...], dqkv[...], TN), (0, 4, 8))
    slots(bdot(n2[...], dcq[...], TN), (12,))
    slots(bdot(frames[0], dk[0], TN) + bdot(frames[1], dk[1], TN), (16,))
    slots(bdot(frames[0], dv[0], TN) + bdot(frames[1], dv[1], TN), (20,))
    grid_of(bdot(attended[...], b1[...], TN), 24, 1)
    grid_of(bdot(mixed[...], b2[...], TN), 28, 1)
    grid_of(bdot(n3[...], grad_up[...], TN), 32, 4)
    grid_of(bdot(active[...], b3[...], TN), 48, 4)
    for i in range(out.shape[0]):
        out[i, out.shape[1] - lines.shape[1] :] = lines[i].astype(jnp.bfloat16)


def weight_grads(rank, slot, sub, side, groups, own_tiles, lines, n1, dqkv, n2, dcq, frames, dk, dv, attended, b1, mixed, b2, n3, grad_up, active, b3):
    def whole(x):
        return pl.BlockSpec(x.shape, lambda i, rank, slot, sub: (0,) * x.ndim)

    def own(x, width):
        return pl.BlockSpec((x.shape[0], width), lambda i, rank, slot, sub: (0, rank[0]))

    def fitted(x):
        return own(x, 4 * side) if x.shape[1] > 4 * side else whole(x)

    shape = (groups, own_tiles * (side + side // 2) + lines.shape[1], LANES)
    return pl.pallas_call(
        functools.partial(weight_grads_kernel, side=side),
        grid_spec=pltpu.PrefetchScalarGridSpec(
            num_scalar_prefetch=3,
            grid=(1,),
            in_specs=[
                whole(n1), whole(dqkv), whole(n2), own(dcq, SLOT), whole(frames), whole(dk), whole(dv),
                own(attended, SLOT), whole(b1), own(mixed, SLOT), whole(b2), whole(n3),
                fitted(grad_up), fitted(active), whole(b3), whole(lines),
            ],
            out_specs=pl.BlockSpec(shape, lambda i, rank, slot, sub: (0, 0, 0)),
        ),
        out_shape=jax.ShapeDtypeStruct(shape, jnp.bfloat16),
        compiler_params=pltpu.CompilerParams(vmem_limit_bytes=60 * 2**20),
        name="weight_grads",
    )(rank, slot, sub, n1, dqkv, n2, dcq, frames, dk, dv, attended, b1, mixed, b2, n3, grad_up, active, b3, lines)


def scatter_blocks(blocks, ranks, groups):
    f32, bf16 = jnp.float32, jnp.bfloat16
    if groups != 8:
        return lax.psum_scatter(blocks, "dp", scatter_dimension=0, tiled=True)[0].astype(f32)

    def sent(values, bits):
        return lax.ppermute(values.astype(bf16), "dp", [(i, i ^ bits) for i in range(groups)]).astype(f32)

    half = groups // 2
    cut = blocks.shape[1] // 32 * 16
    chip = (blocks[:half].astype(f32) + sent(blocks[half:], 1)).astype(bf16)
    low, high = chip[:, :cut], chip[:, cut:]
    low_x, high_y = sent(jnp.stack([low[1], low[3]]), 2), sent(high[2:], 4)
    low = jnp.stack([low[0], low[2]]).astype(f32) + low_x
    high = high[:2].astype(f32) + high_y
    low_y, high_x = sent(low[1], 4), sent(high[1], 2)
    return jnp.concatenate([low[0] + low_y, high[0] + high_x], axis=0)


def first_back_kernel(rank, dqkv, query_weight, key_weight, value_weight, hidden, out, sums):
    weights = jnp.concatenate([query_weight[...], key_weight[...], value_weight[...]], axis=1)
    made = bdot(dqkv[...], weights, NT)
    unit, _ = unit_rows(hidden[...])
    sums[0:1] = jnp.sum(made * unit, axis=0, keepdims=True)
    sums[1:2] = jnp.sum(made, axis=0, keepdims=True)
    out[...] = made.astype(jnp.bfloat16)


def first_back(rank, dqkv, weight, hidden, ranks):
    tokens, width = hidden.shape
    own = lambda offset: pl.BlockSpec((width, SLOT), lambda i, rank: (0, offset + rank[0]))
    whole = lambda shape: pl.BlockSpec(shape, lambda i, rank: (0, 0))
    return pl.pallas_call(
        first_back_kernel,
        grid_spec=pltpu.PrefetchScalarGridSpec(
            num_scalar_prefetch=1,
            grid=(1,),
            in_specs=[whole(dqkv.shape), own(0), own(ranks), own(2 * ranks), whole(hidden.shape)],
            out_specs=[whole((tokens, width)), whole((2, width))],
        ),
        out_shape=[jax.ShapeDtypeStruct((tokens, width), jnp.bfloat16), jax.ShapeDtypeStruct((2, width), jnp.float32)],
        compiler_params=pltpu.CompilerParams(vmem_limit_bytes=VM),
        name="first_back",
    )(rank, dqkv, weight, weight, weight, hidden)


def frames_kernel(frames, weight, bias, out):
    out[0] = (bdot(frames[0], weight[...], NN) + bias[...]).astype(jnp.bfloat16)


def frame_projection(frames, weight, bias):
    seqs, count, width = frames.shape
    total = weight.shape[1]
    return pl.pallas_call(
        frames_kernel,
        grid=(seqs, total // 512),
        in_specs=[
            pl.BlockSpec((1, count, width), lambda b, c: (b, 0, 0)),
            pl.BlockSpec((width, 512), lambda b, c: (0, c)),
            pl.BlockSpec((1, 512), lambda b, c: (0, c)),
        ],
        out_specs=pl.BlockSpec((1, count, 512), lambda b, c: (b, 0, c)),
        out_shape=jax.ShapeDtypeStruct((seqs, count, total), jnp.bfloat16),
        compiler_params=pltpu.CompilerParams(vmem_limit_bytes=VM),
        name="frame_projection",
    )(frames, weight, bias[None])


def frames_back_kernel(rank, dk, dv, key_weight, value_weight, out, *, parts):
    made = bdot(dk[0], key_weight[...], NT) + bdot(dv[0], value_weight[...], NT)
    share = made.shape[0] // parts
    for part in range(parts):
        piece = made[part * share : (part + 1) * share]
        out[part, 0] = jnp.concatenate([piece, jnp.zeros((out.shape[2] - share, piece.shape[1]), jnp.float32)], axis=0).astype(jnp.bfloat16)


def frames_back(rank, dk, dv, weight, parts):
    seqs, count, slot = dk.shape
    width = weight.shape[0]
    padded = -(-(count // parts) // 16) * 16
    own = pl.BlockSpec((1, count, slot), lambda b, rank: (b, 0, 0))
    return pl.pallas_call(
        functools.partial(frames_back_kernel, parts=parts),
        grid_spec=pltpu.PrefetchScalarGridSpec(
            num_scalar_prefetch=1,
            grid=(seqs,),
            in_specs=[
                own, own,
                pl.BlockSpec((width, slot), lambda b, rank: (0, rank[0])),
                pl.BlockSpec((width, slot), lambda b, rank: (0, parts + rank[0])),
            ],
            out_specs=pl.BlockSpec((parts, 1, padded, width), lambda b, rank: (0, b, 0, 0)),
        ),
        out_shape=jax.ShapeDtypeStruct((parts, seqs, padded, width), jnp.bfloat16),
        compiler_params=pltpu.CompilerParams(vmem_limit_bytes=VM),
        name="frames_back",
    )(rank, dk, dv, weight, weight)


def product(left_part, right_part):
    return jnp.dot(left_part, right_part, preferred_element_type=jnp.float32)


def times_transpose(left_part, right_part):
    return lax.dot_general(left_part, right_part, (NT, ((), ())), preferred_element_type=jnp.float32)


def unit_rows(values):
    centre = jnp.mean(values, axis=-1, keepdims=True)
    centred = values - centre
    inverse = lax.rsqrt(jnp.mean(centred * centred, axis=-1, keepdims=True) + norm_eps)
    return centred * inverse, inverse


def normalize(values, gain, shift):
    return unit_rows(values)[0] * gain + shift


def normalize_back(values, gain, grads):
    unit, inverse = unit_rows(values)
    scaled = grads * gain
    result = inverse * (
        scaled
        - jnp.mean(scaled, axis=-1, keepdims=True)
        - unit * jnp.mean(scaled * unit, axis=-1, keepdims=True)
    )
    return result, jnp.sum(grads * unit, axis=0), jnp.sum(grads, axis=0)


def gelu_pair(value):
    size = jnp.abs(value) * 0.7071067811865476
    bell = jnp.exp(-size * size)
    t = 1.0 / (1.0 + 0.3275911 * size)
    poly = t * (0.254829592 + t * (-0.284496736 + t * (1.421413741 + t * (-1.453152027 + t * 1.061405429))))
    tail = 0.5 * poly * bell
    level = jnp.where(value >= 0, 1.0 - tail, tail)
    return value * level, level + value * bell * 0.3989422804014327


def middle_kernel(
    rank, mixed, first_sum, top_grad, c_o, w_in, w_out, vectors, inner_bias,
    block_out, grad_out, grad_mixed, n3_out, b2_out, b3_out, active_out, up_out, sums, up_sums, acts, slopes, ups,
):
    f32, bf16 = jnp.float32, jnp.bfloat16
    width = first_sum.shape[1]
    parts = acts.shape[0]
    row = lambda i: vectors[i : i + 1]
    cut = lambda i: slice(i * width, (i + 1) * width)
    fold = lambda values: jnp.sum(values, axis=0, keepdims=True)

    def back(unit, inverse, scaled):
        centre = jnp.mean(scaled, axis=-1, keepdims=True)
        return inverse * (scaled - centre - unit * jnp.mean(scaled * unit, axis=-1, keepdims=True))

    second_sum = first_sum[...] + bdot(mixed[...], c_o[...], NN) + row(9)
    unit, inverse = unit_rows(second_sum)
    n3 = (unit * row(4) + row(5)).astype(bf16)
    n3_out[...] = n3
    third_sum = second_sum + row(10)
    for i in range(parts):
        value, slope = gelu_pair(bdot(n3, w_in[:, cut(i)], NN) + inner_bias[:, cut(i)])
        acts[i] = value.astype(bf16)
        slopes[i] = slope.astype(bf16)
        third_sum = third_sum + bdot(acts[i], w_out[cut(i)], NN)
    active_out[...] = acts[rank[0]]
    last, last_inverse = unit_rows(third_sum)
    block_out[...] = last * row(6) + row(7)
    grads = top_grad[...].astype(f32)
    grad_third = back(last, last_inverse, grads * row(6))
    b3 = grad_third.astype(bf16)
    b3_out[...] = b3
    grad_normed, ups_now = None, []
    for i in range(parts):
        grad_up = (bdot(b3, w_out[cut(i)], NT) * slopes[i].astype(f32)).astype(bf16)
        ups[i] = grad_up
        ups_now.append(fold(grad_up.astype(f32)))
        term = bdot(grad_up, w_in[:, cut(i)], NT)
        grad_normed = term if grad_normed is None else grad_normed + term
    up_out[...] = ups[rank[0]]
    grad_second = grad_third + back(unit, inverse, grad_normed * row(4))
    grad_out[...] = grad_second
    b2 = grad_second.astype(bf16)
    b2_out[...] = b2
    grad_mixed[...] = bdot(b2, c_o[...], NT).astype(bf16)
    now = jnp.concatenate(
        [
            fold(grad_normed * unit), fold(grad_normed), fold(grads * last), fold(grads),
            fold(b2.astype(f32)), fold(b3.astype(f32)), jnp.zeros((2, width), f32),
        ],
        axis=0,
    )
    ups_all = jnp.concatenate(ups_now, axis=0)
    start = pl.program_id(0) == 0

    @pl.when(start)
    def _():
        sums[...] = now
        up_sums[...] = ups_all

    @pl.when(jnp.logical_not(start))
    def _():
        sums[...] += now
        up_sums[...] += ups_all


def middle(rank, mixed, first_sum, top_grad, c_o, w_in, w_out, vectors, inner_bias, block=224):
    f32, bf16 = jnp.float32, jnp.bfloat16
    tokens, width = first_sum.shape
    slots, hidden = mixed.shape[1], w_in.shape[1]
    parts = hidden // width
    rows = lambda size: pl.BlockSpec((block, size), lambda i, rank: (i, 0))
    once = lambda x: pl.BlockSpec(x.shape, lambda i, rank: (0, 0), pipeline_mode=pl.Buffered(1))
    total = lambda count: pl.BlockSpec((count, width), lambda i, rank: (0, 0))
    out = lambda size, kind: jax.ShapeDtypeStruct((tokens, size), kind)
    return pl.pallas_call(
        middle_kernel,
        grid_spec=pltpu.PrefetchScalarGridSpec(
            num_scalar_prefetch=1,
            grid=(tokens // block,),
            in_specs=[
                rows(slots), rows(width), rows(width), once(c_o), once(w_in), once(w_out), once(vectors), once(inner_bias),
            ],
            out_specs=[rows(width), rows(width), rows(slots)] + [rows(width)] * 5 + [total(8), total(parts)],
            scratch_shapes=[pltpu.VMEM((parts, block, width), bf16)] * 3,
        ),
        out_shape=[out(width, f32), out(width, f32), out(slots, bf16)]
        + [out(width, bf16)] * 5
        + [jax.ShapeDtypeStruct((8, width), f32), jax.ShapeDtypeStruct((parts, width), f32)],
        compiler_params=pltpu.CompilerParams(vmem_limit_bytes=VM),
        name="middle",
    )(rank, mixed, first_sum, top_grad, c_o, w_in, w_out, vectors, inner_bias)


def spread_heads(rows, ranks):
    lead = rows.shape[0]
    side = rows.shape[1] // ranks
    return jnp.pad(rows.reshape(lead, ranks, side), ((0, 0), (0, 0), (0, SLOT - side))).reshape(lead, ranks * SLOT)


def shards(
    hidden_in, frames, cotangent, segments, stamps, owner_list, master_tiles, tile_first, tile_second,
    tile_stats, tile_bases, master_vectors, vector_first, vector_second,
):
    f32, bf16 = jnp.float32, jnp.bfloat16
    ranks, groups = lax.axis_size("tensor"), lax.axis_size("dp")
    rank, group = lax.axis_index("tensor"), lax.axis_index("dp")
    seqs, local_rows, width = hidden_in.shape
    rows = local_rows * ranks
    tokens = seqs * rows
    own_tiles, side = master_tiles.shape[1], master_tiles.shape[-1]
    heads = side // HEAD
    rank_ref = rank.astype(jnp.int32)[None]

    length = master_vectors.shape[0]
    line_rows = -(-length // (16 * LANES)) * 16
    line = jnp.pad(master_vectors, (0, line_rows * LANES - length)).reshape(line_rows, LANES)
    block = pack(master_tiles[0], line)
    ready = soap_pre(tile_first[0], tile_stats[0], tile_bases[0])
    frames = with_layout_constraint(frames, Layout(major_to_minor=(0, 1, 2)))
    arrays, where, last, (ready, frames) = gather_blocks(block, ranks, groups, (ready, frames))
    if where is None:
        source_rank = jnp.tile(jnp.arange(ranks, dtype=jnp.int32), groups)
        source_group = jnp.repeat(jnp.arange(groups, dtype=jnp.int32), ranks)
        lines = arrays[0].reshape(groups, ranks, -1, LANES)[:, 0, -line_rows:].reshape(groups, -1)[:, :length]
    else:
        steps = jnp.array([step for array in where for step, _ in array], jnp.int32)
        bits = jnp.array([bit for array in where for _, bit in array], jnp.int32)
        source_rank = (rank - steps) % ranks
        source_group = group ^ bits
        lines = jnp.concatenate([array[:, -line_rows:] for array in arrays[:2]], axis=0).reshape(groups, -1)[:, :length]
        spots = source_group[:groups]
        order = jnp.arange(groups, dtype=jnp.int32)
        lines = jnp.sum(jnp.where((spots[None] == order[:, None])[:, :, None], lines[None].astype(f32), 0.0), axis=1)
    vectors = lines.astype(f32).reshape(19, width)

    count = owner_list.shape[0]
    position = jnp.arange(count, dtype=jnp.int32)
    place = jnp.sum(jnp.where(owner_list[None, :] == position[:, None], position[None, :], 0), axis=1)
    spot = (source_group[:, None] * own_tiles + jnp.arange(own_tiles, dtype=jnp.int32)[None]).reshape(-1)
    ident = jnp.sum(jnp.where(spot[:, None] == position[None, :], owner_list[None, :], 0), axis=1)
    target = jnp.repeat(source_rank, own_tiles) * count + ident
    w_qkv, c_kv, c_q, w_o, c_o, w_in, w_out = assemble(target, arrays, own_tiles, side)

    rows_in = jnp.stack([hidden_in, cotangent])
    if where is not None:
        rows_in, _ = lax.optimization_barrier((rows_in, last))
    both = lax.all_gather(rows_in, "tensor", axis=2, tiled=True)
    hidden = both[0].reshape(tokens, width).astype(f32)

    head_bias = spread_heads(vectors[11:15], ranks)
    none = jnp.zeros_like(head_bias[0])
    inner_bias = vectors[15:19].reshape(-1)
    seg_col, seg_row = segments[:, :, None], segments[:, None, :]
    stamp_col, stamp_row = stamps[:, :, None], stamps[:, None, :]

    def split(values):
        return values.reshape(seqs, rows, values.shape[-1])

    def flat(values):
        return values.reshape(tokens, values.shape[-1])

    def own_rows(values):
        return lax.dynamic_slice_in_dim(split(values), rank * local_rows, local_rows, axis=1)

    keys_values = frame_projection(frames, c_kv, jnp.concatenate([none, head_bias[3]]))
    n1 = normalize(hidden, vectors[0], vectors[1]).astype(bf16)
    qkv = split((product(n1, w_qkv) + jnp.concatenate([head_bias[0], none, head_bias[1]])).astype(bf16))
    attended, self_logs = self_forward(qkv, seg_col, seg_row, stamp_row, ranks, heads)
    attended = flat(attended)
    first_sum = hidden + product(attended, w_o) + vectors[8]
    n2 = normalize(first_sum, vectors[2], vectors[3]).astype(bf16)
    cross_queries = split((product(n2, c_q) + head_bias[2]).astype(bf16))
    mixed, cross_logs = cross_forward(cross_queries, keys_values, ranks, heads)
    mixed = flat(mixed)
    top_grad = both[1].reshape(tokens, width)
    out_rows, grad_second, grad_mixed, n3, b2, b3, active, grad_up, sums, up_sum = middle(
        rank_ref, mixed, first_sum, top_grad, c_o, w_in, w_out, vectors, inner_bias[None]
    )
    block_out = own_rows(out_rows)
    grad_mixed = split(grad_mixed)
    dcq, dk, dv = cross_backward(
        rank_ref, cross_queries, keys_values, grad_mixed, split(mixed), cross_logs, ranks, heads
    )
    dcq = flat(dcq)
    frames_part = frames_back(rank_ref, dk, dv, c_kv, ranks)
    dcq, frames_part = lax.optimization_barrier((dcq, frames_part))
    frames_sum = lax.psum_scatter(
        frames_part.reshape(ranks * seqs, frames_part.shape[2], width), "tensor", scatter_dimension=0, tiled=True
    )
    frames_grad = frames_sum[:, : frames.shape[1] // ranks].astype(f32)
    back, gain_two, shift_two = normalize_back(first_sum, vectors[2], times_transpose(dcq, c_q))
    grad_first = grad_second + back
    b1 = grad_first.astype(bf16)
    grad_attended = split(times_transpose(b1, w_o).astype(bf16))
    dqkv = flat(
        self_backward(
            rank_ref, qkv, grad_attended, split(attended), self_logs, seg_col, seg_row, stamp_col, ranks, heads
        )
    )

    part_one, first_sums = first_back(rank_ref, dqkv, w_qkv, hidden, ranks)
    grad_one = lax.psum_scatter(split(part_one), "tensor", scatter_dimension=1, tiled=True).astype(f32)
    back, _, _ = normalize_back(
        hidden_in.astype(f32).reshape(-1, width), vectors[0], grad_one.reshape(-1, width)
    )
    input_grad = own_rows(grad_first) + back.reshape(hidden_in.shape)

    def total(values):
        return jnp.sum(values.astype(f32), axis=tuple(range(values.ndim - 1)))

    same = jnp.stack(
        [gain_two, shift_two, sums[0], sums[1], sums[2], sums[3], total(b1), sums[4], sums[5]]
    )
    query_sum = total(dcq).reshape(ranks, SLOT)[:, :side].reshape(1, width)
    even = 1.0 / ranks
    dqkv_sum = total(dqkv)
    own_sums = jnp.stack([dqkv_sum[:side], dqkv_sum[2 * SLOT : 2 * SLOT + side], total(dv)[:side]])
    own_sums = lax.dynamic_update_slice(jnp.zeros((3, width), f32), own_sums, (0, rank * side))
    vector_terms = jnp.concatenate(
        [first_sums, same * even, own_sums[:2], query_sum * even, own_sums[2:], up_sum * even]
    )
    lines = vector_terms.reshape(groups, length)
    owner = place // own_tiles
    if groups == 8:
        bits = owner ^ group
        slot = (bits & 1) * (groups // 2) + (bits >> 1)
        at = jnp.arange(groups, dtype=jnp.int32)
        wanted = group ^ (2 * (at % (groups // 2)) + at // (groups // 2))
        lines = jnp.sum(jnp.where((wanted[:, None] == at[None])[:, :, None], lines[None], 0.0), axis=1)
    else:
        slot = owner
    lines = jnp.pad(lines, ((0, 0), (0, line_rows * LANES - length))).reshape(groups, line_rows, LANES)
    blocks = weight_grads(
        rank_ref, slot, place % own_tiles, side, groups, own_tiles, lines,
        n1, dqkv, n2, dcq, frames, dk, dv, attended, b1, mixed, b2, n3, grad_up, active, b3,
    )
    owned = scatter_blocks(blocks, ranks, groups)
    line = owned[-line_rows:]
    turns = [[(i, (i + step) % ranks) for i in range(ranks)] for step in range(1, ranks)]
    vector_grad = (line + sum(lax.ppermute(line, "tensor", turn) for turn in turns)).reshape(-1)[:length]

    new_first, new_second, new_master, new_stats, new_bases = soap(
        owned, master_tiles[0], tile_first[0], tile_second[0], tile_stats[0], tile_bases[0], *ready
    )
    new_vector_first = beta_one * vector_first + (1.0 - beta_one) * vector_grad
    new_vector_second = beta_two * vector_second + (1.0 - beta_two) * vector_grad * vector_grad
    new_vectors = master_vectors - rate_vectors * (new_vector_first / (1.0 - beta_one**STEP)) / (
        jnp.sqrt(new_vector_second / (1.0 - beta_two**STEP)) + adam_eps
    )
    return (
        block_out, input_grad, frames_grad, new_master[None], new_first[None], new_second[None],
        new_stats[None], new_bases[None], new_vectors, new_vector_first, new_vector_second,
    )


def solution(mesh):
    rows, seqs, tiles, pairs = (
        P("dp", "tensor", None), P("dp", None), P("tensor", "dp", None, None), P("tensor", "dp", None, None, None)
    )
    line = P("dp")
    in_specs = (
        rows, P("dp", None, None), rows, seqs, seqs, P(), tiles, tiles, tiles, pairs, pairs, line, line, line
    )
    out_specs = (rows, rows, rows, tiles, tiles, tiles, pairs, pairs, line, line, line)
    return jax.shard_map(shards, mesh=mesh, in_specs=in_specs, out_specs=out_specs, check_vma=False)
```

```python
import functools

import jax
import jax.numpy as jnp
from jax import lax
from jax.experimental import pallas as pl
from jax.experimental.pallas import tpu as pltpu
from jax.experimental.layout import Layout, with_layout_constraint
from jax.sharding import PartitionSpec as P

HEAD = 64
FF = 3072
STEP = 5
LANES = 128
SLOT = 256
VM = 56 * 2**20
HI = lax.Precision.HIGHEST

norm_eps = 1e-05
beta_one = 0.9
beta_two = 0.95
adam_eps = 1e-08
rate_tiles = 0.05
rate_vectors = 0.3
score_scale = 0.125


def split2(a):
    hi = a.astype(jnp.bfloat16)
    lo = (a - hi.astype(jnp.float32)).astype(jnp.bfloat16)
    return hi, lo

def bdot(a, b, dims):
    return lax.dot_general(a, b, (dims, ((), ())), preferred_element_type=jnp.float32)

NN = ((1,), (0,)); TN = ((0,), (0,)); NT = ((1,), (1,))

def dot3(a, b, dims):
    (ah, al), (bh, bl) = a, b
    return bdot(ah, bh, dims) + (bdot(ah, bl, dims) + bdot(al, bh, dims))

def dothi(a, b, dims):
    return lax.dot_general(a, b, (dims, ((), ())), precision=HI, preferred_element_type=jnp.float32)

def soap_pre_kernel(first, stats, bases, rot_first, stats_rot):
    ql, qr = split2(bases[0, 0]), split2(bases[0, 1])
    inner = split2(dot3(ql, split2(first[0]), TN))
    rot_first[0] = dot3(inner, qr, NN)
    stats_rot[0, 0] = dot3(split2(stats[0, 0]), ql, NN)
    stats_rot[0, 1] = dot3(split2(stats[0, 1]), qr, NN)

def soap_main_kernel(grad, master, first, second, stats, bases, rot_first, stats_rot,
                     new_master, new_first, new_second, new_stats, turned, grams):
    side = master.shape[1]
    rest = grad[side:]
    rest = jnp.concatenate([rest[:, : side - LANES], rest[:, side - LANES :]], axis=0)
    g32 = jnp.concatenate([grad[:side], rest], axis=1)
    g, ql, qr = split2(g32), split2(bases[0, 0]), split2(bases[0, 1])
    new_first[0] = beta_one * first[0] + (1.0 - beta_one) * g32
    part_left = split2(dot3(ql, g, TN))
    rotated = dot3(part_left, qr, NN)
    fresh = beta_two * second[0] + (1.0 - beta_two) * rotated * rotated
    new_second[0] = fresh
    moment = (beta_one * rot_first[0] + (1.0 - beta_one) * rotated) / (1.0 - beta_one**STEP)
    step = moment / (jnp.sqrt(fresh / (1.0 - beta_two**STEP)) + adam_eps)
    back = split2(dot3(ql, split2(step), NN))
    new_master[0] = master[0] - rate_tiles * dot3(back, qr, NT)
    new_stats[0, 0] = beta_two * stats[0, 0] + (1.0 - beta_two) * dot3(g, g, NT)
    new_stats[0, 1] = beta_two * stats[0, 1] + (1.0 - beta_two) * dot3(g, g, TN)
    part_right = split2(dot3(g, qr, NN))
    for side, term in ((0, dot3(g, part_left, NT)), (1, dot3(g, part_right, TN))):
        side_turned = beta_two * stats_rot[0, side] + (1.0 - beta_two) * term
        turned[0, side] = side_turned
        halves = split2(side_turned)
        grams[0, side] = dot3(halves, halves, TN)

def chol_kernel(turned, grams, out, work, fac, *, block, unroll, passes):
    count, side = work.shape[0], work.shape[1]
    wide = work.shape[2] // 2
    for m in range(count):
        work[m, :, :side] = grams[m]
        work[m, :, side:wide] = jnp.zeros((side, wide - side), jnp.float32)
        work[m, :, wide : wide + side] = turned[m].T
        work[m, :, wide + side :] = jnp.zeros((side, wide - side), jnp.float32)
    brow = lax.broadcasted_iota(jnp.int32, (count, block, 2 * block), 1)
    bcol = lax.broadcasted_iota(jnp.int32, (count, block, 2 * block), 2)
    aug_eye = ((bcol - block) == brow).astype(jnp.float32)
    for k in range(side // block):
        lo, hi = k * block, (k + 1) * block
        diag = work[:, lo:hi, lo:hi]
        w = jnp.concatenate([diag, jnp.zeros_like(diag)], axis=2) + aug_eye
        for j in range(block - 1):
            piv = w[:, j : j + 1, :]
            ratio = w[:, :, j : j + 1] / w[:, j : j + 1, j : j + 1]
            w = w - jnp.where(brow > j, ratio * piv, 0.0)
        d = jnp.sum(jnp.where(brow == bcol, w, 0.0), axis=2, keepdims=True)
        fac[...] = w[:, :, block:] * lax.rsqrt(d)

        def several(i, _):
            for u in range(unroll):
                m = i * unroll + u
                if passes == 6:
                    y = dothi(fac[m], work[m, lo:hi, :], NN)
                else:
                    y = dot3(split2(fac[m]), split2(work[m, lo:hi, :]), NN)
                work[m, lo:hi, :] = y
                if hi < side:
                    turn = y[:, :side].T[hi:]
                    if passes == 6:
                        step = dothi(turn, y, NN)
                    else:
                        step = dot3(split2(turn), split2(y), NN)
                    work[m, hi:, :] = work[m, hi:, :] - step
            return 0
        lax.fori_loop(0, count // unroll, several, 0)
    for m in range(count):
        out[m] = work[m, :, wide : wide + side].T

def tile_spec(side):
    return pl.BlockSpec((1, side, side), lambda i: (i, 0, 0))
def pair_spec(side):
    return pl.BlockSpec((1, 2, side, side), lambda i: (i, 0, 0, 0))

def soap_pre(first, stats, bases):
    n, side = first.shape[0], first.shape[1]
    t, p = tile_spec(side), pair_spec(side)
    return pl.pallas_call(soap_pre_kernel, grid=(n,), in_specs=[t, p, p], out_specs=[t, p],
        out_shape=[jax.ShapeDtypeStruct(first.shape, jnp.float32), jax.ShapeDtypeStruct(stats.shape, jnp.float32)],
        name="soap_pre")(first, stats, bases)

def soap_main(grad, master, first, second, stats, bases, rot_first, stats_rot):
    n, side = first.shape[0], first.shape[1]
    t, p = tile_spec(side), pair_spec(side)
    f = jnp.float32
    ts, ps = jax.ShapeDtypeStruct(first.shape, f), jax.ShapeDtypeStruct(stats.shape, f)
    return pl.pallas_call(soap_main_kernel, grid=(n,), in_specs=[pl.BlockSpec((side + side // 2, LANES), lambda i: (i, 0)), t, t, t, p, p, t, p],
        out_specs=[t, t, t, p, p, p], out_shape=[ts, ts, ts, ps, ps, ps], name="soap_main")(
        grad, master, first, second, stats, bases, rot_first, stats_rot)

def chol_bases(turned, grams, block=64, unroll=4, passes=3):
    n, _, side, _ = turned.shape
    shape = (2 * n, side, side)
    unroll = min(unroll, 2 * n)
    out = pl.pallas_call(functools.partial(chol_kernel, block=block, unroll=unroll, passes=passes),
        out_shape=jax.ShapeDtypeStruct(shape, jnp.float32),
        scratch_shapes=[pltpu.VMEM((2 * n, side, 512), jnp.float32), pltpu.VMEM((2*n, block, block), jnp.float32)],
        compiler_params=pltpu.CompilerParams(vmem_limit_bytes=48 * 2**20), name="chol_bases")(
        turned.reshape(shape), grams.reshape(shape))
    return out.reshape(turned.shape)


def soap(gradient, master, first, second, statistics, bases, rot_first, stats_rot):
    nm, nf, ns, nst, turned, grams = soap_main(gradient, master, first, second, statistics, bases, rot_first, stats_rot)
    return nf, ns, nm, nst, chol_bases(turned, grams)


def head_pick(shape, head):
    lane = lax.broadcasted_iota(jnp.int32, shape, len(shape) - 1)
    return (lane >= HEAD) if head % 2 else (lane < HEAD)


def forward_heads(query, key, value, allowed, heads, chunk):
    rows = query.shape[0]
    units = [(low, head) for low in range(0, rows, chunk) for head in range(heads)]
    spans = [slice(head // 2 * LANES, head // 2 * LANES + LANES) for head in range(heads)]
    own_values = []
    for head in range(heads):
        block = value[:, spans[head]]
        own_values.append(jnp.where(head_pick(block.shape, head), block, jnp.ones_like(block)))

    def scores_of(unit):
        low, head = unit
        block = query[low : low + chunk, spans[head]]
        own = jnp.where(head_pick(block.shape, head), block, jnp.zeros_like(block)) * jnp.bfloat16(score_scale)
        return bdot(own, key[:, spans[head]], NT)

    done, logs = {}, {}
    ahead = scores_of(units[0])
    for i, (low, head) in enumerate(units):
        scores = ahead
        if i + 1 < len(units):
            ahead = scores_of(units[i + 1])
        if allowed is not None:
            scores = jnp.where(allowed[low : low + chunk], scores, -1e30)
        top = jnp.max(scores, axis=1, keepdims=True)
        weights = jnp.exp(scores - top).astype(jnp.bfloat16)
        both = bdot(weights, own_values[head], NN)
        turned = pltpu.roll(both, HEAD, 1)
        pick = head_pick(both.shape, head)
        done[low, head] = both / turned
        logs[low, head] = top + jnp.log(jnp.where(pick, turned, both))
    columns, lines = [], []
    for low in range(0, rows, chunk):
        blocks = []
        lane = lax.broadcasted_iota(jnp.int32, (chunk, LANES), 1)
        line = jnp.zeros((chunk, LANES), jnp.float32)
        for first in range(0, heads, 2):
            other = done[low, first + 1] if first + 1 < heads else 0.0
            blocks.append(jnp.where(lane < HEAD, done[low, first], other).astype(jnp.bfloat16))
        for head in range(heads):
            line = jnp.where(lane == head, logs[low, head], line)
        columns.append(jnp.concatenate(blocks, axis=1))
        lines.append(line)
    return jnp.concatenate(columns, axis=0), jnp.concatenate(lines, axis=0).T[:8]


def cross_forward_kernel(query, key, value, out, logs, *, heads, chunk):
    out[0], logs[0, 0] = forward_heads(query[0], key[0, 0], value[0, 0], None, heads, chunk)


def self_forward_kernel(query, key, value, seg_col, seg_row, stamp_row, out, logs, *, heads, chunk):
    rows = query.shape[1]
    at = lax.broadcasted_iota(jnp.int32, (rows, rows), 0)
    key_at = lax.broadcasted_iota(jnp.int32, (rows, rows), 1)
    allowed = (key_at <= at) & (seg_col[0] == seg_row[0]) & ((stamp_row[0] == 0) | (key_at == at))
    out[0], logs[0, 0] = forward_heads(query[0], key[0], value[0], allowed, heads, chunk)


def backward_heads(query, key, value, grad, mixed, logs, allowed, heads, chunk, probs_ref, scores_ref):
    keys = key.shape[0]
    spans = [slice(head // 2 * LANES, head // 2 * LANES + LANES) for head in range(heads)]
    products = (grad.astype(jnp.float32) * mixed.astype(jnp.float32)).T
    own_query, own_grad, turned, dots, total = [], [], [], [], [None] * heads
    for head in range(heads):
        pick = head_pick((query.shape[0], LANES), head)
        zero = jnp.zeros((query.shape[0], LANES), jnp.bfloat16)
        own_query.append(jnp.where(pick, query[:, spans[head]], zero) * jnp.bfloat16(score_scale))
        own_grad.append(jnp.where(pick, grad[:, spans[head]], zero))
        dots.append(jnp.sum(products[head * HEAD : (head + 1) * HEAD], axis=0, keepdims=True))
        if head % 2 == 0:
            turned.append(key[:, spans[head]].T)
    units = [(low, head) for low in range(0, keys, chunk) for head in range(heads)]

    def products_of(unit):
        low, head = unit
        high = min(low + chunk, keys)
        return bdot(key[low:high, spans[head]], own_query[head], NT), bdot(value[low:high, spans[head]], own_grad[head], NT)

    ahead = products_of(units[0])
    for i, (low, head) in enumerate(units):
        high = min(low + chunk, keys)
        scores, grad_probs = ahead
        if i + 1 < len(units):
            ahead = products_of(units[i + 1])
        if allowed is not None:
            scores = jnp.where(allowed[low:high], scores, -1e30)
        probs = jnp.exp(scores - logs[head : head + 1])
        grad_scores = (probs * (grad_probs - dots[head])).astype(jnp.bfloat16)
        probs_ref[head, low:high] = probs.astype(jnp.bfloat16)
        scores_ref[head, low:high] = grad_scores
        half = head % 2 * HEAD
        term = bdot(turned[head // 2][half : half + HEAD, low:high], grad_scores, NN)
        total[head] = term if total[head] is None else total[head] + term
    if heads % 2:
        total.append(jnp.zeros_like(total[0]))
    return (jnp.concatenate(total, axis=0).T * score_scale).astype(jnp.bfloat16)


def key_value_grads(query, grad, heads, probs_ref, scores_ref):
    keys, values = [], []
    for first in range(0, heads, 2):
        span = slice(first * HEAD, first * HEAD + LANES)
        made_key = made_value = None
        for head in range(first, min(first + 2, heads)):
            grad_key = bdot(scores_ref[head], query[:, span], NN) * score_scale
            grad_value = bdot(probs_ref[head], grad[:, span], NN)
            pick = head_pick(grad_key.shape, head)
            made_key = jnp.where(pick, grad_key, 0.0 if made_key is None else made_key)
            made_value = jnp.where(pick, grad_value, 0.0 if made_value is None else made_value)
        keys.append(made_key.astype(jnp.bfloat16))
        values.append(made_value.astype(jnp.bfloat16))
    return jnp.concatenate(keys, axis=1), jnp.concatenate(values, axis=1)


def cross_backward_kernel(
    rank, query, key, value, grad, mixed, logs, grad_query, grad_key, grad_value, probs_ref, scores_ref, *, heads, chunk
):
    grad_query[0] = backward_heads(
        query[0], key[0, 0], value[0, 0], grad[0], mixed[0], logs[0, 0], None, heads, chunk, probs_ref, scores_ref
    )

    @pl.when(pl.program_id(1) == rank[0])
    def _():
        made = key_value_grads(query[0], grad[0], heads, probs_ref, scores_ref)
        grad_key[0], grad_value[0] = made


def self_backward_kernel(
    rank, query, key, value, grad, mixed, logs, seg_col, seg_row, stamp_col, out, probs_ref, scores_ref, *, heads, chunk
):
    rows = query.shape[1]
    key_at = lax.broadcasted_iota(jnp.int32, (rows, rows), 0)
    at = lax.broadcasted_iota(jnp.int32, (rows, rows), 1)
    allowed = (key_at <= at) & (seg_col[0] == seg_row[0]) & ((stamp_col[0] == 0) | (key_at == at))
    grad_query = backward_heads(
        query[0], key[0], value[0], grad[0], mixed[0], logs[0, 0], allowed, heads, chunk, probs_ref, scores_ref
    )
    grad_key, grad_value = key_value_grads(query[0], grad[0], heads, probs_ref, scores_ref)
    out[0] = jnp.concatenate([grad_query, grad_key, grad_value], axis=1)


def slot_spec(rows, offset):
    return pl.BlockSpec((1, rows, SLOT), lambda b, r: (b, 0, offset + r))


def major_spec(rows, offset):
    return pl.BlockSpec((1, 1, rows, SLOT), lambda b, r: (offset + r, b, 0, 0))


def self_forward(qkv, seg_col, seg_row, stamp_row, ranks, heads, chunk=448):
    seqs, rows, _ = qkv.shape
    col = pl.BlockSpec((1, rows, 1), lambda b, r: (b, 0, 0))
    row = pl.BlockSpec((1, 1, rows), lambda b, r: (b, 0, 0))
    return pl.pallas_call(
        functools.partial(self_forward_kernel, heads=heads, chunk=chunk),
        grid=(seqs, ranks),
        in_specs=[slot_spec(rows, 0), slot_spec(rows, ranks), slot_spec(rows, 2 * ranks), col, row, row],
        out_specs=[slot_spec(rows, 0), pl.BlockSpec((1, 1, 8, rows), lambda b, r: (b, r, 0, 0))],
        out_shape=[
            jax.ShapeDtypeStruct((seqs, rows, ranks * SLOT), jnp.bfloat16),
            jax.ShapeDtypeStruct((seqs, ranks, 8, rows), jnp.float32),
        ],
        compiler_params=pltpu.CompilerParams(vmem_limit_bytes=VM),
        name="self_forward",
    )(qkv, qkv, qkv, seg_col, seg_row, stamp_row)


def cross_forward(queries, keys_values, ranks, heads, chunk=448):
    seqs, rows, _ = queries.shape
    frames = keys_values.shape[2]
    return pl.pallas_call(
        functools.partial(cross_forward_kernel, heads=heads, chunk=chunk),
        grid=(seqs, ranks),
        in_specs=[slot_spec(rows, 0), major_spec(frames, 0), major_spec(frames, ranks)],
        out_specs=[slot_spec(rows, 0), pl.BlockSpec((1, 1, 8, rows), lambda b, r: (b, r, 0, 0))],
        out_shape=[
            jax.ShapeDtypeStruct((seqs, rows, ranks * SLOT), jnp.bfloat16),
            jax.ShapeDtypeStruct((seqs, ranks, 8, rows), jnp.float32),
        ],
        compiler_params=pltpu.CompilerParams(vmem_limit_bytes=VM),
        name="cross_forward",
    )(queries, keys_values, keys_values)


def ranked_spec(rows, offset):
    return pl.BlockSpec((1, rows, SLOT), lambda b, r, rank: (b, 0, offset + r))


def cross_backward(rank, queries, keys_values, grads, mixed, logs, ranks, heads, chunk=512):
    seqs, rows, _ = queries.shape
    frames = keys_values.shape[2]
    kept = pl.BlockSpec((1, frames, SLOT), lambda b, r, rank: (b, 0, 0))
    bf = jnp.bfloat16
    return pl.pallas_call(
        functools.partial(cross_backward_kernel, heads=heads, chunk=chunk),
        grid_spec=pltpu.PrefetchScalarGridSpec(
            num_scalar_prefetch=1,
            grid=(seqs, ranks),
            in_specs=[
                ranked_spec(rows, 0), pl.BlockSpec((1, 1, frames, SLOT), lambda b, r, rank: (r, b, 0, 0)),
                pl.BlockSpec((1, 1, frames, SLOT), lambda b, r, rank: (ranks + r, b, 0, 0)), ranked_spec(rows, 0), ranked_spec(rows, 0),
                pl.BlockSpec((1, 1, 8, rows), lambda b, r, rank: (b, r, 0, 0)),
            ],
            out_specs=[ranked_spec(rows, 0), kept, kept],
            scratch_shapes=[pltpu.VMEM((heads, frames, rows), bf), pltpu.VMEM((heads, frames, rows), bf)],
        ),
        out_shape=[
            jax.ShapeDtypeStruct((seqs, rows, ranks * SLOT), bf),
            jax.ShapeDtypeStruct((seqs, frames, SLOT), bf),
            jax.ShapeDtypeStruct((seqs, frames, SLOT), bf),
        ],
        compiler_params=pltpu.CompilerParams(vmem_limit_bytes=VM),
        name="cross_backward",
    )(rank, queries, keys_values, keys_values, grads, mixed, logs)


def self_backward(rank, qkv, grads, mixed, logs, seg_col, seg_row, stamp_col, ranks, heads, chunk=224):
    seqs, rows, _ = qkv.shape
    bf = jnp.bfloat16
    own = lambda offset: pl.BlockSpec((1, rows, SLOT), lambda b, rank: (b, 0, offset + rank[0]))
    col = pl.BlockSpec((1, rows, 1), lambda b, rank: (b, 0, 0))
    row = pl.BlockSpec((1, 1, rows), lambda b, rank: (b, 0, 0))
    return pl.pallas_call(
        functools.partial(self_backward_kernel, heads=heads, chunk=chunk),
        grid_spec=pltpu.PrefetchScalarGridSpec(
            num_scalar_prefetch=1,
            grid=(seqs,),
            in_specs=[
                own(0), own(ranks), own(2 * ranks), own(0), own(0),
                pl.BlockSpec((1, 1, 8, rows), lambda b, rank: (b, rank[0], 0, 0)), col, row, col,
            ],
            out_specs=pl.BlockSpec((1, rows, 3 * SLOT), lambda b, rank: (b, 0, 0)),
            scratch_shapes=[pltpu.VMEM((heads, rows, rows), bf), pltpu.VMEM((heads, rows, rows), bf)],
        ),
        out_shape=jax.ShapeDtypeStruct((seqs, rows, 3 * SLOT), bf),
        compiler_params=pltpu.CompilerParams(vmem_limit_bytes=VM),
        name="self_backward",
    )(rank, qkv, qkv, qkv, grads, mixed, logs, seg_col, seg_row, stamp_col)


def pack_kernel(tiles, line, out):
    side = tiles.shape[1]
    half, extra = side // 2, side - LANES
    for i in range(tiles.shape[0]):
        tile = tiles[i].astype(jnp.bfloat16)
        low = i * (side + half)
        out[low : low + side] = tile[:, :LANES]
        out[low + side : low + side + half] = jnp.concatenate([tile[:half, LANES:], tile[half:, LANES:]], axis=1)
    out[out.shape[0] - line.shape[0] :] = line[...].astype(jnp.bfloat16)


def pack(tiles, line):
    count, side, _ = tiles.shape
    rows = count * (side + side // 2) + line.shape[0]
    return pl.pallas_call(
        pack_kernel, out_shape=jax.ShapeDtypeStruct((rows, LANES), jnp.bfloat16), name="pack"
    )(tiles, line)


def gather_blocks(block, ranks, groups, ready):
    if ranks != 4 or groups != 8:
        return [lax.all_gather(block, ("dp", "tensor"), axis=0)], None, None, ready

    def flip(values, bits):
        return lax.ppermute(values, "dp", [(i, i ^ bits) for i in range(groups)])

    def turn(values, step):
        return lax.ppermute(values, "tensor", [(i, (i + step) % ranks) for i in range(ranks)])

    cut = block.shape[0] // 32 * 16
    one, three = turn(block, 1), turn(block, 3)
    held = block[None]
    sides = flip(held, 2), flip(held, 4)
    later, _ = lax.optimization_barrier((block, sides))
    two = turn(later, 2)
    units, before = [(0, held, sides)], sides
    for step, values in ((1, one), (3, three), (2, two)):
        if step == 1:
            values, ready = lax.optimization_barrier((values, ready))
        held, _ = lax.optimization_barrier((values[None], before))
        before = flip(held, 2), flip(held, 4)
        units.append((step, held, before))
    arrays, where = [], []
    for step, held, (across, along) in units:
        low, high = flip(across[:, :cut], 4), flip(along[:, cut:], 2)
        even = jnp.concatenate([held, across, along, jnp.concatenate([low, high], axis=1)], axis=0)
        for parity, array in enumerate((even, flip(even, 1))):
            arrays.append(array)
            where.append([(step, 2 * k + parity) for k in range(4)])
    return arrays, where, two, ready


def assemble_kernel(target, *refs, sources, own_tiles, tile_rows):
    ins, outs = refs[:sources], refs[sources : sources + 13]
    staging, (f_qkv, f_ckv, f_cq, f_wo, f_co, *f_wide), arrived, sent = refs[sources + 13], refs[sources + 14 : -2], refs[-2], refs[-1]
    side = tile_rows * 2 // 3
    half = side // 2
    at = 0
    for source in ins:
        blocks = source.shape[0]

        def fetch(k, _, source=source, at=at):
            for slot in range(own_tiles):
                pltpu.make_async_copy(
                    source.at[k, pl.ds(slot * tile_rows, tile_rows)],
                    staging.at[target[at + k * own_tiles + slot]],
                    arrived,
                ).start()
            return 0

        lax.fori_loop(0, blocks, fetch, 0)
        at += blocks * own_tiles
    pltpu.make_async_copy(staging, staging, arrived).wait()

    def parts(rank, ident):
        packed = staging.at[rank * 64 + ident]
        low = packed[side:]
        return packed[:side], jnp.concatenate([low[:, : side - LANES], low[:, side - LANES :]], axis=0)

    def columns(out, base, offset):
        for rank in range(4):
            for i in range(4):
                main, rest = parts(rank, base + i)
                rest = jnp.concatenate([rest, jnp.zeros((side, SLOT - side), jnp.bfloat16)], axis=1)
                out[i * side : (i + 1) * side, offset + rank * SLOT : offset + (rank + 1) * SLOT] = jnp.concatenate([main, rest], axis=1)

    def joined(rank, base):
        pieces = []
        for i in range(4):
            pieces.extend(parts(rank, base + i))
        return jnp.concatenate(pieces, axis=1)

    def padded_rows(out, base):
        for rank in range(4):
            out[rank * SLOT : rank * SLOT + side, :] = joined(rank, base)
            out[rank * SLOT + side : (rank + 1) * SLOT, :] = jnp.zeros((SLOT - side, 4 * side), jnp.bfloat16)

    copies = []

    def send(i, held):
        copy = pltpu.make_async_copy(held, outs[i], sent.at[i])
        copy.start()
        copies.append(copy)

    for m, base in enumerate((0, 4, 8)):
        columns(f_qkv, base, m * 4 * SLOT)
    send(0, f_qkv)
    for m, base in enumerate((16, 20)):
        columns(f_ckv, base, m * 4 * SLOT)
    send(1, f_ckv)
    columns(f_cq, 12, 0)
    send(2, f_cq)
    padded_rows(f_wo, 24)
    send(3, f_wo)
    padded_rows(f_co, 28)
    send(4, f_co)
    for m, base in enumerate((32, 48)):
        for rank in range(4):
            held = f_wide[m * 4 + rank]
            for i in range(4):
                held[i * side : (i + 1) * side] = joined(rank, base + 4 * i)
            send(5 + m * 4 + rank, held)
    for copy in copies:
        copy.wait()


def assemble(target, arrays, own_tiles, side):
    width = 4 * side
    tile_rows = side + side // 2
    bf = jnp.bfloat16
    shapes = [
        (width, 12 * SLOT), (width, 8 * SLOT), (width, 4 * SLOT), (4 * SLOT, width), (4 * SLOT, width),
    ] + [(width, width)] * 8
    anywhere = pl.BlockSpec(memory_space=pl.ANY)
    return pl.pallas_call(
        functools.partial(assemble_kernel, sources=len(arrays), own_tiles=own_tiles, tile_rows=tile_rows),
        grid_spec=pltpu.PrefetchScalarGridSpec(
            num_scalar_prefetch=1,
            grid=(1,),
            in_specs=[anywhere] * len(arrays),
            out_specs=[anywhere] * 13,
            scratch_shapes=[pltpu.VMEM((256, tile_rows, LANES), bf)]
            + [pltpu.VMEM(shape, bf) for shape in shapes]
            + [pltpu.SemaphoreType.DMA, pltpu.SemaphoreType.DMA((13,))],
        ),
        out_shape=[jax.ShapeDtypeStruct(shape, bf) for shape in shapes],
        compiler_params=pltpu.CompilerParams(vmem_limit_bytes=56 * 2**20),
        name="assemble",
    )(target, *arrays)


def weight_grads_kernel(
    rank, slot, sub, *refs, side, owned
):
    sources, lines, out, held, arrived = refs[: len(owned)], refs[len(owned)], refs[len(owned) + 1], refs[len(owned) + 2 : -1], refs[-1]
    copies = []
    for i, (source, to, own) in enumerate(zip(sources, held, owned)):
        if own:
            wide = to.shape[-1]
            source = source.at[:, pl.ds(pl.multiple_of(rank[0] * wide, LANES), wide)]
        copies.append(pltpu.make_async_copy(source, to, arrived.at[i]))
        copies[-1].start()

    def take(*which):
        for i in which:
            copies[i].wait()
        return [held[i] for i in which]

    half = side // 2
    tile_rows = side + half

    def keep(tile, ident):
        tile = tile.astype(jnp.bfloat16)
        at = pl.multiple_of(sub[ident] * tile_rows, 32)
        out[slot[ident], pl.ds(at, side)] = tile[:, :LANES]
        rest = tile[:, LANES:]
        out[slot[ident], pl.ds(at + side, half)] = jnp.concatenate([rest[:half], rest[half:]], axis=1)

    def slots(made, bases):
        for m, base in enumerate(bases):
            for i in range(4):
                keep(made[i * side : (i + 1) * side, m * SLOT : m * SLOT + side], base + i)

    def grid_of(made, base, rows):
        for i in range(rows):
            for j in range(4):
                keep(made[i * side : (i + 1) * side, j * side : (j + 1) * side], base + i * 4 + j)

    n3, grad_up = take(0, 1)
    grid_of(bdot(n3[...], grad_up[...], TN), 32, 4)
    active, b3 = take(2, 3)
    grid_of(bdot(active[...], b3[...], TN), 48, 4)
    mixed, b2 = take(4, 5)
    grid_of(bdot(mixed[...], b2[...], TN), 28, 1)
    frames, dk, dv = take(6, 7, 8)
    slots(bdot(frames[0], dk[0], TN) + bdot(frames[1], dk[1], TN), (16,))
    slots(bdot(frames[0], dv[0], TN) + bdot(frames[1], dv[1], TN), (20,))
    n2, dcq = take(9, 10)
    slots(bdot(n2[...], dcq[...], TN), (12,))
    attended, b1 = take(11, 12)
    grid_of(bdot(attended[...], b1[...], TN), 24, 1)
    n1, dqkv = take(13, 14)
    slots(bdot(n1[...], dqkv[...], TN), (0, 4, 8))
    for i in range(out.shape[0]):
        out[i, out.shape[1] - lines.shape[1] :] = lines[i].astype(jnp.bfloat16)


def weight_grads(rank, slot, sub, side, groups, own_tiles, lines, n1, dqkv, n2, dcq, frames, dk, dv, attended, b1, mixed, b2, n3, grad_up, active, b3):
    wide = 4 * side
    inputs = [n3, grad_up, active, b3, mixed, b2, frames, dk, dv, n2, dcq, attended, b1, n1, dqkv]
    widths = [0, wide, wide, 0, SLOT, 0, 0, 0, 0, 0, SLOT, SLOT, 0, 0, 0]
    owned = [0 < size < x.shape[-1] for x, size in zip(inputs, widths)]
    shapes = [(x.shape[0], size) if own else x.shape for x, size, own in zip(inputs, widths, owned)]
    shape = (groups, own_tiles * (side + side // 2) + lines.shape[1], LANES)
    return pl.pallas_call(
        functools.partial(weight_grads_kernel, side=side, owned=owned),
        grid_spec=pltpu.PrefetchScalarGridSpec(
            num_scalar_prefetch=3,
            grid=(1,),
            in_specs=[pl.BlockSpec(memory_space=pl.ANY)] * len(inputs)
            + [pl.BlockSpec(lines.shape, lambda i, rank, slot, sub: (0, 0, 0))],
            out_specs=pl.BlockSpec(shape, lambda i, rank, slot, sub: (0, 0, 0)),
            scratch_shapes=[pltpu.VMEM(size, jnp.bfloat16) for size in shapes] + [pltpu.SemaphoreType.DMA((len(inputs),))],
        ),
        out_shape=jax.ShapeDtypeStruct(shape, jnp.bfloat16),
        compiler_params=pltpu.CompilerParams(vmem_limit_bytes=60 * 2**20),
        name="weight_grads",
    )(rank, slot, sub, *inputs, lines)


def scatter_blocks(blocks, ranks, groups):
    f32, bf16 = jnp.float32, jnp.bfloat16
    if groups != 8:
        return lax.psum_scatter(blocks, "dp", scatter_dimension=0, tiled=True)[0].astype(f32)

    def sent(values, bits):
        return lax.ppermute(values.astype(bf16), "dp", [(i, i ^ bits) for i in range(groups)]).astype(f32)

    half = groups // 2
    cut = blocks.shape[1] // 32 * 16
    chip = (blocks[:half].astype(f32) + sent(blocks[half:], 1)).astype(bf16)
    low, high = chip[:, :cut], chip[:, cut:]
    low_x, high_y = sent(jnp.stack([low[1], low[3]]), 2), sent(high[2:], 4)
    low = jnp.stack([low[0], low[2]]).astype(f32) + low_x
    high = high[:2].astype(f32) + high_y
    low_y, high_x = sent(low[1], 4), sent(high[1], 2)
    return jnp.concatenate([low[0] + low_y, high[0] + high_x], axis=0)


def first_back_kernel(rank, dqkv, query_weight, key_weight, value_weight, hidden, out, sums):
    weights = jnp.concatenate([query_weight[...], key_weight[...], value_weight[...]], axis=1)
    made = bdot(dqkv[...], weights, NT)
    unit, _ = unit_rows(hidden[0].astype(jnp.float32))
    sums[0:1] = jnp.sum(made * unit, axis=0, keepdims=True)
    sums[1:2] = jnp.sum(made, axis=0, keepdims=True)
    out[...] = made.astype(jnp.bfloat16)


def first_back(rank, dqkv, weight, hidden, ranks):
    _, tokens, width = hidden.shape
    own = lambda offset: pl.BlockSpec((width, SLOT), lambda i, rank: (0, offset + rank[0]))
    whole = lambda shape: pl.BlockSpec(shape, lambda i, rank: (0, 0))
    return pl.pallas_call(
        first_back_kernel,
        grid_spec=pltpu.PrefetchScalarGridSpec(
            num_scalar_prefetch=1,
            grid=(1,),
            in_specs=[whole(dqkv.shape), own(0), own(ranks), own(2 * ranks), pl.BlockSpec((1, tokens, width), lambda i, rank: (0, 0, 0))],
            out_specs=[whole((tokens, width)), whole((2, width))],
        ),
        out_shape=[jax.ShapeDtypeStruct((tokens, width), jnp.bfloat16), jax.ShapeDtypeStruct((2, width), jnp.float32)],
        compiler_params=pltpu.CompilerParams(vmem_limit_bytes=VM),
        name="first_back",
    )(rank, dqkv, weight, weight, weight, hidden)


def frames_kernel(frames, weight, bias, out):
    for i in range(out.shape[0]):
        span = slice(i * SLOT, (i + 1) * SLOT)
        out[i, 0] = (bdot(frames[0], weight[:, span], NN) + bias[i]).astype(jnp.bfloat16)


def frame_projection(frames, weight, bias):
    seqs, count, width = frames.shape
    slots = weight.shape[1] // SLOT
    return pl.pallas_call(
        frames_kernel,
        grid=(seqs, slots // 4),
        in_specs=[
            pl.BlockSpec((1, count, width), lambda b, c: (b, 0, 0)),
            pl.BlockSpec((width, 4 * SLOT), lambda b, c: (0, c)),
            pl.BlockSpec((4, 1, SLOT), lambda b, c: (c, 0, 0)),
        ],
        out_specs=pl.BlockSpec((4, 1, count, SLOT), lambda b, c: (c, b, 0, 0)),
        out_shape=jax.ShapeDtypeStruct((slots, seqs, count, SLOT), jnp.bfloat16),
        compiler_params=pltpu.CompilerParams(vmem_limit_bytes=VM),
        name="frame_projection",
    )(frames, weight, bias.reshape(slots, 1, SLOT))


def frames_back_kernel(rank, dk, dv, key_weight, value_weight, out, *, parts):
    made = bdot(dk[0], key_weight[...], NT) + bdot(dv[0], value_weight[...], NT)
    share = made.shape[0] // parts
    for part in range(parts):
        piece = made[part * share : (part + 1) * share]
        out[part, 0] = jnp.concatenate([piece, jnp.zeros((out.shape[2] - share, piece.shape[1]), jnp.float32)], axis=0).astype(jnp.bfloat16)


def frames_back(rank, dk, dv, weight, parts):
    seqs, count, slot = dk.shape
    width = weight.shape[0]
    padded = -(-(count // parts) // 16) * 16
    own = pl.BlockSpec((1, count, slot), lambda b, rank: (b, 0, 0))
    return pl.pallas_call(
        functools.partial(frames_back_kernel, parts=parts),
        grid_spec=pltpu.PrefetchScalarGridSpec(
            num_scalar_prefetch=1,
            grid=(seqs,),
            in_specs=[
                own, own,
                pl.BlockSpec((width, slot), lambda b, rank: (0, rank[0])),
                pl.BlockSpec((width, slot), lambda b, rank: (0, parts + rank[0])),
            ],
            out_specs=pl.BlockSpec((parts, 1, padded, width), lambda b, rank: (0, b, 0, 0)),
        ),
        out_shape=jax.ShapeDtypeStruct((parts, seqs, padded, width), jnp.bfloat16),
        compiler_params=pltpu.CompilerParams(vmem_limit_bytes=VM),
        name="frames_back",
    )(rank, dk, dv, weight, weight)


def product(left_part, right_part):
    return jnp.dot(left_part, right_part, preferred_element_type=jnp.float32)


def times_transpose(left_part, right_part):
    return lax.dot_general(left_part, right_part, (NT, ((), ())), preferred_element_type=jnp.float32)


def unit_rows(values):
    centre = jnp.mean(values, axis=-1, keepdims=True)
    centred = values - centre
    inverse = lax.rsqrt(jnp.mean(centred * centred, axis=-1, keepdims=True) + norm_eps)
    return centred * inverse, inverse


def normalize(values, gain, shift):
    return unit_rows(values)[0] * gain + shift


def normalize_back(values, gain, grads):
    unit, inverse = unit_rows(values)
    scaled = grads * gain
    result = inverse * (
        scaled
        - jnp.mean(scaled, axis=-1, keepdims=True)
        - unit * jnp.mean(scaled * unit, axis=-1, keepdims=True)
    )
    return result, jnp.sum(grads * unit, axis=0), jnp.sum(grads, axis=0)


def gelu_pair(value):
    size = jnp.abs(value) * 0.7071067811865476
    bell = jnp.exp(-size * size)
    t = 1.0 / (1.0 + 0.3275911 * size)
    poly = t * (0.254829592 + t * (-0.284496736 + t * (1.421413741 + t * (-1.453152027 + t * 1.061405429))))
    tail = 0.5 * poly * bell
    level = jnp.where(value >= 0, 1.0 - tail, tail)
    return value * level, level + value * bell * 0.3989422804014327


def middle_kernel(rank, *refs, parts):
    mixed, first_sum, top_grad, vectors, inner_bias, c_o = refs[:6]
    w_in, w_out = refs[6 : 6 + parts], refs[6 + parts : 6 + 2 * parts]
    (
        block_out, grad_out, grad_mixed, n3_out, b2_out, b3_out, active_out, up_out, sums, up_sums, acts, slopes, ups,
    ) = refs[6 + 2 * parts :]
    f32, bf16 = jnp.float32, jnp.bfloat16
    width = first_sum.shape[1]
    row = lambda i: vectors[i : i + 1]
    cut = lambda i: slice(i * width, (i + 1) * width)
    fold = lambda values: jnp.sum(values, axis=0, keepdims=True)

    def back(unit, inverse, scaled):
        centre = jnp.mean(scaled, axis=-1, keepdims=True)
        return inverse * (scaled - centre - unit * jnp.mean(scaled * unit, axis=-1, keepdims=True))

    second_sum = first_sum[...] + bdot(mixed[...], c_o[...], NN) + row(9)
    unit, inverse = unit_rows(second_sum)
    n3 = (unit * row(4) + row(5)).astype(bf16)
    n3_out[...] = n3
    third_sum = second_sum + row(10)
    for i in range(parts):
        value, slope = gelu_pair(bdot(n3, w_in[i][...], NN) + inner_bias[:, cut(i)])
        acts[i] = value.astype(bf16)
        slopes[i] = slope.astype(bf16)
        third_sum = third_sum + bdot(acts[i], w_out[i][...], NN)
    active_out[...] = acts[rank[0]]
    last, last_inverse = unit_rows(third_sum)
    block_out[...] = last * row(6) + row(7)
    grads = top_grad[0].astype(f32)
    grad_third = back(last, last_inverse, grads * row(6))
    b3 = grad_third.astype(bf16)
    b3_out[...] = b3
    grad_normed, ups_now = None, []
    for i in range(parts):
        grad_up = (bdot(b3, w_out[i][...], NT) * slopes[i].astype(f32)).astype(bf16)
        ups[i] = grad_up
        ups_now.append(fold(grad_up.astype(f32)))
        term = bdot(grad_up, w_in[i][...], NT)
        grad_normed = term if grad_normed is None else grad_normed + term
    up_out[...] = ups[rank[0]]
    grad_second = grad_third + back(unit, inverse, grad_normed * row(4))
    grad_out[...] = grad_second
    b2 = grad_second.astype(bf16)
    b2_out[...] = b2
    grad_mixed[...] = bdot(b2, c_o[...], NT).astype(bf16)
    now = jnp.concatenate(
        [
            fold(grad_normed * unit), fold(grad_normed), fold(grads * last), fold(grads),
            fold(b2.astype(f32)), fold(b3.astype(f32)), jnp.zeros((2, width), f32),
        ],
        axis=0,
    )
    ups_all = jnp.concatenate(ups_now, axis=0)
    start = pl.program_id(0) == 0

    @pl.when(start)
    def _():
        sums[...] = now
        up_sums[...] = ups_all

    @pl.when(jnp.logical_not(start))
    def _():
        sums[...] += now
        up_sums[...] += ups_all


def middle(rank, mixed, first_sum, top_grad, c_o, w_in, w_out, vectors, inner_bias, block=448):
    f32, bf16 = jnp.float32, jnp.bfloat16
    tokens, width = first_sum.shape
    slots, parts = mixed.shape[1], len(w_in)
    rows = lambda size: pl.BlockSpec((block, size), lambda i, rank: (i, 0))
    once = lambda x: pl.BlockSpec(x.shape, lambda i, rank: (0, 0), pipeline_mode=pl.Buffered(1))
    total = lambda count: pl.BlockSpec((count, width), lambda i, rank: (0, 0))
    out = lambda size, kind: jax.ShapeDtypeStruct((tokens, size), kind)
    fixed = [vectors, inner_bias, c_o, *w_in, *w_out]
    return pl.pallas_call(
        functools.partial(middle_kernel, parts=parts),
        grid_spec=pltpu.PrefetchScalarGridSpec(
            num_scalar_prefetch=1,
            grid=(tokens // block,),
            in_specs=[rows(slots), rows(width), pl.BlockSpec((1, block, width), lambda i, rank: (1, i, 0))]
            + [once(x) for x in fixed],
            out_specs=[rows(width), rows(width), rows(slots)] + [rows(width)] * 5 + [total(8), total(parts)],
            scratch_shapes=[pltpu.VMEM((parts, block, width), bf16)] * 3,
        ),
        out_shape=[out(width, f32), out(width, f32), out(slots, bf16)]
        + [out(width, bf16)] * 5
        + [jax.ShapeDtypeStruct((8, width), f32), jax.ShapeDtypeStruct((parts, width), f32)],
        compiler_params=pltpu.CompilerParams(vmem_limit_bytes=VM),
        name="middle",
    )(rank, mixed, first_sum, top_grad, *fixed)


def first_kernel(hidden, vectors, bias, weight, n1, out):
    made = (unit_rows(hidden[0].astype(jnp.float32))[0] * vectors[0:1] + vectors[1:2]).astype(jnp.bfloat16)
    n1[...] = made
    for low in range(0, weight.shape[1], 4 * SLOT):
        span = slice(low, low + 4 * SLOT)
        out[:, span] = (bdot(made, weight[:, span], NN) + bias[:, span]).astype(jnp.bfloat16)


def first_projections(both, vectors, bias, weight, block=448):
    _, tokens, width = both.shape
    wide = weight.shape[1]
    once = lambda x: pl.BlockSpec(x.shape, lambda i: (0, 0), pipeline_mode=pl.Buffered(1))
    return pl.pallas_call(
        first_kernel,
        grid=(tokens // block,),
        in_specs=[pl.BlockSpec((1, block, width), lambda i: (0, i, 0)), once(vectors), once(bias), once(weight)],
        out_specs=[pl.BlockSpec((block, width), lambda i: (i, 0)), pl.BlockSpec((block, wide), lambda i: (i, 0))],
        out_shape=[jax.ShapeDtypeStruct((tokens, width), jnp.bfloat16), jax.ShapeDtypeStruct((tokens, wide), jnp.bfloat16)],
        compiler_params=pltpu.CompilerParams(vmem_limit_bytes=VM),
        name="first_projections",
    )(both, vectors, bias, weight)


def spread_heads(rows, ranks):
    lead = rows.shape[0]
    side = rows.shape[1] // ranks
    return jnp.pad(rows.reshape(lead, ranks, side), ((0, 0), (0, 0), (0, SLOT - side))).reshape(lead, ranks * SLOT)


def shards(
    hidden_in, frames, cotangent, segments, stamps, owner_list, master_tiles, tile_first, tile_second,
    tile_stats, tile_bases, master_vectors, vector_first, vector_second,
):
    f32, bf16 = jnp.float32, jnp.bfloat16
    ranks, groups = lax.axis_size("tensor"), lax.axis_size("dp")
    rank, group = lax.axis_index("tensor"), lax.axis_index("dp")
    seqs, local_rows, width = hidden_in.shape
    rows = local_rows * ranks
    tokens = seqs * rows
    own_tiles, side = master_tiles.shape[1], master_tiles.shape[-1]
    heads = side // HEAD
    rank_ref = rank.astype(jnp.int32)[None]

    length = master_vectors.shape[0]
    line_rows = -(-length // (16 * LANES)) * 16
    line = jnp.pad(master_vectors, (0, line_rows * LANES - length)).reshape(line_rows, LANES)
    block = pack(master_tiles[0], line)
    ready = soap_pre(tile_first[0], tile_stats[0], tile_bases[0])
    frames = with_layout_constraint(frames, Layout(major_to_minor=(0, 1, 2)))
    arrays, where, last, (ready, frames) = gather_blocks(block, ranks, groups, (ready, frames))
    if where is None:
        source_rank = jnp.tile(jnp.arange(ranks, dtype=jnp.int32), groups)
        source_group = jnp.repeat(jnp.arange(groups, dtype=jnp.int32), ranks)
        lines = arrays[0].reshape(groups, ranks, -1, LANES)[:, 0, -line_rows:].reshape(groups, -1)[:, :length]
    else:
        steps = jnp.array([step for array in where for step, _ in array], jnp.int32)
        bits = jnp.array([bit for array in where for _, bit in array], jnp.int32)
        source_rank = (rank - steps) % ranks
        source_group = group ^ bits
        lines = jnp.concatenate([array[:, -line_rows:] for array in arrays[:2]], axis=0).reshape(groups, -1)[:, :length]
        spots = source_group[:groups]
        order = jnp.arange(groups, dtype=jnp.int32)
        lines = jnp.sum(jnp.where((spots[None] == order[:, None])[:, :, None], lines[None].astype(f32), 0.0), axis=1)
    vectors = lines.astype(f32).reshape(19, width)

    count = owner_list.shape[0]
    position = jnp.arange(count, dtype=jnp.int32)
    place = jnp.sum(jnp.where(owner_list[None, :] == position[:, None], position[None, :], 0), axis=1)
    spot = (source_group[:, None] * own_tiles + jnp.arange(own_tiles, dtype=jnp.int32)[None]).reshape(-1)
    ident = jnp.sum(jnp.where(spot[:, None] == position[None, :], owner_list[None, :], 0), axis=1)
    target = jnp.repeat(source_rank, own_tiles) * count + ident
    w_qkv, c_kv, c_q, w_o, c_o, *wide = assemble(target, arrays, own_tiles, side)
    w_in, w_out = wide[:4], wide[4:]

    rows_in = jnp.stack([hidden_in, cotangent])
    if where is not None:
        rows_in, _ = lax.optimization_barrier((rows_in, last))
    both = lax.all_gather(rows_in, "tensor", axis=2, tiled=True)
    both = both.reshape(2, tokens, width)
    hidden = both[0].astype(f32)

    head_bias = spread_heads(vectors[11:15], ranks)
    none = jnp.zeros_like(head_bias[0])
    inner_bias = vectors[15:19].reshape(-1)
    seg_col, seg_row = segments[:, :, None], segments[:, None, :]
    stamp_col, stamp_row = stamps[:, :, None], stamps[:, None, :]

    def split(values):
        return values.reshape(seqs, rows, values.shape[-1])

    def flat(values):
        return values.reshape(tokens, values.shape[-1])

    def own_rows(values):
        return lax.dynamic_slice_in_dim(split(values), rank * local_rows, local_rows, axis=1)

    keys_values = frame_projection(frames, c_kv, jnp.concatenate([none, head_bias[3]]))
    n1, qkv = first_projections(both, vectors, jnp.concatenate([head_bias[0], none, head_bias[1]])[None], w_qkv)
    qkv = split(qkv)
    attended, self_logs = self_forward(qkv, seg_col, seg_row, stamp_row, ranks, heads)
    attended = flat(attended)
    first_sum = hidden + product(attended, w_o) + vectors[8]
    n2 = normalize(first_sum, vectors[2], vectors[3]).astype(bf16)
    cross_queries = split((product(n2, c_q) + head_bias[2]).astype(bf16))
    mixed, cross_logs = cross_forward(cross_queries, keys_values, ranks, heads)
    mixed = flat(mixed)
    out_rows, grad_second, grad_mixed, n3, b2, b3, active, grad_up, sums, up_sum = middle(
        rank_ref, mixed, first_sum, both, c_o, w_in, w_out, vectors, inner_bias[None]
    )
    block_out = own_rows(out_rows)
    grad_mixed = split(grad_mixed)
    dcq, dk, dv = cross_backward(
        rank_ref, cross_queries, keys_values, grad_mixed, split(mixed), cross_logs, ranks, heads
    )
    dcq = flat(dcq)
    frames_part = frames_back(rank_ref, dk, dv, c_kv, ranks)
    dcq, frames_part = lax.optimization_barrier((dcq, frames_part))
    frames_sum = lax.psum_scatter(
        frames_part.reshape(ranks * seqs, frames_part.shape[2], width), "tensor", scatter_dimension=0, tiled=True
    )
    frames_grad = frames_sum[:, : frames.shape[1] // ranks].astype(f32)
    back, gain_two, shift_two = normalize_back(first_sum, vectors[2], times_transpose(dcq, c_q))
    grad_first = grad_second + back
    b1 = grad_first.astype(bf16)
    grad_attended = split(times_transpose(b1, w_o).astype(bf16))
    dqkv = flat(
        self_backward(
            rank_ref, qkv, grad_attended, split(attended), self_logs, seg_col, seg_row, stamp_col, ranks, heads
        )
    )

    part_one, first_sums = first_back(rank_ref, dqkv, w_qkv, both, ranks)
    grad_one = lax.psum_scatter(split(part_one), "tensor", scatter_dimension=1, tiled=True).astype(f32)
    back, _, _ = normalize_back(
        hidden_in.astype(f32).reshape(-1, width), vectors[0], grad_one.reshape(-1, width)
    )
    input_grad = own_rows(grad_first) + back.reshape(hidden_in.shape)

    def total(values):
        return jnp.sum(values.astype(f32), axis=tuple(range(values.ndim - 1)))

    same = jnp.stack(
        [gain_two, shift_two, sums[0], sums[1], sums[2], sums[3], total(b1), sums[4], sums[5]]
    )
    query_sum = total(dcq).reshape(ranks, SLOT)[:, :side].reshape(1, width)
    even = 1.0 / ranks
    dqkv_sum = total(dqkv)
    own_sums = jnp.stack([dqkv_sum[:side], dqkv_sum[2 * SLOT : 2 * SLOT + side], total(dv)[:side]])
    own_sums = lax.dynamic_update_slice(jnp.zeros((3, width), f32), own_sums, (0, rank * side))
    vector_terms = jnp.concatenate(
        [first_sums, same * even, own_sums[:2], query_sum * even, own_sums[2:], up_sum * even]
    )
    lines = vector_terms.reshape(groups, length)
    owner = place // own_tiles
    if groups == 8:
        bits = owner ^ group
        slot = (bits & 1) * (groups // 2) + (bits >> 1)
        at = jnp.arange(groups, dtype=jnp.int32)
        wanted = group ^ (2 * (at % (groups // 2)) + at // (groups // 2))
        lines = jnp.sum(jnp.where((wanted[:, None] == at[None])[:, :, None], lines[None], 0.0), axis=1)
    else:
        slot = owner
    lines = jnp.pad(lines, ((0, 0), (0, line_rows * LANES - length))).reshape(groups, line_rows, LANES)
    blocks = weight_grads(
        rank_ref, slot, place % own_tiles, side, groups, own_tiles, lines,
        n1, dqkv, n2, dcq, frames, dk, dv, attended, b1, mixed, b2, n3, grad_up, active, b3,
    )
    owned = scatter_blocks(blocks, ranks, groups)
    line = owned[-line_rows:]
    new_first, new_second, new_master, new_stats, new_bases = soap(
        owned, master_tiles[0], tile_first[0], tile_second[0], tile_stats[0], tile_bases[0], *ready
    )
    reach = 1
    while reach < ranks:
        other = lax.ppermute(line, "tensor", [(i, i ^ reach) for i in range(ranks)])
        other, _ = lax.optimization_barrier((other, new_second if reach == 1 else new_bases))
        line = line + other
        reach *= 2
    vector_grad = line.reshape(-1)[:length]
    new_vector_first = beta_one * vector_first + (1.0 - beta_one) * vector_grad
    new_vector_second = beta_two * vector_second + (1.0 - beta_two) * vector_grad * vector_grad
    new_vectors = master_vectors - rate_vectors * (new_vector_first / (1.0 - beta_one**STEP)) / (
        jnp.sqrt(new_vector_second / (1.0 - beta_two**STEP)) + adam_eps
    )
    return (
        block_out, input_grad, frames_grad, new_master[None], new_first[None], new_second[None],
        new_stats[None], new_bases[None], new_vectors, new_vector_first, new_vector_second,
    )


def solution(mesh):
    rows, seqs, tiles, pairs = (
        P("dp", "tensor", None), P("dp", None), P("tensor", "dp", None, None), P("tensor", "dp", None, None, None)
    )
    line = P("dp")
    in_specs = (
        rows, P("dp", None, None), rows, seqs, seqs, P(), tiles, tiles, tiles, pairs, pairs, line, line, line
    )
    out_specs = (rows, rows, rows, tiles, tiles, tiles, pairs, pairs, line, line, line)
    return jax.shard_map(shards, mesh=mesh, in_specs=in_specs, out_specs=out_specs, check_vma=False)
```

```python
import functools

import jax
import jax.numpy as jnp
from jax import lax
from jax.experimental import pallas as pl
from jax.experimental.pallas import tpu as pltpu
from jax.experimental.layout import Layout, with_layout_constraint
from jax.sharding import PartitionSpec as P

HEAD = 64
FF = 3072
STEP = 5
LANES = 128
SLOT = 256
VM = 56 * 2**20
HI = lax.Precision.HIGHEST

norm_eps = 1e-05
beta_one = 0.9
beta_two = 0.95
adam_eps = 1e-08
rate_tiles = 0.05
rate_vectors = 0.3
score_scale = 0.125


def split2(a):
    hi = a.astype(jnp.bfloat16)
    lo = (a - hi.astype(jnp.float32)).astype(jnp.bfloat16)
    return hi, lo

def bdot(a, b, dims):
    return lax.dot_general(a, b, (dims, ((), ())), preferred_element_type=jnp.float32)

NN = ((1,), (0,)); TN = ((0,), (0,)); NT = ((1,), (1,))

def dot3(a, b, dims):
    (ah, al), (bh, bl) = a, b
    return bdot(ah, bh, dims) + (bdot(ah, bl, dims) + bdot(al, bh, dims))

def dothi(a, b, dims):
    return lax.dot_general(a, b, (dims, ((), ())), precision=HI, preferred_element_type=jnp.float32)

def soap_pre_kernel(first, stats, bases, rot_first, stats_rot):
    ql, qr = split2(bases[0, 0]), split2(bases[0, 1])
    inner = split2(dot3(ql, split2(first[0]), TN))
    rot_first[0] = dot3(inner, qr, NN)
    stats_rot[0, 0] = dot3(split2(stats[0, 0]), ql, NN)
    stats_rot[0, 1] = dot3(split2(stats[0, 1]), qr, NN)

def soap_main_kernel(grad, master, first, second, stats, bases, rot_first, stats_rot,
                     new_master, new_first, new_second, new_stats, turned, grams):
    side = master.shape[1]
    rest = grad[side:]
    rest = jnp.concatenate([rest[:, : side - LANES], rest[:, side - LANES :]], axis=0)
    g32 = jnp.concatenate([grad[:side], rest], axis=1)
    g, ql, qr = split2(g32), split2(bases[0, 0]), split2(bases[0, 1])
    new_first[0] = beta_one * first[0] + (1.0 - beta_one) * g32
    part_left = split2(dot3(ql, g, TN))
    rotated = dot3(part_left, qr, NN)
    fresh = beta_two * second[0] + (1.0 - beta_two) * rotated * rotated
    new_second[0] = fresh
    moment = (beta_one * rot_first[0] + (1.0 - beta_one) * rotated) / (1.0 - beta_one**STEP)
    step = moment / (jnp.sqrt(fresh / (1.0 - beta_two**STEP)) + adam_eps)
    back = split2(dot3(ql, split2(step), NN))
    new_master[0] = master[0] - rate_tiles * dot3(back, qr, NT)
    new_stats[0, 0] = beta_two * stats[0, 0] + (1.0 - beta_two) * dot3(g, g, NT)
    new_stats[0, 1] = beta_two * stats[0, 1] + (1.0 - beta_two) * dot3(g, g, TN)
    part_right = split2(dot3(g, qr, NN))
    for side, term in ((0, dot3(g, part_left, NT)), (1, dot3(g, part_right, TN))):
        side_turned = beta_two * stats_rot[0, side] + (1.0 - beta_two) * term
        turned[0, side] = side_turned
        halves = split2(side_turned)
        grams[0, side] = dot3(halves, halves, TN)

def chol_kernel(turned, grams, out, work, fac, *, block, unroll, passes):
    count, side = work.shape[0], work.shape[1]
    wide = work.shape[2] // 2
    for m in range(count):
        work[m, :, :side] = grams[m]
        work[m, :, side:wide] = jnp.zeros((side, wide - side), jnp.float32)
        work[m, :, wide : wide + side] = turned[m].T
        work[m, :, wide + side :] = jnp.zeros((side, wide - side), jnp.float32)
    brow = lax.broadcasted_iota(jnp.int32, (count, block, 2 * block), 1)
    bcol = lax.broadcasted_iota(jnp.int32, (count, block, 2 * block), 2)
    aug_eye = ((bcol - block) == brow).astype(jnp.float32)
    for k in range(side // block):
        lo, hi = k * block, (k + 1) * block
        diag = work[:, lo:hi, lo:hi]
        w = jnp.concatenate([diag, jnp.zeros_like(diag)], axis=2) + aug_eye
        for j in range(block - 1):
            piv = w[:, j : j + 1, :]
            ratio = w[:, :, j : j + 1] / w[:, j : j + 1, j : j + 1]
            w = w - jnp.where(brow > j, ratio * piv, 0.0)
        d = jnp.sum(jnp.where(brow == bcol, w, 0.0), axis=2, keepdims=True)
        fac[...] = w[:, :, block:] * lax.rsqrt(d)

        def several(i, _):
            for u in range(unroll):
                m = i * unroll + u
                if passes == 6:
                    y = dothi(fac[m], work[m, lo:hi, :], NN)
                else:
                    y = dot3(split2(fac[m]), split2(work[m, lo:hi, :]), NN)
                work[m, lo:hi, :] = y
                if hi < side:
                    turn = y[:, :side].T[hi:]
                    if passes == 6:
                        step = dothi(turn, y, NN)
                    else:
                        step = dot3(split2(turn), split2(y), NN)
                    work[m, hi:, :] = work[m, hi:, :] - step
            return 0
        lax.fori_loop(0, count // unroll, several, 0)
    for m in range(count):
        out[m] = work[m, :, wide : wide + side].T

def tile_spec(side):
    return pl.BlockSpec((1, side, side), lambda i: (i, 0, 0))
def pair_spec(side):
    return pl.BlockSpec((1, 2, side, side), lambda i: (i, 0, 0, 0))

def soap_pre(first, stats, bases):
    n, side = first.shape[0], first.shape[1]
    t, p = tile_spec(side), pair_spec(side)
    return pl.pallas_call(soap_pre_kernel, grid=(n,), in_specs=[t, p, p], out_specs=[t, p],
        out_shape=[jax.ShapeDtypeStruct(first.shape, jnp.float32), jax.ShapeDtypeStruct(stats.shape, jnp.float32)],
        name="soap_pre")(first, stats, bases)

def soap_main(grad, master, first, second, stats, bases, rot_first, stats_rot):
    n, side = first.shape[0], first.shape[1]
    t, p = tile_spec(side), pair_spec(side)
    f = jnp.float32
    ts, ps = jax.ShapeDtypeStruct(first.shape, f), jax.ShapeDtypeStruct(stats.shape, f)
    return pl.pallas_call(soap_main_kernel, grid=(n,), in_specs=[pl.BlockSpec((side + side // 2, LANES), lambda i: (i, 0)), t, t, t, p, p, t, p],
        out_specs=[t, t, t, p, p, p], out_shape=[ts, ts, ts, ps, ps, ps], name="soap_main")(
        grad, master, first, second, stats, bases, rot_first, stats_rot)

def chol_bases(turned, grams, block=64, unroll=4, passes=3):
    n, _, side, _ = turned.shape
    shape = (2 * n, side, side)
    unroll = min(unroll, 2 * n)
    out = pl.pallas_call(functools.partial(chol_kernel, block=block, unroll=unroll, passes=passes),
        out_shape=jax.ShapeDtypeStruct(shape, jnp.float32),
        scratch_shapes=[pltpu.VMEM((2 * n, side, 512), jnp.float32), pltpu.VMEM((2*n, block, block), jnp.float32)],
        compiler_params=pltpu.CompilerParams(vmem_limit_bytes=48 * 2**20), name="chol_bases")(
        turned.reshape(shape), grams.reshape(shape))
    return out.reshape(turned.shape)


def soap(gradient, master, first, second, statistics, bases, rot_first, stats_rot):
    nm, nf, ns, nst, turned, grams = soap_main(gradient, master, first, second, statistics, bases, rot_first, stats_rot)
    return nf, ns, nm, nst, chol_bases(turned, grams)


def head_pick(shape, head):
    lane = lax.broadcasted_iota(jnp.int32, shape, len(shape) - 1)
    return (lane >= HEAD) if head % 2 else (lane < HEAD)


def forward_heads(query, key, value, allowed, heads, chunk):
    rows = query.shape[0]
    units = [(low, head) for low in range(0, rows, chunk) for head in range(heads)]
    spans = [slice(head // 2 * LANES, head // 2 * LANES + LANES) for head in range(heads)]
    own_values = []
    for head in range(heads):
        block = value[:, spans[head]]
        own_values.append(jnp.where(head_pick(block.shape, head), block, jnp.ones_like(block)))

    def scores_of(unit):
        low, head = unit
        block = query[low : low + chunk, spans[head]]
        own = jnp.where(head_pick(block.shape, head), block, jnp.zeros_like(block)) * jnp.bfloat16(score_scale)
        return bdot(own, key[:, spans[head]], NT)

    done, logs = {}, {}
    ahead = scores_of(units[0])
    for i, (low, head) in enumerate(units):
        scores = ahead
        if i + 1 < len(units):
            ahead = scores_of(units[i + 1])
        if allowed is not None:
            scores = jnp.where(allowed[low : low + chunk], scores, -1e30)
        top = jnp.max(scores, axis=1, keepdims=True)
        weights = jnp.exp(scores - top).astype(jnp.bfloat16)
        both = bdot(weights, own_values[head], NN)
        turned = pltpu.roll(both, HEAD, 1)
        pick = head_pick(both.shape, head)
        done[low, head] = both / turned
        logs[low, head] = top + jnp.log(jnp.where(pick, turned, both))
    columns, lines = [], []
    for low in range(0, rows, chunk):
        blocks = []
        lane = lax.broadcasted_iota(jnp.int32, (chunk, LANES), 1)
        line = jnp.zeros((chunk, LANES), jnp.float32)
        for first in range(0, heads, 2):
            other = done[low, first + 1] if first + 1 < heads else 0.0
            blocks.append(jnp.where(lane < HEAD, done[low, first], other).astype(jnp.bfloat16))
        for head in range(heads):
            line = jnp.where(lane == head, logs[low, head], line)
        columns.append(jnp.concatenate(blocks, axis=1))
        lines.append(line)
    return jnp.concatenate(columns, axis=0), jnp.concatenate(lines, axis=0).T[:8]


def cross_forward_kernel(query, key, value, out, logs, *, heads, chunk):
    out[0], logs[0, 0] = forward_heads(query[0], key[0, 0], value[0, 0], None, heads, chunk)


def self_forward_kernel(query, key, value, seg_col, seg_row, stamp_row, out, logs, *, heads, chunk):
    rows = query.shape[1]
    at = lax.broadcasted_iota(jnp.int32, (rows, rows), 0)
    key_at = lax.broadcasted_iota(jnp.int32, (rows, rows), 1)
    allowed = (key_at <= at) & (seg_col[0] == seg_row[0]) & ((stamp_row[0] == 0) | (key_at == at))
    out[0], logs[0, 0] = forward_heads(query[0], key[0], value[0], allowed, heads, chunk)


def backward_heads(query, key, value, grad, mixed, logs, allowed, heads, chunk, probs_ref, scores_ref):
    keys = key.shape[0]
    spans = [slice(head // 2 * LANES, head // 2 * LANES + LANES) for head in range(heads)]
    products = (grad.astype(jnp.float32) * mixed.astype(jnp.float32)).T
    own_query, own_grad, turned, dots, total = [], [], [], [], [None] * heads
    for head in range(heads):
        pick = head_pick((query.shape[0], LANES), head)
        zero = jnp.zeros((query.shape[0], LANES), jnp.bfloat16)
        own_query.append(jnp.where(pick, query[:, spans[head]], zero) * jnp.bfloat16(score_scale))
        own_grad.append(jnp.where(pick, grad[:, spans[head]], zero))
        dots.append(jnp.sum(products[head * HEAD : (head + 1) * HEAD], axis=0, keepdims=True))
        if head % 2 == 0:
            turned.append(key[:, spans[head]].T)
    units = [(low, head) for low in range(0, keys, chunk) for head in range(heads)]

    def products_of(unit):
        low, head = unit
        high = min(low + chunk, keys)
        return bdot(key[low:high, spans[head]], own_query[head], NT), bdot(value[low:high, spans[head]], own_grad[head], NT)

    ahead = products_of(units[0])
    for i, (low, head) in enumerate(units):
        high = min(low + chunk, keys)
        scores, grad_probs = ahead
        if i + 1 < len(units):
            ahead = products_of(units[i + 1])
        if allowed is not None:
            scores = jnp.where(allowed[low:high], scores, -1e30)
        probs = jnp.exp(scores - logs[head : head + 1])
        grad_scores = (probs * (grad_probs - dots[head])).astype(jnp.bfloat16)
        probs_ref[head, low:high] = probs.astype(jnp.bfloat16)
        scores_ref[head, low:high] = grad_scores
        half = head % 2 * HEAD
        term = bdot(turned[head // 2][half : half + HEAD, low:high], grad_scores, NN)
        total[head] = term if total[head] is None else total[head] + term
    if heads % 2:
        total.append(jnp.zeros_like(total[0]))
    return (jnp.concatenate(total, axis=0).T * score_scale).astype(jnp.bfloat16)


def key_value_grads(query, grad, heads, probs_ref, scores_ref):
    keys, values = [], []
    for first in range(0, heads, 2):
        span = slice(first * HEAD, first * HEAD + LANES)
        made_key = made_value = None
        for head in range(first, min(first + 2, heads)):
            grad_key = bdot(scores_ref[head], query[:, span], NN) * score_scale
            grad_value = bdot(probs_ref[head], grad[:, span], NN)
            pick = head_pick(grad_key.shape, head)
            made_key = jnp.where(pick, grad_key, 0.0 if made_key is None else made_key)
            made_value = jnp.where(pick, grad_value, 0.0 if made_value is None else made_value)
        keys.append(made_key.astype(jnp.bfloat16))
        values.append(made_value.astype(jnp.bfloat16))
    return jnp.concatenate(keys, axis=1), jnp.concatenate(values, axis=1)


def cross_backward_kernel(
    rank, query, key, value, grad, mixed, logs, grad_query, grad_key, grad_value, probs_ref, scores_ref, *, heads, chunk
):
    grad_query[0] = backward_heads(
        query[0], key[0, 0], value[0, 0], grad[0], mixed[0], logs[0, 0], None, heads, chunk, probs_ref, scores_ref
    )

    @pl.when(pl.program_id(1) == rank[0])
    def _():
        made = key_value_grads(query[0], grad[0], heads, probs_ref, scores_ref)
        grad_key[0], grad_value[0] = made


def self_backward_kernel(
    rank, query, key, value, grad, mixed, logs, seg_col, seg_row, stamp_col, out, probs_ref, scores_ref, *, heads, chunk
):
    rows = query.shape[1]
    key_at = lax.broadcasted_iota(jnp.int32, (rows, rows), 0)
    at = lax.broadcasted_iota(jnp.int32, (rows, rows), 1)
    allowed = (key_at <= at) & (seg_col[0] == seg_row[0]) & ((stamp_col[0] == 0) | (key_at == at))
    grad_query = backward_heads(
        query[0], key[0], value[0], grad[0], mixed[0], logs[0, 0], allowed, heads, chunk, probs_ref, scores_ref
    )
    grad_key, grad_value = key_value_grads(query[0], grad[0], heads, probs_ref, scores_ref)
    out[0] = jnp.concatenate([grad_query, grad_key, grad_value], axis=1)


def slot_spec(rows, offset):
    return pl.BlockSpec((1, rows, SLOT), lambda b, r: (b, 0, offset + r))


def major_spec(rows, offset):
    return pl.BlockSpec((1, 1, rows, SLOT), lambda b, r: (offset + r, b, 0, 0))


def self_forward(qkv, seg_col, seg_row, stamp_row, ranks, heads, chunk=448):
    seqs, rows, _ = qkv.shape
    col = pl.BlockSpec((1, rows, 1), lambda b, r: (b, 0, 0))
    row = pl.BlockSpec((1, 1, rows), lambda b, r: (b, 0, 0))
    return pl.pallas_call(
        functools.partial(self_forward_kernel, heads=heads, chunk=chunk),
        grid=(seqs, ranks),
        in_specs=[slot_spec(rows, 0), slot_spec(rows, ranks), slot_spec(rows, 2 * ranks), col, row, row],
        out_specs=[slot_spec(rows, 0), pl.BlockSpec((1, 1, 8, rows), lambda b, r: (b, r, 0, 0))],
        out_shape=[
            jax.ShapeDtypeStruct((seqs, rows, ranks * SLOT), jnp.bfloat16),
            jax.ShapeDtypeStruct((seqs, ranks, 8, rows), jnp.float32),
        ],
        compiler_params=pltpu.CompilerParams(vmem_limit_bytes=VM),
        name="self_forward",
    )(qkv, qkv, qkv, seg_col, seg_row, stamp_row)


def cross_forward(queries, keys_values, ranks, heads, chunk=448):
    seqs, rows, _ = queries.shape
    frames = keys_values.shape[2]
    return pl.pallas_call(
        functools.partial(cross_forward_kernel, heads=heads, chunk=chunk),
        grid=(seqs, ranks),
        in_specs=[slot_spec(rows, 0), major_spec(frames, 0), major_spec(frames, ranks)],
        out_specs=[slot_spec(rows, 0), pl.BlockSpec((1, 1, 8, rows), lambda b, r: (b, r, 0, 0))],
        out_shape=[
            jax.ShapeDtypeStruct((seqs, rows, ranks * SLOT), jnp.bfloat16),
            jax.ShapeDtypeStruct((seqs, ranks, 8, rows), jnp.float32),
        ],
        compiler_params=pltpu.CompilerParams(vmem_limit_bytes=VM),
        name="cross_forward",
    )(queries, keys_values, keys_values)


def ranked_spec(rows, offset):
    return pl.BlockSpec((1, rows, SLOT), lambda b, r, rank: (b, 0, offset + r))


def cross_backward(rank, queries, keys_values, grads, mixed, logs, ranks, heads, chunk=512):
    seqs, rows, _ = queries.shape
    frames = keys_values.shape[2]
    kept = pl.BlockSpec((1, frames, SLOT), lambda b, r, rank: (b, 0, 0))
    bf = jnp.bfloat16
    return pl.pallas_call(
        functools.partial(cross_backward_kernel, heads=heads, chunk=chunk),
        grid_spec=pltpu.PrefetchScalarGridSpec(
            num_scalar_prefetch=1,
            grid=(seqs, ranks),
            in_specs=[
                ranked_spec(rows, 0), pl.BlockSpec((1, 1, frames, SLOT), lambda b, r, rank: (r, b, 0, 0)),
                pl.BlockSpec((1, 1, frames, SLOT), lambda b, r, rank: (ranks + r, b, 0, 0)), ranked_spec(rows, 0), ranked_spec(rows, 0),
                pl.BlockSpec((1, 1, 8, rows), lambda b, r, rank: (b, r, 0, 0)),
            ],
            out_specs=[ranked_spec(rows, 0), kept, kept],
            scratch_shapes=[pltpu.VMEM((heads, frames, rows), bf), pltpu.VMEM((heads, frames, rows), bf)],
        ),
        out_shape=[
            jax.ShapeDtypeStruct((seqs, rows, ranks * SLOT), bf),
            jax.ShapeDtypeStruct((seqs, frames, SLOT), bf),
            jax.ShapeDtypeStruct((seqs, frames, SLOT), bf),
        ],
        compiler_params=pltpu.CompilerParams(vmem_limit_bytes=VM),
        name="cross_backward",
    )(rank, queries, keys_values, keys_values, grads, mixed, logs)


def self_backward(rank, qkv, grads, mixed, logs, seg_col, seg_row, stamp_col, ranks, heads, chunk=224):
    seqs, rows, _ = qkv.shape
    bf = jnp.bfloat16
    own = lambda offset: pl.BlockSpec((1, rows, SLOT), lambda b, rank: (b, 0, offset + rank[0]))
    col = pl.BlockSpec((1, rows, 1), lambda b, rank: (b, 0, 0))
    row = pl.BlockSpec((1, 1, rows), lambda b, rank: (b, 0, 0))
    return pl.pallas_call(
        functools.partial(self_backward_kernel, heads=heads, chunk=chunk),
        grid_spec=pltpu.PrefetchScalarGridSpec(
            num_scalar_prefetch=1,
            grid=(seqs,),
            in_specs=[
                own(0), own(ranks), own(2 * ranks), own(0), own(0),
                pl.BlockSpec((1, 1, 8, rows), lambda b, rank: (b, rank[0], 0, 0)), col, row, col,
            ],
            out_specs=pl.BlockSpec((1, rows, 3 * SLOT), lambda b, rank: (b, 0, 0)),
            scratch_shapes=[pltpu.VMEM((heads, rows, rows), bf), pltpu.VMEM((heads, rows, rows), bf)],
        ),
        out_shape=jax.ShapeDtypeStruct((seqs, rows, 3 * SLOT), bf),
        compiler_params=pltpu.CompilerParams(vmem_limit_bytes=VM),
        name="self_backward",
    )(rank, qkv, qkv, qkv, grads, mixed, logs, seg_col, seg_row, stamp_col)


def pack_kernel(tiles, line, out):
    side = tiles.shape[1]
    half, extra = side // 2, side - LANES
    for i in range(tiles.shape[0]):
        tile = tiles[i].astype(jnp.bfloat16)
        low = i * (side + half)
        out[low : low + side] = tile[:, :LANES]
        out[low + side : low + side + half] = jnp.concatenate([tile[:half, LANES:], tile[half:, LANES:]], axis=1)
    out[out.shape[0] - line.shape[0] :] = line[...].astype(jnp.bfloat16)


def pack(tiles, line):
    count, side, _ = tiles.shape
    rows = count * (side + side // 2) + line.shape[0]
    return pl.pallas_call(
        pack_kernel, out_shape=jax.ShapeDtypeStruct((rows, LANES), jnp.bfloat16), name="pack"
    )(tiles, line)


def gather_blocks(block, ranks, groups, ready):
    if ranks != 4 or groups != 8:
        return [lax.all_gather(block, ("dp", "tensor"), axis=0)], None, None, ready

    def flip(values, bits):
        return lax.ppermute(values, "dp", [(i, i ^ bits) for i in range(groups)])

    def turn(values, step):
        return lax.ppermute(values, "tensor", [(i, (i + step) % ranks) for i in range(ranks)])

    cut = block.shape[0] // 32 * 16
    one, three = turn(block, 1), turn(block, 3)
    held = block[None]
    sides = flip(held, 2), flip(held, 4)
    later, _ = lax.optimization_barrier((block, sides))
    two = turn(later, 2)
    units, before = [(0, held, sides)], sides
    for step, values in ((1, one), (3, three), (2, two)):
        if step == 1:
            values, ready = lax.optimization_barrier((values, ready))
        held, _ = lax.optimization_barrier((values[None], before))
        before = flip(held, 2), flip(held, 4)
        units.append((step, held, before))
    arrays, where = [], []
    for step, held, (across, along) in units:
        low, high = flip(across[:, :cut], 4), flip(along[:, cut:], 2)
        even = jnp.concatenate([held, across, along, jnp.concatenate([low, high], axis=1)], axis=0)
        for parity, array in enumerate((even, flip(even, 1))):
            arrays.append(array)
            where.append([(step, 2 * k + parity) for k in range(4)])
    return arrays, where, two, ready


def assemble_kernel(target, *refs, sources, own_tiles, tile_rows):
    ins, outs = refs[:sources], refs[sources : sources + 13]
    staging, (f_qkv, f_ckv, f_cq, f_wo, f_co, *f_wide), arrived, sent = refs[sources + 13], refs[sources + 14 : -2], refs[-2], refs[-1]
    side = tile_rows * 2 // 3
    half = side // 2
    at = 0
    for source in ins:
        blocks = source.shape[0]

        def fetch(k, _, source=source, at=at):
            for slot in range(own_tiles):
                pltpu.make_async_copy(
                    source.at[k, pl.ds(slot * tile_rows, tile_rows)],
                    staging.at[target[at + k * own_tiles + slot]],
                    arrived,
                ).start()
            return 0

        lax.fori_loop(0, blocks, fetch, 0)
        at += blocks * own_tiles
    pltpu.make_async_copy(staging, staging, arrived).wait()

    def parts(rank, ident):
        packed = staging.at[rank * 64 + ident]
        low = packed[side:]
        return packed[:side], jnp.concatenate([low[:, : side - LANES], low[:, side - LANES :]], axis=0)

    def columns(out, base, offset):
        for rank in range(4):
            for i in range(4):
                main, rest = parts(rank, base + i)
                rest = jnp.concatenate([rest, jnp.zeros((side, SLOT - side), jnp.bfloat16)], axis=1)
                out[i * side : (i + 1) * side, offset + rank * SLOT : offset + (rank + 1) * SLOT] = jnp.concatenate([main, rest], axis=1)

    def joined(rank, base):
        pieces = []
        for i in range(4):
            pieces.extend(parts(rank, base + i))
        return jnp.concatenate(pieces, axis=1)

    def padded_rows(out, base):
        for rank in range(4):
            out[rank * SLOT : rank * SLOT + side, :] = joined(rank, base)
            out[rank * SLOT + side : (rank + 1) * SLOT, :] = jnp.zeros((SLOT - side, 4 * side), jnp.bfloat16)

    copies = []

    def send(i, held):
        copy = pltpu.make_async_copy(held, outs[i], sent.at[i])
        copy.start()
        copies.append(copy)

    for m, base in enumerate((0, 4, 8)):
        columns(f_qkv, base, m * 4 * SLOT)
    send(0, f_qkv)
    for m, base in enumerate((16, 20)):
        columns(f_ckv, base, m * 4 * SLOT)
    send(1, f_ckv)
    columns(f_cq, 12, 0)
    send(2, f_cq)
    padded_rows(f_wo, 24)
    send(3, f_wo)
    padded_rows(f_co, 28)
    send(4, f_co)
    for m, base in enumerate((32, 48)):
        for rank in range(4):
            held = f_wide[m * 4 + rank]
            for i in range(4):
                held[i * side : (i + 1) * side] = joined(rank, base + 4 * i)
            send(5 + m * 4 + rank, held)
    for copy in copies:
        copy.wait()


def assemble(target, arrays, own_tiles, side):
    width = 4 * side
    tile_rows = side + side // 2
    bf = jnp.bfloat16
    shapes = [
        (width, 12 * SLOT), (width, 8 * SLOT), (width, 4 * SLOT), (4 * SLOT, width), (4 * SLOT, width),
    ] + [(width, width)] * 8
    anywhere = pl.BlockSpec(memory_space=pl.ANY)
    return pl.pallas_call(
        functools.partial(assemble_kernel, sources=len(arrays), own_tiles=own_tiles, tile_rows=tile_rows),
        grid_spec=pltpu.PrefetchScalarGridSpec(
            num_scalar_prefetch=1,
            grid=(1,),
            in_specs=[anywhere] * len(arrays),
            out_specs=[anywhere] * 13,
            scratch_shapes=[pltpu.VMEM((256, tile_rows, LANES), bf)]
            + [pltpu.VMEM(shape, bf) for shape in shapes]
            + [pltpu.SemaphoreType.DMA, pltpu.SemaphoreType.DMA((13,))],
        ),
        out_shape=[jax.ShapeDtypeStruct(shape, bf) for shape in shapes],
        compiler_params=pltpu.CompilerParams(vmem_limit_bytes=56 * 2**20),
        name="assemble",
    )(target, *arrays)


def weight_grads_kernel(
    rank, slot, sub, *refs, side, owned
):
    sources, lines, out, held, arrived = refs[: len(owned)], refs[len(owned)], refs[len(owned) + 1], refs[len(owned) + 2 : -1], refs[-1]
    copies = []
    for i, (source, to, own) in enumerate(zip(sources, held, owned)):
        if own:
            wide = to.shape[-1]
            source = source.at[:, pl.ds(pl.multiple_of(rank[0] * wide, LANES), wide)]
        copies.append(pltpu.make_async_copy(source, to, arrived.at[i]))
        copies[-1].start()

    def take(*which):
        for i in which:
            copies[i].wait()
        return [held[i] for i in which]

    half = side // 2
    tile_rows = side + half

    def keep(tile, ident):
        tile = tile.astype(jnp.bfloat16)
        at = pl.multiple_of(sub[ident] * tile_rows, 32)
        out[slot[ident], pl.ds(at, side)] = tile[:, :LANES]
        rest = tile[:, LANES:]
        out[slot[ident], pl.ds(at + side, half)] = jnp.concatenate([rest[:half], rest[half:]], axis=1)

    def slots(made, bases):
        for m, base in enumerate(bases):
            for i in range(4):
                keep(made[i * side : (i + 1) * side, m * SLOT : m * SLOT + side], base + i)

    def grid_of(made, base, rows):
        for i in range(rows):
            for j in range(4):
                keep(made[i * side : (i + 1) * side, j * side : (j + 1) * side], base + i * 4 + j)

    n3, grad_up = take(0, 1)
    grid_of(bdot(n3[...], grad_up[...], TN), 32, 4)
    active, b3 = take(2, 3)
    grid_of(bdot(active[...], b3[...], TN), 48, 4)
    mixed, b2 = take(4, 5)
    grid_of(bdot(mixed[...], b2[...], TN), 28, 1)
    frames, dk, dv = take(6, 7, 8)
    slots(bdot(frames[0], dk[0], TN) + bdot(frames[1], dk[1], TN), (16,))
    slots(bdot(frames[0], dv[0], TN) + bdot(frames[1], dv[1], TN), (20,))
    n2, dcq = take(9, 10)
    slots(bdot(n2[...], dcq[...], TN), (12,))
    attended, b1 = take(11, 12)
    grid_of(bdot(attended[...], b1[...], TN), 24, 1)
    n1, dqkv = take(13, 14)
    slots(bdot(n1[...], dqkv[...], TN), (0, 4, 8))
    for i in range(out.shape[0]):
        out[i, out.shape[1] - lines.shape[1] :] = lines[i].astype(jnp.bfloat16)


def weight_grads(rank, slot, sub, side, groups, own_tiles, lines, n1, dqkv, n2, dcq, frames, dk, dv, attended, b1, mixed, b2, n3, grad_up, active, b3):
    wide = 4 * side
    inputs = [n3, grad_up, active, b3, mixed, b2, frames, dk, dv, n2, dcq, attended, b1, n1, dqkv]
    widths = [0, wide, wide, 0, SLOT, 0, 0, 0, 0, 0, SLOT, SLOT, 0, 0, 0]
    owned = [0 < size < x.shape[-1] for x, size in zip(inputs, widths)]
    shapes = [(x.shape[0], size) if own else x.shape for x, size, own in zip(inputs, widths, owned)]
    shape = (groups, own_tiles * (side + side // 2) + lines.shape[1], LANES)
    return pl.pallas_call(
        functools.partial(weight_grads_kernel, side=side, owned=owned),
        grid_spec=pltpu.PrefetchScalarGridSpec(
            num_scalar_prefetch=3,
            grid=(1,),
            in_specs=[pl.BlockSpec(memory_space=pl.ANY)] * len(inputs)
            + [pl.BlockSpec(lines.shape, lambda i, rank, slot, sub: (0, 0, 0))],
            out_specs=pl.BlockSpec(shape, lambda i, rank, slot, sub: (0, 0, 0)),
            scratch_shapes=[pltpu.VMEM(size, jnp.bfloat16) for size in shapes] + [pltpu.SemaphoreType.DMA((len(inputs),))],
        ),
        out_shape=jax.ShapeDtypeStruct(shape, jnp.bfloat16),
        compiler_params=pltpu.CompilerParams(vmem_limit_bytes=60 * 2**20),
        name="weight_grads",
    )(rank, slot, sub, *inputs, lines)


def scatter_blocks(blocks, ranks, groups):
    f32, bf16 = jnp.float32, jnp.bfloat16
    if groups != 8:
        return lax.psum_scatter(blocks, "dp", scatter_dimension=0, tiled=True)[0].astype(f32)

    def sent(values, bits):
        return lax.ppermute(values.astype(bf16), "dp", [(i, i ^ bits) for i in range(groups)]).astype(f32)

    half = groups // 2
    cut = blocks.shape[1] // 32 * 16
    chip = (blocks[:half].astype(f32) + sent(blocks[half:], 1)).astype(bf16)
    low, high = chip[:, :cut], chip[:, cut:]
    low_x, high_y = sent(jnp.stack([low[1], low[3]]), 2), sent(high[2:], 4)
    low = jnp.stack([low[0], low[2]]).astype(f32) + low_x
    high = high[:2].astype(f32) + high_y
    low_y, high_x = sent(low[1], 4), sent(high[1], 2)
    return jnp.concatenate([low[0] + low_y, high[0] + high_x], axis=0)


def first_back_kernel(rank, dqkv, query_weight, key_weight, value_weight, hidden, out, sums, own_sums):
    weights = jnp.concatenate([query_weight[...], key_weight[...], value_weight[...]], axis=1)
    made = bdot(dqkv[...], weights, NT)
    unit, _ = unit_rows(hidden[0].astype(jnp.float32))
    sums[0:1] = jnp.sum(made * unit, axis=0, keepdims=True)
    sums[1:2] = jnp.sum(made, axis=0, keepdims=True)
    own_sums[...] = jnp.sum(dqkv[...].astype(jnp.float32), axis=0, keepdims=True)
    out[...] = made.astype(jnp.bfloat16)


def first_back(rank, dqkv, weight, hidden, ranks):
    _, tokens, width = hidden.shape
    own = lambda offset: pl.BlockSpec((width, SLOT), lambda i, rank: (0, offset + rank[0]))
    whole = lambda shape: pl.BlockSpec(shape, lambda i, rank: (0, 0))
    return pl.pallas_call(
        first_back_kernel,
        grid_spec=pltpu.PrefetchScalarGridSpec(
            num_scalar_prefetch=1,
            grid=(1,),
            in_specs=[whole(dqkv.shape), own(0), own(ranks), own(2 * ranks), pl.BlockSpec((1, tokens, width), lambda i, rank: (0, 0, 0))],
            out_specs=[whole((tokens, width)), whole((2, width)), whole((1, dqkv.shape[1]))],
        ),
        out_shape=[
            jax.ShapeDtypeStruct((tokens, width), jnp.bfloat16), jax.ShapeDtypeStruct((2, width), jnp.float32),
            jax.ShapeDtypeStruct((1, dqkv.shape[1]), jnp.float32),
        ],
        compiler_params=pltpu.CompilerParams(vmem_limit_bytes=VM),
        name="first_back",
    )(rank, dqkv, weight, weight, weight, hidden)


def frames_kernel(frames, weight, bias, out):
    for i in range(out.shape[0]):
        span = slice(i * SLOT, (i + 1) * SLOT)
        out[i, 0] = (bdot(frames[0], weight[:, span], NN) + bias[i]).astype(jnp.bfloat16)


def frame_projection(frames, weight, bias):
    seqs, count, width = frames.shape
    slots = weight.shape[1] // SLOT
    return pl.pallas_call(
        frames_kernel,
        grid=(seqs, slots // 4),
        in_specs=[
            pl.BlockSpec((1, count, width), lambda b, c: (b, 0, 0)),
            pl.BlockSpec((width, 4 * SLOT), lambda b, c: (0, c)),
            pl.BlockSpec((4, 1, SLOT), lambda b, c: (c, 0, 0)),
        ],
        out_specs=pl.BlockSpec((4, 1, count, SLOT), lambda b, c: (c, b, 0, 0)),
        out_shape=jax.ShapeDtypeStruct((slots, seqs, count, SLOT), jnp.bfloat16),
        compiler_params=pltpu.CompilerParams(vmem_limit_bytes=VM),
        name="frame_projection",
    )(frames, weight, bias.reshape(slots, 1, SLOT))


def frames_back_kernel(rank, dk, dv, key_weight, value_weight, out, *, parts):
    made = bdot(dk[0], key_weight[...], NT) + bdot(dv[0], value_weight[...], NT)
    share = made.shape[0] // parts
    for part in range(parts):
        piece = made[part * share : (part + 1) * share]
        out[part, 0] = jnp.concatenate([piece, jnp.zeros((out.shape[2] - share, piece.shape[1]), jnp.float32)], axis=0).astype(jnp.bfloat16)


def frames_back(rank, dk, dv, weight, parts):
    seqs, count, slot = dk.shape
    width = weight.shape[0]
    padded = -(-(count // parts) // 16) * 16
    own = pl.BlockSpec((1, count, slot), lambda b, rank: (b, 0, 0))
    return pl.pallas_call(
        functools.partial(frames_back_kernel, parts=parts),
        grid_spec=pltpu.PrefetchScalarGridSpec(
            num_scalar_prefetch=1,
            grid=(seqs,),
            in_specs=[
                own, own,
                pl.BlockSpec((width, slot), lambda b, rank: (0, rank[0])),
                pl.BlockSpec((width, slot), lambda b, rank: (0, parts + rank[0])),
            ],
            out_specs=pl.BlockSpec((parts, 1, padded, width), lambda b, rank: (0, b, 0, 0)),
        ),
        out_shape=jax.ShapeDtypeStruct((parts, seqs, padded, width), jnp.bfloat16),
        compiler_params=pltpu.CompilerParams(vmem_limit_bytes=VM),
        name="frames_back",
    )(rank, dk, dv, weight, weight)


def product(left_part, right_part):
    return jnp.dot(left_part, right_part, preferred_element_type=jnp.float32)


def times_transpose(left_part, right_part):
    return lax.dot_general(left_part, right_part, (NT, ((), ())), preferred_element_type=jnp.float32)


def unit_rows(values):
    centre = jnp.mean(values, axis=-1, keepdims=True)
    centred = values - centre
    inverse = lax.rsqrt(jnp.mean(centred * centred, axis=-1, keepdims=True) + norm_eps)
    return centred * inverse, inverse


def normalize(values, gain, shift):
    return unit_rows(values)[0] * gain + shift


def normalize_back(values, gain, grads):
    unit, inverse = unit_rows(values)
    scaled = grads * gain
    result = inverse * (
        scaled
        - jnp.mean(scaled, axis=-1, keepdims=True)
        - unit * jnp.mean(scaled * unit, axis=-1, keepdims=True)
    )
    return result, jnp.sum(grads * unit, axis=0), jnp.sum(grads, axis=0)


def gelu_pair(value):
    size = jnp.abs(value) * 0.7071067811865476
    bell = jnp.exp(-size * size)
    t = 1.0 / (1.0 + 0.3275911 * size)
    poly = t * (0.254829592 + t * (-0.284496736 + t * (1.421413741 + t * (-1.453152027 + t * 1.061405429))))
    tail = 0.5 * poly * bell
    level = jnp.where(value >= 0, 1.0 - tail, tail)
    return value * level, level + value * bell * 0.3989422804014327


def middle_kernel(rank, *refs, parts):
    mixed, first_sum, top_grad, vectors, inner_bias, c_o = refs[:6]
    w_in, w_out = refs[6 : 6 + parts], refs[6 + parts : 6 + 2 * parts]
    (
        block_out, grad_out, grad_mixed, n3_out, b2_out, b3_out, active_out, up_out, sums, up_sums, acts, slopes, ups,
    ) = refs[6 + 2 * parts :]
    f32, bf16 = jnp.float32, jnp.bfloat16
    width = first_sum.shape[1]
    row = lambda i: vectors[i : i + 1]
    cut = lambda i: slice(i * width, (i + 1) * width)
    fold = lambda values: jnp.sum(values, axis=0, keepdims=True)

    def back(unit, inverse, scaled):
        centre = jnp.mean(scaled, axis=-1, keepdims=True)
        return inverse * (scaled - centre - unit * jnp.mean(scaled * unit, axis=-1, keepdims=True))

    second_sum = first_sum[...] + bdot(mixed[...], c_o[...], NN) + row(9)
    unit, inverse = unit_rows(second_sum)
    n3 = (unit * row(4) + row(5)).astype(bf16)
    n3_out[...] = n3
    third_sum = second_sum + row(10)
    for i in range(parts):
        value, slope = gelu_pair(bdot(n3, w_in[i][...], NN) + inner_bias[:, cut(i)])
        acts[i] = value.astype(bf16)
        slopes[i] = slope.astype(bf16)
        third_sum = third_sum + bdot(acts[i], w_out[i][...], NN)
    active_out[...] = acts[rank[0]]
    last, last_inverse = unit_rows(third_sum)
    block_out[...] = last * row(6) + row(7)
    grads = top_grad[0].astype(f32)
    grad_third = back(last, last_inverse, grads * row(6))
    b3 = grad_third.astype(bf16)
    b3_out[...] = b3
    grad_normed, ups_now = None, []
    for i in range(parts):
        grad_up = (bdot(b3, w_out[i][...], NT) * slopes[i].astype(f32)).astype(bf16)
        ups[i] = grad_up
        ups_now.append(fold(grad_up.astype(f32)))
        term = bdot(grad_up, w_in[i][...], NT)
        grad_normed = term if grad_normed is None else grad_normed + term
    up_out[...] = ups[rank[0]]
    grad_second = grad_third + back(unit, inverse, grad_normed * row(4))
    grad_out[...] = grad_second
    b2 = grad_second.astype(bf16)
    b2_out[...] = b2
    grad_mixed[...] = bdot(b2, c_o[...], NT).astype(bf16)
    now = jnp.concatenate(
        [
            fold(grad_normed * unit), fold(grad_normed), fold(grads * last), fold(grads),
            fold(b2.astype(f32)), fold(b3.astype(f32)), jnp.zeros((2, width), f32),
        ],
        axis=0,
    )
    ups_all = jnp.concatenate(ups_now, axis=0)
    start = pl.program_id(0) == 0

    @pl.when(start)
    def _():
        sums[...] = now
        up_sums[...] = ups_all

    @pl.when(jnp.logical_not(start))
    def _():
        sums[...] += now
        up_sums[...] += ups_all


def middle(rank, mixed, first_sum, top_grad, c_o, w_in, w_out, vectors, inner_bias, block=448):
    f32, bf16 = jnp.float32, jnp.bfloat16
    tokens, width = first_sum.shape
    slots, parts = mixed.shape[1], len(w_in)
    rows = lambda size: pl.BlockSpec((block, size), lambda i, rank: (i, 0))
    once = lambda x: pl.BlockSpec(x.shape, lambda i, rank: (0, 0), pipeline_mode=pl.Buffered(1))
    total = lambda count: pl.BlockSpec((count, width), lambda i, rank: (0, 0))
    out = lambda size, kind: jax.ShapeDtypeStruct((tokens, size), kind)
    fixed = [vectors, inner_bias, c_o, *w_in, *w_out]
    return pl.pallas_call(
        functools.partial(middle_kernel, parts=parts),
        grid_spec=pltpu.PrefetchScalarGridSpec(
            num_scalar_prefetch=1,
            grid=(tokens // block,),
            in_specs=[rows(slots), rows(width), pl.BlockSpec((1, block, width), lambda i, rank: (1, i, 0))]
            + [once(x) for x in fixed],
            out_specs=[rows(width), rows(width), rows(slots)] + [rows(width)] * 5 + [total(8), total(parts)],
            scratch_shapes=[pltpu.VMEM((parts, block, width), bf16)] * 3,
        ),
        out_shape=[out(width, f32), out(width, f32), out(slots, bf16)]
        + [out(width, bf16)] * 5
        + [jax.ShapeDtypeStruct((8, width), f32), jax.ShapeDtypeStruct((parts, width), f32)],
        compiler_params=pltpu.CompilerParams(vmem_limit_bytes=VM),
        name="middle",
    )(rank, mixed, first_sum, top_grad, *fixed)


def first_kernel(hidden, vectors, bias, weight, n1, out):
    made = (unit_rows(hidden[0].astype(jnp.float32))[0] * vectors[0:1] + vectors[1:2]).astype(jnp.bfloat16)
    n1[...] = made
    for low in range(0, weight.shape[1], 4 * SLOT):
        span = slice(low, low + 4 * SLOT)
        out[:, span] = (bdot(made, weight[:, span], NN) + bias[:, span]).astype(jnp.bfloat16)


def first_projections(both, vectors, bias, weight, block=448):
    _, tokens, width = both.shape
    wide = weight.shape[1]
    once = lambda x: pl.BlockSpec(x.shape, lambda i: (0, 0), pipeline_mode=pl.Buffered(1))
    return pl.pallas_call(
        first_kernel,
        grid=(tokens // block,),
        in_specs=[pl.BlockSpec((1, block, width), lambda i: (0, i, 0)), once(vectors), once(bias), once(weight)],
        out_specs=[pl.BlockSpec((block, width), lambda i: (i, 0)), pl.BlockSpec((block, wide), lambda i: (i, 0))],
        out_shape=[jax.ShapeDtypeStruct((tokens, width), jnp.bfloat16), jax.ShapeDtypeStruct((tokens, wide), jnp.bfloat16)],
        compiler_params=pltpu.CompilerParams(vmem_limit_bytes=VM),
        name="first_projections",
    )(both, vectors, bias, weight)


def spread_heads(rows, ranks):
    lead = rows.shape[0]
    side = rows.shape[1] // ranks
    return jnp.pad(rows.reshape(lead, ranks, side), ((0, 0), (0, 0), (0, SLOT - side))).reshape(lead, ranks * SLOT)


def shards(
    hidden_in, frames, cotangent, segments, stamps, owner_list, master_tiles, tile_first, tile_second,
    tile_stats, tile_bases, master_vectors, vector_first, vector_second,
):
    f32, bf16 = jnp.float32, jnp.bfloat16
    ranks, groups = lax.axis_size("tensor"), lax.axis_size("dp")
    rank, group = lax.axis_index("tensor"), lax.axis_index("dp")
    seqs, local_rows, width = hidden_in.shape
    rows = local_rows * ranks
    tokens = seqs * rows
    own_tiles, side = master_tiles.shape[1], master_tiles.shape[-1]
    heads = side // HEAD
    rank_ref = rank.astype(jnp.int32)[None]

    length = master_vectors.shape[0]
    line_rows = -(-length // (16 * LANES)) * 16
    line = jnp.pad(master_vectors, (0, line_rows * LANES - length)).reshape(line_rows, LANES)
    block = pack(master_tiles[0], line)
    ready = soap_pre(tile_first[0], tile_stats[0], tile_bases[0])
    frames = with_layout_constraint(frames, Layout(major_to_minor=(0, 1, 2)))
    arrays, where, last, (ready, frames) = gather_blocks(block, ranks, groups, (ready, frames))
    if where is None:
        source_rank = jnp.tile(jnp.arange(ranks, dtype=jnp.int32), groups)
        source_group = jnp.repeat(jnp.arange(groups, dtype=jnp.int32), ranks)
        lines = arrays[0].reshape(groups, ranks, -1, LANES)[:, 0, -line_rows:].reshape(groups, -1)[:, :length]
    else:
        steps = jnp.array([step for array in where for step, _ in array], jnp.int32)
        bits = jnp.array([bit for array in where for _, bit in array], jnp.int32)
        source_rank = (rank - steps) % ranks
        source_group = group ^ bits
        lines = jnp.concatenate([array[:, -line_rows:] for array in arrays[:2]], axis=0).reshape(groups, -1)[:, :length]
        spots = source_group[:groups]
        order = jnp.arange(groups, dtype=jnp.int32)
        lines = jnp.sum(jnp.where((spots[None] == order[:, None])[:, :, None], lines[None].astype(f32), 0.0), axis=1)
    vectors = lines.astype(f32).reshape(19, width)

    count = owner_list.shape[0]
    position = jnp.arange(count, dtype=jnp.int32)
    place = jnp.sum(jnp.where(owner_list[None, :] == position[:, None], position[None, :], 0), axis=1)
    spot = (source_group[:, None] * own_tiles + jnp.arange(own_tiles, dtype=jnp.int32)[None]).reshape(-1)
    ident = jnp.sum(jnp.where(spot[:, None] == position[None, :], owner_list[None, :], 0), axis=1)
    target = jnp.repeat(source_rank, own_tiles) * count + ident
    w_qkv, c_kv, c_q, w_o, c_o, *wide = assemble(target, arrays, own_tiles, side)
    w_in, w_out = wide[:4], wide[4:]

    rows_in = jnp.stack([hidden_in, cotangent])
    if where is not None:
        rows_in, _ = lax.optimization_barrier((rows_in, last))
    both = lax.all_gather(rows_in, "tensor", axis=2, tiled=True)
    both = both.reshape(2, tokens, width)
    hidden = both[0].astype(f32)

    head_bias = spread_heads(vectors[11:15], ranks)
    none = jnp.zeros_like(head_bias[0])
    inner_bias = vectors[15:19].reshape(-1)
    seg_col, seg_row = segments[:, :, None], segments[:, None, :]
    stamp_col, stamp_row = stamps[:, :, None], stamps[:, None, :]

    def split(values):
        return values.reshape(seqs, rows, values.shape[-1])

    def flat(values):
        return values.reshape(tokens, values.shape[-1])

    def own_rows(values):
        return lax.dynamic_slice_in_dim(split(values), rank * local_rows, local_rows, axis=1)

    keys_values = frame_projection(frames, c_kv, jnp.concatenate([none, head_bias[3]]))
    n1, qkv = first_projections(both, vectors, jnp.concatenate([head_bias[0], none, head_bias[1]])[None], w_qkv)
    qkv = split(qkv)
    attended, self_logs = self_forward(qkv, seg_col, seg_row, stamp_row, ranks, heads)
    attended = flat(attended)
    first_sum = hidden + product(attended, w_o) + vectors[8]
    n2 = normalize(first_sum, vectors[2], vectors[3]).astype(bf16)
    cross_queries = split((product(n2, c_q) + head_bias[2]).astype(bf16))
    mixed, cross_logs = cross_forward(cross_queries, keys_values, ranks, heads)
    mixed = flat(mixed)
    out_rows, grad_second, grad_mixed, n3, b2, b3, active, grad_up, sums, up_sum = middle(
        rank_ref, mixed, first_sum, both, c_o, w_in, w_out, vectors, inner_bias[None]
    )
    block_out = own_rows(out_rows)
    grad_mixed = split(grad_mixed)
    dcq, dk, dv = cross_backward(
        rank_ref, cross_queries, keys_values, grad_mixed, split(mixed), cross_logs, ranks, heads
    )
    dcq = flat(dcq)
    frames_part = frames_back(rank_ref, dk, dv, c_kv, ranks)
    dcq, frames_part = lax.optimization_barrier((dcq, frames_part))
    frames_sum = lax.psum_scatter(
        frames_part.reshape(ranks * seqs, frames_part.shape[2], width), "tensor", scatter_dimension=0, tiled=True
    )
    frames_grad = frames_sum[:, : frames.shape[1] // ranks].astype(f32)
    back, gain_two, shift_two = normalize_back(first_sum, vectors[2], times_transpose(dcq, c_q))
    grad_first = grad_second + back
    b1 = grad_first.astype(bf16)
    grad_attended = split(times_transpose(b1, w_o).astype(bf16))
    dqkv = flat(
        self_backward(
            rank_ref, qkv, grad_attended, split(attended), self_logs, seg_col, seg_row, stamp_col, ranks, heads
        )
    )

    part_one, first_sums, dqkv_sum = first_back(rank_ref, dqkv, w_qkv, both, ranks)
    grad_one = lax.psum_scatter(split(part_one), "tensor", scatter_dimension=1, tiled=True).astype(f32)
    back, _, _ = normalize_back(
        hidden_in.astype(f32).reshape(-1, width), vectors[0], grad_one.reshape(-1, width)
    )
    input_grad = own_rows(grad_first) + back.reshape(hidden_in.shape)

    def total(values):
        return jnp.sum(values.astype(f32), axis=tuple(range(values.ndim - 1)))

    same = jnp.stack(
        [gain_two, shift_two, sums[0], sums[1], sums[2], sums[3], total(b1), sums[4], sums[5]]
    )
    query_sum = total(dcq).reshape(ranks, SLOT)[:, :side].reshape(1, width)
    even = 1.0 / ranks
    dqkv_sum = dqkv_sum[0]
    own_sums = jnp.stack([dqkv_sum[:side], dqkv_sum[2 * SLOT : 2 * SLOT + side], total(dv)[:side]])
    own_sums = lax.dynamic_update_slice(jnp.zeros((3, width), f32), own_sums, (0, rank * side))
    vector_terms = jnp.concatenate(
        [first_sums, same * even, own_sums[:2], query_sum * even, own_sums[2:], up_sum * even]
    )
    lines = vector_terms.reshape(groups, length)
    owner = place // own_tiles
    if groups == 8:
        bits = owner ^ group
        slot = (bits & 1) * (groups // 2) + (bits >> 1)
        at = jnp.arange(groups, dtype=jnp.int32)
        wanted = group ^ (2 * (at % (groups // 2)) + at // (groups // 2))
        lines = jnp.sum(jnp.where((wanted[:, None] == at[None])[:, :, None], lines[None], 0.0), axis=1)
    else:
        slot = owner
    lines = jnp.pad(lines, ((0, 0), (0, line_rows * LANES - length))).reshape(groups, line_rows, LANES)
    blocks = weight_grads(
        rank_ref, slot, place % own_tiles, side, groups, own_tiles, lines,
        n1, dqkv, n2, dcq, frames, dk, dv, attended, b1, mixed, b2, n3, grad_up, active, b3,
    )
    owned = scatter_blocks(blocks, ranks, groups)
    line = owned[-line_rows:]
    new_first, new_second, new_master, new_stats, new_bases = soap(
        owned, master_tiles[0], tile_first[0], tile_second[0], tile_stats[0], tile_bases[0], *ready
    )
    reach = 1
    while reach < ranks:
        other = lax.ppermute(line, "tensor", [(i, i ^ reach) for i in range(ranks)])
        other, _ = lax.optimization_barrier((other, new_second if reach == 1 else new_bases))
        line = line + other
        reach *= 2
    vector_grad = line.reshape(-1)[:length]
    new_vector_first = beta_one * vector_first + (1.0 - beta_one) * vector_grad
    new_vector_second = beta_two * vector_second + (1.0 - beta_two) * vector_grad * vector_grad
    new_vectors = master_vectors - rate_vectors * (new_vector_first / (1.0 - beta_one**STEP)) / (
        jnp.sqrt(new_vector_second / (1.0 - beta_two**STEP)) + adam_eps
    )
    return (
        block_out, input_grad, frames_grad, new_master[None], new_first[None], new_second[None],
        new_stats[None], new_bases[None], new_vectors, new_vector_first, new_vector_second,
    )


def solution(mesh):
    rows, seqs, tiles, pairs = (
        P("dp", "tensor", None), P("dp", None), P("tensor", "dp", None, None), P("tensor", "dp", None, None, None)
    )
    line = P("dp")
    in_specs = (
        rows, P("dp", None, None), rows, seqs, seqs, P(), tiles, tiles, tiles, pairs, pairs, line, line, line
    )
    out_specs = (rows, rows, rows, tiles, tiles, tiles, pairs, pairs, line, line, line)
    return jax.shard_map(shards, mesh=mesh, in_specs=in_specs, out_specs=out_specs, check_vma=False)
```

```python
import functools

import jax
import jax.numpy as jnp
from jax import lax
from jax.experimental import pallas as pl
from jax.experimental.pallas import tpu as pltpu
from jax.experimental.layout import Layout, with_layout_constraint
from jax.sharding import PartitionSpec as P

HEAD = 64
FF = 3072
STEP = 5
LANES = 128
SLOT = 256
VM = 56 * 2**20
HI = lax.Precision.HIGHEST

norm_eps = 1e-05
beta_one = 0.9
beta_two = 0.95
adam_eps = 1e-08
rate_tiles = 0.05
rate_vectors = 0.3
score_scale = 0.125


def split2(a):
    hi = a.astype(jnp.bfloat16)
    lo = (a - hi.astype(jnp.float32)).astype(jnp.bfloat16)
    return hi, lo

def bdot(a, b, dims):
    return lax.dot_general(a, b, (dims, ((), ())), preferred_element_type=jnp.float32)

NN = ((1,), (0,)); TN = ((0,), (0,)); NT = ((1,), (1,))

def dot3(a, b, dims):
    (ah, al), (bh, bl) = a, b
    return bdot(ah, bh, dims) + (bdot(ah, bl, dims) + bdot(al, bh, dims))

def dothi(a, b, dims):
    return lax.dot_general(a, b, (dims, ((), ())), precision=HI, preferred_element_type=jnp.float32)

def soap_pre_kernel(first, stats, bases, rot_first, stats_rot):
    ql, qr = split2(bases[0, 0]), split2(bases[0, 1])
    inner = split2(dot3(ql, split2(first[0]), TN))
    rot_first[0] = dot3(inner, qr, NN)
    stats_rot[0, 0] = dot3(split2(stats[0, 0]), ql, NN)
    stats_rot[0, 1] = dot3(split2(stats[0, 1]), qr, NN)

def soap_main_kernel(grad, master, first, second, stats, bases, rot_first, stats_rot,
                     new_master, new_first, new_second, new_stats, turned, grams):
    side = master.shape[1]
    rest = grad[side:]
    rest = jnp.concatenate([rest[:, : side - LANES], rest[:, side - LANES :]], axis=0)
    g32 = jnp.concatenate([grad[:side], rest], axis=1)
    g, ql, qr = split2(g32), split2(bases[0, 0]), split2(bases[0, 1])
    new_first[0] = beta_one * first[0] + (1.0 - beta_one) * g32
    part_left = split2(dot3(ql, g, TN))
    rotated = dot3(part_left, qr, NN)
    fresh = beta_two * second[0] + (1.0 - beta_two) * rotated * rotated
    new_second[0] = fresh
    moment = (beta_one * rot_first[0] + (1.0 - beta_one) * rotated) / (1.0 - beta_one**STEP)
    step = moment / (jnp.sqrt(fresh / (1.0 - beta_two**STEP)) + adam_eps)
    back = split2(dot3(ql, split2(step), NN))
    new_master[0] = master[0] - rate_tiles * dot3(back, qr, NT)
    new_stats[0, 0] = beta_two * stats[0, 0] + (1.0 - beta_two) * dot3(g, g, NT)
    new_stats[0, 1] = beta_two * stats[0, 1] + (1.0 - beta_two) * dot3(g, g, TN)
    part_right = split2(dot3(g, qr, NN))
    for side, term in ((0, dot3(g, part_left, NT)), (1, dot3(g, part_right, TN))):
        side_turned = beta_two * stats_rot[0, side] + (1.0 - beta_two) * term
        turned[0, side] = side_turned
        halves = split2(side_turned)
        grams[0, side] = dot3(halves, halves, TN)

def chol_kernel(turned, grams, out, work, fac, *, block, unroll, passes):
    count, side = work.shape[0], work.shape[1]
    wide = work.shape[2] // 2
    for m in range(count):
        work[m, :, :side] = grams[m]
        work[m, :, side:wide] = jnp.zeros((side, wide - side), jnp.float32)
        work[m, :, wide : wide + side] = turned[m].T
        work[m, :, wide + side :] = jnp.zeros((side, wide - side), jnp.float32)
    brow = lax.broadcasted_iota(jnp.int32, (count, block, 2 * block), 1)
    bcol = lax.broadcasted_iota(jnp.int32, (count, block, 2 * block), 2)
    aug_eye = ((bcol - block) == brow).astype(jnp.float32)
    for k in range(side // block):
        lo, hi = k * block, (k + 1) * block
        diag = work[:, lo:hi, lo:hi]
        w = jnp.concatenate([diag, jnp.zeros_like(diag)], axis=2) + aug_eye
        for j in range(block - 1):
            piv = w[:, j : j + 1, :]
            ratio = w[:, :, j : j + 1] / w[:, j : j + 1, j : j + 1]
            w = w - jnp.where(brow > j, ratio * piv, 0.0)
        d = jnp.sum(jnp.where(brow == bcol, w, 0.0), axis=2, keepdims=True)
        fac[...] = w[:, :, block:] * lax.rsqrt(d)

        def several(i, _):
            for u in range(unroll):
                m = i * unroll + u
                if passes == 6:
                    y = dothi(fac[m], work[m, lo:hi, :], NN)
                else:
                    y = dot3(split2(fac[m]), split2(work[m, lo:hi, :]), NN)
                work[m, lo:hi, :] = y
                if hi < side:
                    turn = y[:, :side].T[hi:]
                    if passes == 6:
                        step = dothi(turn, y, NN)
                    else:
                        step = dot3(split2(turn), split2(y), NN)
                    work[m, hi:, :] = work[m, hi:, :] - step
            return 0
        lax.fori_loop(0, count // unroll, several, 0)
    for m in range(count):
        out[m] = work[m, :, wide : wide + side].T

def tile_spec(side):
    return pl.BlockSpec((1, side, side), lambda i: (i, 0, 0))
def pair_spec(side):
    return pl.BlockSpec((1, 2, side, side), lambda i: (i, 0, 0, 0))

def soap_pre(first, stats, bases):
    n, side = first.shape[0], first.shape[1]
    t, p = tile_spec(side), pair_spec(side)
    return pl.pallas_call(soap_pre_kernel, grid=(n,), in_specs=[t, p, p], out_specs=[t, p],
        out_shape=[jax.ShapeDtypeStruct(first.shape, jnp.float32), jax.ShapeDtypeStruct(stats.shape, jnp.float32)],
        name="soap_pre")(first, stats, bases)

def soap_main(grad, master, first, second, stats, bases, rot_first, stats_rot):
    n, side = first.shape[0], first.shape[1]
    t, p = tile_spec(side), pair_spec(side)
    f = jnp.float32
    ts, ps = jax.ShapeDtypeStruct(first.shape, f), jax.ShapeDtypeStruct(stats.shape, f)
    return pl.pallas_call(soap_main_kernel, grid=(n,), in_specs=[pl.BlockSpec((side + side // 2, LANES), lambda i: (i, 0)), t, t, t, p, p, t, p],
        out_specs=[t, t, t, p, p, p], out_shape=[ts, ts, ts, ps, ps, ps], name="soap_main")(
        grad, master, first, second, stats, bases, rot_first, stats_rot)

def chol_bases(turned, grams, block=64, unroll=8, passes=3):
    n, _, side, _ = turned.shape
    shape = (2 * n, side, side)
    unroll = min(unroll, 2 * n)
    out = pl.pallas_call(functools.partial(chol_kernel, block=block, unroll=unroll, passes=passes),
        out_shape=jax.ShapeDtypeStruct(shape, jnp.float32),
        scratch_shapes=[pltpu.VMEM((2 * n, side, 512), jnp.float32), pltpu.VMEM((2*n, block, block), jnp.float32)],
        compiler_params=pltpu.CompilerParams(vmem_limit_bytes=48 * 2**20), name="chol_bases")(
        turned.reshape(shape), grams.reshape(shape))
    return out.reshape(turned.shape)


def soap(gradient, master, first, second, statistics, bases, rot_first, stats_rot):
    nm, nf, ns, nst, turned, grams = soap_main(gradient, master, first, second, statistics, bases, rot_first, stats_rot)
    return nf, ns, nm, nst, chol_bases(turned, grams)


def head_pick(shape, head):
    lane = lax.broadcasted_iota(jnp.int32, shape, len(shape) - 1)
    return (lane >= HEAD) if head % 2 else (lane < HEAD)


def forward_heads(query, key, value, allowed, heads, chunk):
    rows = query.shape[0]
    units = [(low, head) for low in range(0, rows, chunk) for head in range(heads)]
    spans = [slice(head // 2 * LANES, head // 2 * LANES + LANES) for head in range(heads)]
    own_values = []
    for head in range(heads):
        block = value[:, spans[head]]
        own_values.append(jnp.where(head_pick(block.shape, head), block, jnp.ones_like(block)))

    def scores_of(unit):
        low, head = unit
        block = query[low : low + chunk, spans[head]]
        own = jnp.where(head_pick(block.shape, head), block, jnp.zeros_like(block)) * jnp.bfloat16(score_scale)
        return bdot(own, key[:, spans[head]], NT)

    done, logs = {}, {}
    ahead = scores_of(units[0])
    for i, (low, head) in enumerate(units):
        scores = ahead
        if i + 1 < len(units):
            ahead = scores_of(units[i + 1])
        if allowed is not None:
            scores = jnp.where(allowed[low : low + chunk], scores, -1e30)
        top = jnp.max(scores, axis=1, keepdims=True)
        weights = jnp.exp(scores - top).astype(jnp.bfloat16)
        both = bdot(weights, own_values[head], NN)
        turned = pltpu.roll(both, HEAD, 1)
        pick = head_pick(both.shape, head)
        done[low, head] = both / turned
        logs[low, head] = top + jnp.log(jnp.where(pick, turned, both))
    columns, lines = [], []
    for low in range(0, rows, chunk):
        blocks = []
        lane = lax.broadcasted_iota(jnp.int32, (chunk, LANES), 1)
        line = jnp.zeros((chunk, LANES), jnp.float32)
        for first in range(0, heads, 2):
            other = done[low, first + 1] if first + 1 < heads else 0.0
            blocks.append(jnp.where(lane < HEAD, done[low, first], other).astype(jnp.bfloat16))
        for head in range(heads):
            line = jnp.where(lane == head, logs[low, head], line)
        columns.append(jnp.concatenate(blocks, axis=1))
        lines.append(line)
    return jnp.concatenate(columns, axis=0), jnp.concatenate(lines, axis=0).T[:8]


def cross_forward_kernel(query, key, value, out, logs, *, heads, chunk):
    out[0], logs[0, 0] = forward_heads(query[0], key[0, 0], value[0, 0], None, heads, chunk)


def self_forward_kernel(query, key, value, seg_col, seg_row, stamp_row, out, logs, *, heads, chunk):
    rows = query.shape[1]
    at = lax.broadcasted_iota(jnp.int32, (rows, rows), 0)
    key_at = lax.broadcasted_iota(jnp.int32, (rows, rows), 1)
    allowed = (key_at <= at) & (seg_col[0] == seg_row[0]) & ((stamp_row[0] == 0) | (key_at == at))
    out[0], logs[0, 0] = forward_heads(query[0], key[0], value[0], allowed, heads, chunk)


def backward_heads(query, key, value, grad, mixed, logs, allowed, heads, chunk, probs_ref, scores_ref):
    keys = key.shape[0]
    spans = [slice(head // 2 * LANES, head // 2 * LANES + LANES) for head in range(heads)]
    products = (grad.astype(jnp.float32) * mixed.astype(jnp.float32)).T
    own_query, own_grad, turned, dots, total = [], [], [], [], [None] * heads
    for head in range(heads):
        pick = head_pick((query.shape[0], LANES), head)
        zero = jnp.zeros((query.shape[0], LANES), jnp.bfloat16)
        own_query.append(jnp.where(pick, query[:, spans[head]], zero) * jnp.bfloat16(score_scale))
        own_grad.append(jnp.where(pick, grad[:, spans[head]], zero))
        dots.append(jnp.sum(products[head * HEAD : (head + 1) * HEAD], axis=0, keepdims=True))
        if head % 2 == 0:
            turned.append(key[:, spans[head]].T)
    units = [(low, head) for low in range(0, keys, chunk) for head in range(heads)]

    def products_of(unit):
        low, head = unit
        high = min(low + chunk, keys)
        return bdot(key[low:high, spans[head]], own_query[head], NT), bdot(value[low:high, spans[head]], own_grad[head], NT)

    ahead = products_of(units[0])
    for i, (low, head) in enumerate(units):
        high = min(low + chunk, keys)
        scores, grad_probs = ahead
        if i + 1 < len(units):
            ahead = products_of(units[i + 1])
        if allowed is not None:
            scores = jnp.where(allowed[low:high], scores, -1e30)
        probs = jnp.exp(scores - logs[head : head + 1])
        grad_scores = (probs * (grad_probs - dots[head])).astype(jnp.bfloat16)
        probs_ref[head, low:high] = probs.astype(jnp.bfloat16)
        scores_ref[head, low:high] = grad_scores
        half = head % 2 * HEAD
        term = bdot(turned[head // 2][half : half + HEAD, low:high], grad_scores, NN)
        total[head] = term if total[head] is None else total[head] + term
    if heads % 2:
        total.append(jnp.zeros_like(total[0]))
    return (jnp.concatenate(total, axis=0).T * score_scale).astype(jnp.bfloat16)


def key_value_grads(query, grad, heads, probs_ref, scores_ref):
    keys, values = [], []
    for first in range(0, heads, 2):
        span = slice(first * HEAD, first * HEAD + LANES)
        made_key = made_value = None
        for head in range(first, min(first + 2, heads)):
            grad_key = bdot(scores_ref[head], query[:, span], NN) * score_scale
            grad_value = bdot(probs_ref[head], grad[:, span], NN)
            pick = head_pick(grad_key.shape, head)
            made_key = jnp.where(pick, grad_key, 0.0 if made_key is None else made_key)
            made_value = jnp.where(pick, grad_value, 0.0 if made_value is None else made_value)
        keys.append(made_key.astype(jnp.bfloat16))
        values.append(made_value.astype(jnp.bfloat16))
    return jnp.concatenate(keys, axis=1), jnp.concatenate(values, axis=1)


def cross_backward_kernel(
    rank, query, key, value, grad, mixed, logs, grad_query, grad_key, grad_value, probs_ref, scores_ref, *, heads, chunk
):
    grad_query[0] = backward_heads(
        query[0], key[0, 0], value[0, 0], grad[0], mixed[0], logs[0, 0], None, heads, chunk, probs_ref, scores_ref
    )

    @pl.when(pl.program_id(1) == rank[0])
    def _():
        made = key_value_grads(query[0], grad[0], heads, probs_ref, scores_ref)
        grad_key[0], grad_value[0] = made


def self_backward_kernel(
    rank, query, key, value, grad, mixed, logs, seg_col, seg_row, stamp_col, out, probs_ref, scores_ref, *, heads, chunk
):
    rows = query.shape[1]
    key_at = lax.broadcasted_iota(jnp.int32, (rows, rows), 0)
    at = lax.broadcasted_iota(jnp.int32, (rows, rows), 1)
    allowed = (key_at <= at) & (seg_col[0] == seg_row[0]) & ((stamp_col[0] == 0) | (key_at == at))
    grad_query = backward_heads(
        query[0], key[0], value[0], grad[0], mixed[0], logs[0, 0], allowed, heads, chunk, probs_ref, scores_ref
    )
    grad_key, grad_value = key_value_grads(query[0], grad[0], heads, probs_ref, scores_ref)
    out[0] = jnp.concatenate([grad_query, grad_key, grad_value], axis=1)


def slot_spec(rows, offset):
    return pl.BlockSpec((1, rows, SLOT), lambda b, r: (b, 0, offset + r))


def major_spec(rows, offset):
    return pl.BlockSpec((1, 1, rows, SLOT), lambda b, r: (offset + r, b, 0, 0))


def self_forward(qkv, seg_col, seg_row, stamp_row, ranks, heads, chunk=448):
    seqs, rows, _ = qkv.shape
    col = pl.BlockSpec((1, rows, 1), lambda b, r: (b, 0, 0))
    row = pl.BlockSpec((1, 1, rows), lambda b, r: (b, 0, 0))
    return pl.pallas_call(
        functools.partial(self_forward_kernel, heads=heads, chunk=chunk),
        grid=(seqs, ranks),
        in_specs=[slot_spec(rows, 0), slot_spec(rows, ranks), slot_spec(rows, 2 * ranks), col, row, row],
        out_specs=[slot_spec(rows, 0), pl.BlockSpec((1, 1, 8, rows), lambda b, r: (b, r, 0, 0))],
        out_shape=[
            jax.ShapeDtypeStruct((seqs, rows, ranks * SLOT), jnp.bfloat16),
            jax.ShapeDtypeStruct((seqs, ranks, 8, rows), jnp.float32),
        ],
        compiler_params=pltpu.CompilerParams(vmem_limit_bytes=VM),
        name="self_forward",
    )(qkv, qkv, qkv, seg_col, seg_row, stamp_row)


def cross_forward(queries, keys_values, ranks, heads, chunk=448):
    seqs, rows, _ = queries.shape
    frames = keys_values.shape[2]
    return pl.pallas_call(
        functools.partial(cross_forward_kernel, heads=heads, chunk=chunk),
        grid=(seqs, ranks),
        in_specs=[slot_spec(rows, 0), major_spec(frames, 0), major_spec(frames, ranks)],
        out_specs=[slot_spec(rows, 0), pl.BlockSpec((1, 1, 8, rows), lambda b, r: (b, r, 0, 0))],
        out_shape=[
            jax.ShapeDtypeStruct((seqs, rows, ranks * SLOT), jnp.bfloat16),
            jax.ShapeDtypeStruct((seqs, ranks, 8, rows), jnp.float32),
        ],
        compiler_params=pltpu.CompilerParams(vmem_limit_bytes=VM),
        name="cross_forward",
    )(queries, keys_values, keys_values)


def ranked_spec(rows, offset):
    return pl.BlockSpec((1, rows, SLOT), lambda b, r, rank: (b, 0, offset + r))


def cross_backward(rank, queries, keys_values, grads, mixed, logs, ranks, heads, chunk=512):
    seqs, rows, _ = queries.shape
    frames = keys_values.shape[2]
    kept = pl.BlockSpec((1, frames, SLOT), lambda b, r, rank: (b, 0, 0))
    bf = jnp.bfloat16
    return pl.pallas_call(
        functools.partial(cross_backward_kernel, heads=heads, chunk=chunk),
        grid_spec=pltpu.PrefetchScalarGridSpec(
            num_scalar_prefetch=1,
            grid=(seqs, ranks),
            in_specs=[
                ranked_spec(rows, 0), pl.BlockSpec((1, 1, frames, SLOT), lambda b, r, rank: (r, b, 0, 0)),
                pl.BlockSpec((1, 1, frames, SLOT), lambda b, r, rank: (ranks + r, b, 0, 0)), ranked_spec(rows, 0), ranked_spec(rows, 0),
                pl.BlockSpec((1, 1, 8, rows), lambda b, r, rank: (b, r, 0, 0)),
            ],
            out_specs=[ranked_spec(rows, 0), kept, kept],
            scratch_shapes=[pltpu.VMEM((heads, frames, rows), bf), pltpu.VMEM((heads, frames, rows), bf)],
        ),
        out_shape=[
            jax.ShapeDtypeStruct((seqs, rows, ranks * SLOT), bf),
            jax.ShapeDtypeStruct((seqs, frames, SLOT), bf),
            jax.ShapeDtypeStruct((seqs, frames, SLOT), bf),
        ],
        compiler_params=pltpu.CompilerParams(vmem_limit_bytes=VM),
        name="cross_backward",
    )(rank, queries, keys_values, keys_values, grads, mixed, logs)


def self_backward(rank, qkv, grads, mixed, logs, seg_col, seg_row, stamp_col, ranks, heads, chunk=224):
    seqs, rows, _ = qkv.shape
    bf = jnp.bfloat16
    own = lambda offset: pl.BlockSpec((1, rows, SLOT), lambda b, rank: (b, 0, offset + rank[0]))
    col = pl.BlockSpec((1, rows, 1), lambda b, rank: (b, 0, 0))
    row = pl.BlockSpec((1, 1, rows), lambda b, rank: (b, 0, 0))
    return pl.pallas_call(
        functools.partial(self_backward_kernel, heads=heads, chunk=chunk),
        grid_spec=pltpu.PrefetchScalarGridSpec(
            num_scalar_prefetch=1,
            grid=(seqs,),
            in_specs=[
                own(0), own(ranks), own(2 * ranks), own(0), own(0),
                pl.BlockSpec((1, 1, 8, rows), lambda b, rank: (b, rank[0], 0, 0)), col, row, col,
            ],
            out_specs=pl.BlockSpec((1, rows, 3 * SLOT), lambda b, rank: (b, 0, 0)),
            scratch_shapes=[pltpu.VMEM((heads, rows, rows), bf), pltpu.VMEM((heads, rows, rows), bf)],
        ),
        out_shape=jax.ShapeDtypeStruct((seqs, rows, 3 * SLOT), bf),
        compiler_params=pltpu.CompilerParams(vmem_limit_bytes=VM),
        name="self_backward",
    )(rank, qkv, qkv, qkv, grads, mixed, logs, seg_col, seg_row, stamp_col)


def pack_kernel(tiles, line, out):
    side = tiles.shape[1]
    half, extra = side // 2, side - LANES
    for i in range(tiles.shape[0]):
        tile = tiles[i].astype(jnp.bfloat16)
        low = i * (side + half)
        out[low : low + side] = tile[:, :LANES]
        out[low + side : low + side + half] = jnp.concatenate([tile[:half, LANES:], tile[half:, LANES:]], axis=1)
    out[out.shape[0] - line.shape[0] :] = line[...].astype(jnp.bfloat16)


def pack(tiles, line):
    count, side, _ = tiles.shape
    rows = count * (side + side // 2) + line.shape[0]
    return pl.pallas_call(
        pack_kernel, out_shape=jax.ShapeDtypeStruct((rows, LANES), jnp.bfloat16), name="pack"
    )(tiles, line)


def gather_blocks(block, ranks, groups, ready):
    if ranks != 4 or groups != 8:
        return [lax.all_gather(block, ("dp", "tensor"), axis=0)], None, None, ready

    def flip(values, bits):
        return lax.ppermute(values, "dp", [(i, i ^ bits) for i in range(groups)])

    def turn(values, step):
        return lax.ppermute(values, "tensor", [(i, (i + step) % ranks) for i in range(ranks)])

    cut = block.shape[0] // 32 * 16
    one, three = turn(block, 1), turn(block, 3)
    held = block[None]
    sides = flip(held, 2), flip(held, 4)
    later, _ = lax.optimization_barrier((block, sides))
    two = turn(later, 2)
    units, before = [(0, held, sides)], sides
    for step, values in ((1, one), (3, three), (2, two)):
        if step == 1:
            values, ready = lax.optimization_barrier((values, ready))
        held, _ = lax.optimization_barrier((values[None], before))
        before = flip(held, 2), flip(held, 4)
        units.append((step, held, before))
    arrays, where = [], []
    for step, held, (across, along) in units:
        low, high = flip(across[:, :cut], 4), flip(along[:, cut:], 2)
        even = jnp.concatenate([held, across, along, jnp.concatenate([low, high], axis=1)], axis=0)
        for parity, array in enumerate((even, flip(even, 1))):
            arrays.append(array)
            where.append([(step, 2 * k + parity) for k in range(4)])
    return arrays, where, two, ready


def assemble_kernel(target, *refs, sources, own_tiles, tile_rows):
    ins, outs = refs[:sources], refs[sources : sources + 13]
    staging, (f_qkv, f_ckv, f_cq, f_wo, f_co, *f_wide), arrived, sent = refs[sources + 13], refs[sources + 14 : -2], refs[-2], refs[-1]
    side = tile_rows * 2 // 3
    half = side // 2
    at = 0
    for source in ins:
        blocks = source.shape[0]

        def fetch(k, _, source=source, at=at):
            for slot in range(own_tiles):
                pltpu.make_async_copy(
                    source.at[k, pl.ds(slot * tile_rows, tile_rows)],
                    staging.at[target[at + k * own_tiles + slot]],
                    arrived,
                ).start()
            return 0

        lax.fori_loop(0, blocks, fetch, 0)
        at += blocks * own_tiles
    pltpu.make_async_copy(staging, staging, arrived).wait()

    def parts(rank, ident):
        packed = staging.at[rank * 64 + ident]
        low = packed[side:]
        return packed[:side], jnp.concatenate([low[:, : side - LANES], low[:, side - LANES :]], axis=0)

    def columns(out, base, offset):
        for rank in range(4):
            for i in range(4):
                main, rest = parts(rank, base + i)
                rest = jnp.concatenate([rest, jnp.zeros((side, SLOT - side), jnp.bfloat16)], axis=1)
                out[i * side : (i + 1) * side, offset + rank * SLOT : offset + (rank + 1) * SLOT] = jnp.concatenate([main, rest], axis=1)

    def joined(rank, base):
        pieces = []
        for i in range(4):
            pieces.extend(parts(rank, base + i))
        return jnp.concatenate(pieces, axis=1)

    def padded_rows(out, base):
        for rank in range(4):
            out[rank * SLOT : rank * SLOT + side, :] = joined(rank, base)
            out[rank * SLOT + side : (rank + 1) * SLOT, :] = jnp.zeros((SLOT - side, 4 * side), jnp.bfloat16)

    copies = []

    def send(i, held):
        copy = pltpu.make_async_copy(held, outs[i], sent.at[i])
        copy.start()
        copies.append(copy)

    for m, base in enumerate((0, 4, 8)):
        columns(f_qkv, base, m * 4 * SLOT)
    send(0, f_qkv)
    for m, base in enumerate((16, 20)):
        columns(f_ckv, base, m * 4 * SLOT)
    send(1, f_ckv)
    columns(f_cq, 12, 0)
    send(2, f_cq)
    padded_rows(f_wo, 24)
    send(3, f_wo)
    padded_rows(f_co, 28)
    send(4, f_co)
    for m, base in enumerate((32, 48)):
        for rank in range(4):
            held = f_wide[m * 4 + rank]
            for i in range(4):
                held[i * side : (i + 1) * side] = joined(rank, base + 4 * i)
            send(5 + m * 4 + rank, held)
    for copy in copies:
        copy.wait()


def assemble(target, arrays, own_tiles, side):
    width = 4 * side
    tile_rows = side + side // 2
    bf = jnp.bfloat16
    shapes = [
        (width, 12 * SLOT), (width, 8 * SLOT), (width, 4 * SLOT), (4 * SLOT, width), (4 * SLOT, width),
    ] + [(width, width)] * 8
    anywhere = pl.BlockSpec(memory_space=pl.ANY)
    return pl.pallas_call(
        functools.partial(assemble_kernel, sources=len(arrays), own_tiles=own_tiles, tile_rows=tile_rows),
        grid_spec=pltpu.PrefetchScalarGridSpec(
            num_scalar_prefetch=1,
            grid=(1,),
            in_specs=[anywhere] * len(arrays),
            out_specs=[anywhere] * 13,
            scratch_shapes=[pltpu.VMEM((256, tile_rows, LANES), bf)]
            + [pltpu.VMEM(shape, bf) for shape in shapes]
            + [pltpu.SemaphoreType.DMA, pltpu.SemaphoreType.DMA((13,))],
        ),
        out_shape=[jax.ShapeDtypeStruct(shape, bf) for shape in shapes],
        compiler_params=pltpu.CompilerParams(vmem_limit_bytes=56 * 2**20),
        name="assemble",
    )(target, *arrays)


def weight_grads_kernel(
    rank, slot, sub, *refs, side, owned
):
    sources, lines, out, held, arrived = refs[: len(owned)], refs[len(owned)], refs[len(owned) + 1], refs[len(owned) + 2 : -1], refs[-1]
    copies = []
    for i, (source, to, own) in enumerate(zip(sources, held, owned)):
        if own:
            wide = to.shape[-1]
            source = source.at[:, pl.ds(pl.multiple_of(rank[0] * wide, LANES), wide)]
        copies.append(pltpu.make_async_copy(source, to, arrived.at[i]))
        copies[-1].start()

    def take(*which):
        for i in which:
            copies[i].wait()
        return [held[i] for i in which]

    half = side // 2
    tile_rows = side + half

    def keep(tile, ident):
        tile = tile.astype(jnp.bfloat16)
        at = pl.multiple_of(sub[ident] * tile_rows, 32)
        out[slot[ident], pl.ds(at, side)] = tile[:, :LANES]
        rest = tile[:, LANES:]
        out[slot[ident], pl.ds(at + side, half)] = jnp.concatenate([rest[:half], rest[half:]], axis=1)

    def slots(made, bases):
        for m, base in enumerate(bases):
            for i in range(4):
                keep(made[i * side : (i + 1) * side, m * SLOT : m * SLOT + side], base + i)

    def grid_of(made, base, rows):
        for i in range(rows):
            for j in range(4):
                keep(made[i * side : (i + 1) * side, j * side : (j + 1) * side], base + i * 4 + j)

    n3, grad_up = take(0, 1)
    grid_of(bdot(n3[...], grad_up[...], TN), 32, 4)
    active, b3 = take(2, 3)
    grid_of(bdot(active[...], b3[...], TN), 48, 4)
    mixed, b2 = take(4, 5)
    grid_of(bdot(mixed[...], b2[...], TN), 28, 1)
    frames, dk, dv = take(6, 7, 8)
    slots(bdot(frames[0], dk[0], TN) + bdot(frames[1], dk[1], TN), (16,))
    slots(bdot(frames[0], dv[0], TN) + bdot(frames[1], dv[1], TN), (20,))
    n2, dcq = take(9, 10)
    slots(bdot(n2[...], dcq[...], TN), (12,))
    attended, b1 = take(11, 12)
    grid_of(bdot(attended[...], b1[...], TN), 24, 1)
    n1, dqkv = take(13, 14)
    slots(bdot(n1[...], dqkv[...], TN), (0, 4, 8))
    for i in range(out.shape[0]):
        out[i, out.shape[1] - lines.shape[1] :] = lines[i].astype(jnp.bfloat16)


def weight_grads(rank, slot, sub, side, groups, own_tiles, lines, n1, dqkv, n2, dcq, frames, dk, dv, attended, b1, mixed, b2, n3, grad_up, active, b3):
    wide = 4 * side
    inputs = [n3, grad_up, active, b3, mixed, b2, frames, dk, dv, n2, dcq, attended, b1, n1, dqkv]
    widths = [0, wide, wide, 0, SLOT, 0, 0, 0, 0, 0, SLOT, SLOT, 0, 0, 0]
    owned = [0 < size < x.shape[-1] for x, size in zip(inputs, widths)]
    shapes = [(x.shape[0], size) if own else x.shape for x, size, own in zip(inputs, widths, owned)]
    shape = (groups, own_tiles * (side + side // 2) + lines.shape[1], LANES)
    return pl.pallas_call(
        functools.partial(weight_grads_kernel, side=side, owned=owned),
        grid_spec=pltpu.PrefetchScalarGridSpec(
            num_scalar_prefetch=3,
            grid=(1,),
            in_specs=[pl.BlockSpec(memory_space=pl.ANY)] * len(inputs)
            + [pl.BlockSpec(lines.shape, lambda i, rank, slot, sub: (0, 0, 0))],
            out_specs=pl.BlockSpec(shape, lambda i, rank, slot, sub: (0, 0, 0)),
            scratch_shapes=[pltpu.VMEM(size, jnp.bfloat16) for size in shapes] + [pltpu.SemaphoreType.DMA((len(inputs),))],
        ),
        out_shape=jax.ShapeDtypeStruct(shape, jnp.bfloat16),
        compiler_params=pltpu.CompilerParams(vmem_limit_bytes=60 * 2**20),
        name="weight_grads",
    )(rank, slot, sub, *inputs, lines)


def scatter_blocks(blocks, ranks, groups):
    f32, bf16 = jnp.float32, jnp.bfloat16
    if groups != 8:
        return lax.psum_scatter(blocks, "dp", scatter_dimension=0, tiled=True)[0].astype(f32)

    def sent(values, bits):
        return lax.ppermute(values.astype(bf16), "dp", [(i, i ^ bits) for i in range(groups)]).astype(f32)

    half = groups // 2
    cut = blocks.shape[1] // 32 * 16
    chip = (blocks[:half].astype(f32) + sent(blocks[half:], 1)).astype(bf16)
    low, high = chip[:, :cut], chip[:, cut:]
    low_x, high_y = sent(jnp.stack([low[1], low[3]]), 2), sent(high[2:], 4)
    low = jnp.stack([low[0], low[2]]).astype(f32) + low_x
    high = high[:2].astype(f32) + high_y
    low_y, high_x = sent(low[1], 4), sent(high[1], 2)
    return jnp.concatenate([low[0] + low_y, high[0] + high_x], axis=0)


def first_back_kernel(rank, dqkv, query_weight, key_weight, value_weight, hidden, out, sums, own_sums):
    weights = jnp.concatenate([query_weight[...], key_weight[...], value_weight[...]], axis=1)
    made = bdot(dqkv[...], weights, NT)
    unit, _ = unit_rows(hidden[0].astype(jnp.float32))
    sums[0:1] = jnp.sum(made * unit, axis=0, keepdims=True)
    sums[1:2] = jnp.sum(made, axis=0, keepdims=True)
    own_sums[...] = jnp.sum(dqkv[...].astype(jnp.float32), axis=0, keepdims=True)
    out[...] = made.astype(jnp.bfloat16)


def first_back(rank, dqkv, weight, hidden, ranks):
    _, tokens, width = hidden.shape
    own = lambda offset: pl.BlockSpec((width, SLOT), lambda i, rank: (0, offset + rank[0]))
    whole = lambda shape: pl.BlockSpec(shape, lambda i, rank: (0, 0))
    return pl.pallas_call(
        first_back_kernel,
        grid_spec=pltpu.PrefetchScalarGridSpec(
            num_scalar_prefetch=1,
            grid=(1,),
            in_specs=[whole(dqkv.shape), own(0), own(ranks), own(2 * ranks), pl.BlockSpec((1, tokens, width), lambda i, rank: (0, 0, 0))],
            out_specs=[whole((tokens, width)), whole((2, width)), whole((1, dqkv.shape[1]))],
        ),
        out_shape=[
            jax.ShapeDtypeStruct((tokens, width), jnp.bfloat16), jax.ShapeDtypeStruct((2, width), jnp.float32),
            jax.ShapeDtypeStruct((1, dqkv.shape[1]), jnp.float32),
        ],
        compiler_params=pltpu.CompilerParams(vmem_limit_bytes=VM),
        name="first_back",
    )(rank, dqkv, weight, weight, weight, hidden)


def frames_kernel(frames, weight, bias, out):
    for i in range(out.shape[0]):
        span = slice(i * SLOT, (i + 1) * SLOT)
        out[i, 0] = (bdot(frames[0], weight[:, span], NN) + bias[i]).astype(jnp.bfloat16)


def frame_projection(frames, weight, bias):
    seqs, count, width = frames.shape
    slots = weight.shape[1] // SLOT
    return pl.pallas_call(
        frames_kernel,
        grid=(seqs, slots // 4),
        in_specs=[
            pl.BlockSpec((1, count, width), lambda b, c: (b, 0, 0)),
            pl.BlockSpec((width, 4 * SLOT), lambda b, c: (0, c)),
            pl.BlockSpec((4, 1, SLOT), lambda b, c: (c, 0, 0)),
        ],
        out_specs=pl.BlockSpec((4, 1, count, SLOT), lambda b, c: (c, b, 0, 0)),
        out_shape=jax.ShapeDtypeStruct((slots, seqs, count, SLOT), jnp.bfloat16),
        compiler_params=pltpu.CompilerParams(vmem_limit_bytes=VM),
        name="frame_projection",
    )(frames, weight, bias.reshape(slots, 1, SLOT))


def frames_back_kernel(rank, dk, dv, key_weight, value_weight, out, *, parts):
    made = bdot(dk[0], key_weight[...], NT) + bdot(dv[0], value_weight[...], NT)
    share = made.shape[0] // parts
    for part in range(parts):
        piece = made[part * share : (part + 1) * share]
        out[part, 0] = jnp.concatenate([piece, jnp.zeros((out.shape[2] - share, piece.shape[1]), jnp.float32)], axis=0).astype(jnp.bfloat16)


def frames_back(rank, dk, dv, weight, parts):
    seqs, count, slot = dk.shape
    width = weight.shape[0]
    padded = -(-(count // parts) // 16) * 16
    own = pl.BlockSpec((1, count, slot), lambda b, rank: (b, 0, 0))
    return pl.pallas_call(
        functools.partial(frames_back_kernel, parts=parts),
        grid_spec=pltpu.PrefetchScalarGridSpec(
            num_scalar_prefetch=1,
            grid=(seqs,),
            in_specs=[
                own, own,
                pl.BlockSpec((width, slot), lambda b, rank: (0, rank[0])),
                pl.BlockSpec((width, slot), lambda b, rank: (0, parts + rank[0])),
            ],
            out_specs=pl.BlockSpec((parts, 1, padded, width), lambda b, rank: (0, b, 0, 0)),
        ),
        out_shape=jax.ShapeDtypeStruct((parts, seqs, padded, width), jnp.bfloat16),
        compiler_params=pltpu.CompilerParams(vmem_limit_bytes=VM),
        name="frames_back",
    )(rank, dk, dv, weight, weight)


def product(left_part, right_part):
    return jnp.dot(left_part, right_part, preferred_element_type=jnp.float32)


def times_transpose(left_part, right_part):
    return lax.dot_general(left_part, right_part, (NT, ((), ())), preferred_element_type=jnp.float32)


def unit_rows(values):
    centre = jnp.mean(values, axis=-1, keepdims=True)
    centred = values - centre
    inverse = lax.rsqrt(jnp.mean(centred * centred, axis=-1, keepdims=True) + norm_eps)
    return centred * inverse, inverse


def normalize(values, gain, shift):
    return unit_rows(values)[0] * gain + shift


def normalize_back(values, gain, grads):
    unit, inverse = unit_rows(values)
    scaled = grads * gain
    result = inverse * (
        scaled
        - jnp.mean(scaled, axis=-1, keepdims=True)
        - unit * jnp.mean(scaled * unit, axis=-1, keepdims=True)
    )
    return result, jnp.sum(grads * unit, axis=0), jnp.sum(grads, axis=0)


def gelu_pair(value):
    size = jnp.abs(value) * 0.7071067811865476
    bell = jnp.exp(-size * size)
    t = 1.0 / (1.0 + 0.3275911 * size)
    poly = t * (0.254829592 + t * (-0.284496736 + t * (1.421413741 + t * (-1.453152027 + t * 1.061405429))))
    tail = 0.5 * poly * bell
    level = jnp.where(value >= 0, 1.0 - tail, tail)
    return value * level, level + value * bell * 0.3989422804014327


def middle_kernel(rank, *refs, parts):
    mixed, first_sum, top_grad, vectors, inner_bias, c_o = refs[:6]
    w_in, w_out = refs[6 : 6 + parts], refs[6 + parts : 6 + 2 * parts]
    (
        block_out, grad_out, grad_mixed, n3_out, b2_out, b3_out, active_out, up_out, sums, up_sums, acts, slopes, ups,
    ) = refs[6 + 2 * parts :]
    f32, bf16 = jnp.float32, jnp.bfloat16
    width = first_sum.shape[1]
    row = lambda i: vectors[i : i + 1]
    cut = lambda i: slice(i * width, (i + 1) * width)
    fold = lambda values: jnp.sum(values, axis=0, keepdims=True)

    def back(unit, inverse, scaled):
        centre = jnp.mean(scaled, axis=-1, keepdims=True)
        return inverse * (scaled - centre - unit * jnp.mean(scaled * unit, axis=-1, keepdims=True))

    second_sum = first_sum[...] + bdot(mixed[...], c_o[...], NN) + row(9)
    unit, inverse = unit_rows(second_sum)
    n3 = (unit * row(4) + row(5)).astype(bf16)
    n3_out[...] = n3
    third_sum = second_sum + row(10)
    for i in range(parts):
        value, slope = gelu_pair(bdot(n3, w_in[i][...], NN) + inner_bias[:, cut(i)])
        acts[i] = value.astype(bf16)
        slopes[i] = slope.astype(bf16)
        third_sum = third_sum + bdot(acts[i], w_out[i][...], NN)
    active_out[...] = acts[rank[0]]
    last, last_inverse = unit_rows(third_sum)
    block_out[...] = last * row(6) + row(7)
    grads = top_grad[0].astype(f32)
    grad_third = back(last, last_inverse, grads * row(6))
    b3 = grad_third.astype(bf16)
    b3_out[...] = b3
    grad_normed, ups_now = None, []
    for i in range(parts):
        grad_up = (bdot(b3, w_out[i][...], NT) * slopes[i].astype(f32)).astype(bf16)
        ups[i] = grad_up
        ups_now.append(fold(grad_up.astype(f32)))
        term = bdot(grad_up, w_in[i][...], NT)
        grad_normed = term if grad_normed is None else grad_normed + term
    up_out[...] = ups[rank[0]]
    grad_second = grad_third + back(unit, inverse, grad_normed * row(4))
    grad_out[...] = grad_second
    b2 = grad_second.astype(bf16)
    b2_out[...] = b2
    grad_mixed[...] = bdot(b2, c_o[...], NT).astype(bf16)
    now = jnp.concatenate(
        [
            fold(grad_normed * unit), fold(grad_normed), fold(grads * last), fold(grads),
            fold(b2.astype(f32)), fold(b3.astype(f32)), jnp.zeros((2, width), f32),
        ],
        axis=0,
    )
    ups_all = jnp.concatenate(ups_now, axis=0)
    start = pl.program_id(0) == 0

    @pl.when(start)
    def _():
        sums[...] = now
        up_sums[...] = ups_all

    @pl.when(jnp.logical_not(start))
    def _():
        sums[...] += now
        up_sums[...] += ups_all


def middle(rank, mixed, first_sum, top_grad, c_o, w_in, w_out, vectors, inner_bias, block=448):
    f32, bf16 = jnp.float32, jnp.bfloat16
    tokens, width = first_sum.shape
    slots, parts = mixed.shape[1], len(w_in)
    rows = lambda size: pl.BlockSpec((block, size), lambda i, rank: (i, 0))
    once = lambda x: pl.BlockSpec(x.shape, lambda i, rank: (0, 0), pipeline_mode=pl.Buffered(1))
    total = lambda count: pl.BlockSpec((count, width), lambda i, rank: (0, 0))
    out = lambda size, kind: jax.ShapeDtypeStruct((tokens, size), kind)
    fixed = [vectors, inner_bias, c_o, *w_in, *w_out]
    return pl.pallas_call(
        functools.partial(middle_kernel, parts=parts),
        grid_spec=pltpu.PrefetchScalarGridSpec(
            num_scalar_prefetch=1,
            grid=(tokens // block,),
            in_specs=[rows(slots), rows(width), pl.BlockSpec((1, block, width), lambda i, rank: (1, i, 0))]
            + [once(x) for x in fixed],
            out_specs=[rows(width), rows(width), rows(slots)] + [rows(width)] * 5 + [total(8), total(parts)],
            scratch_shapes=[pltpu.VMEM((parts, block, width), bf16)] * 3,
        ),
        out_shape=[out(width, f32), out(width, f32), out(slots, bf16)]
        + [out(width, bf16)] * 5
        + [jax.ShapeDtypeStruct((8, width), f32), jax.ShapeDtypeStruct((parts, width), f32)],
        compiler_params=pltpu.CompilerParams(vmem_limit_bytes=VM),
        name="middle",
    )(rank, mixed, first_sum, top_grad, *fixed)


def first_kernel(hidden, vectors, bias, weight, n1, out):
    made = (unit_rows(hidden[0].astype(jnp.float32))[0] * vectors[0:1] + vectors[1:2]).astype(jnp.bfloat16)
    n1[...] = made
    for low in range(0, weight.shape[1], 4 * SLOT):
        span = slice(low, low + 4 * SLOT)
        out[:, span] = (bdot(made, weight[:, span], NN) + bias[:, span]).astype(jnp.bfloat16)


def first_projections(both, vectors, bias, weight, block=448):
    _, tokens, width = both.shape
    wide = weight.shape[1]
    once = lambda x: pl.BlockSpec(x.shape, lambda i: (0, 0), pipeline_mode=pl.Buffered(1))
    return pl.pallas_call(
        first_kernel,
        grid=(tokens // block,),
        in_specs=[pl.BlockSpec((1, block, width), lambda i: (0, i, 0)), once(vectors), once(bias), once(weight)],
        out_specs=[pl.BlockSpec((block, width), lambda i: (i, 0)), pl.BlockSpec((block, wide), lambda i: (i, 0))],
        out_shape=[jax.ShapeDtypeStruct((tokens, width), jnp.bfloat16), jax.ShapeDtypeStruct((tokens, wide), jnp.bfloat16)],
        compiler_params=pltpu.CompilerParams(vmem_limit_bytes=VM),
        name="first_projections",
    )(both, vectors, bias, weight)


def spread_heads(rows, ranks):
    lead = rows.shape[0]
    side = rows.shape[1] // ranks
    return jnp.pad(rows.reshape(lead, ranks, side), ((0, 0), (0, 0), (0, SLOT - side))).reshape(lead, ranks * SLOT)


def shards(
    hidden_in, frames, cotangent, segments, stamps, owner_list, master_tiles, tile_first, tile_second,
    tile_stats, tile_bases, master_vectors, vector_first, vector_second,
):
    f32, bf16 = jnp.float32, jnp.bfloat16
    ranks, groups = lax.axis_size("tensor"), lax.axis_size("dp")
    rank, group = lax.axis_index("tensor"), lax.axis_index("dp")
    seqs, local_rows, width = hidden_in.shape
    rows = local_rows * ranks
    tokens = seqs * rows
    own_tiles, side = master_tiles.shape[1], master_tiles.shape[-1]
    heads = side // HEAD
    rank_ref = rank.astype(jnp.int32)[None]

    length = master_vectors.shape[0]
    line_rows = -(-length // (16 * LANES)) * 16
    line = jnp.pad(master_vectors, (0, line_rows * LANES - length)).reshape(line_rows, LANES)
    block = pack(master_tiles[0], line)
    ready = soap_pre(tile_first[0], tile_stats[0], tile_bases[0])
    frames = with_layout_constraint(frames, Layout(major_to_minor=(0, 1, 2)))
    arrays, where, last, (ready, frames) = gather_blocks(block, ranks, groups, (ready, frames))
    if where is None:
        source_rank = jnp.tile(jnp.arange(ranks, dtype=jnp.int32), groups)
        source_group = jnp.repeat(jnp.arange(groups, dtype=jnp.int32), ranks)
        lines = arrays[0].reshape(groups, ranks, -1, LANES)[:, 0, -line_rows:].reshape(groups, -1)[:, :length]
    else:
        steps = jnp.array([step for array in where for step, _ in array], jnp.int32)
        bits = jnp.array([bit for array in where for _, bit in array], jnp.int32)
        source_rank = (rank - steps) % ranks
        source_group = group ^ bits
        lines = jnp.concatenate([array[:, -line_rows:] for array in arrays[:2]], axis=0).reshape(groups, -1)[:, :length]
        spots = source_group[:groups]
        order = jnp.arange(groups, dtype=jnp.int32)
        lines = jnp.sum(jnp.where((spots[None] == order[:, None])[:, :, None], lines[None].astype(f32), 0.0), axis=1)
    vectors = lines.astype(f32).reshape(19, width)

    count = owner_list.shape[0]
    position = jnp.arange(count, dtype=jnp.int32)
    place = jnp.sum(jnp.where(owner_list[None, :] == position[:, None], position[None, :], 0), axis=1)
    spot = (source_group[:, None] * own_tiles + jnp.arange(own_tiles, dtype=jnp.int32)[None]).reshape(-1)
    ident = jnp.sum(jnp.where(spot[:, None] == position[None, :], owner_list[None, :], 0), axis=1)
    target = jnp.repeat(source_rank, own_tiles) * count + ident
    w_qkv, c_kv, c_q, w_o, c_o, *wide = assemble(target, arrays, own_tiles, side)
    w_in, w_out = wide[:4], wide[4:]

    rows_in = jnp.stack([hidden_in, cotangent])
    if where is not None:
        rows_in, _ = lax.optimization_barrier((rows_in, last))
    both = lax.all_gather(rows_in, "tensor", axis=2, tiled=True)
    both = both.reshape(2, tokens, width)
    hidden = both[0].astype(f32)

    head_bias = spread_heads(vectors[11:15], ranks)
    none = jnp.zeros_like(head_bias[0])
    inner_bias = vectors[15:19].reshape(-1)
    seg_col, seg_row = segments[:, :, None], segments[:, None, :]
    stamp_col, stamp_row = stamps[:, :, None], stamps[:, None, :]

    def split(values):
        return values.reshape(seqs, rows, values.shape[-1])

    def flat(values):
        return values.reshape(tokens, values.shape[-1])

    def own_rows(values):
        return lax.dynamic_slice_in_dim(split(values), rank * local_rows, local_rows, axis=1)

    keys_values = frame_projection(frames, c_kv, jnp.concatenate([none, head_bias[3]]))
    n1, qkv = first_projections(both, vectors, jnp.concatenate([head_bias[0], none, head_bias[1]])[None], w_qkv)
    qkv = split(qkv)
    attended, self_logs = self_forward(qkv, seg_col, seg_row, stamp_row, ranks, heads)
    attended = flat(attended)
    first_sum = hidden + product(attended, w_o) + vectors[8]
    n2 = normalize(first_sum, vectors[2], vectors[3]).astype(bf16)
    cross_queries = split((product(n2, c_q) + head_bias[2]).astype(bf16))
    mixed, cross_logs = cross_forward(cross_queries, keys_values, ranks, heads)
    mixed = flat(mixed)
    out_rows, grad_second, grad_mixed, n3, b2, b3, active, grad_up, sums, up_sum = middle(
        rank_ref, mixed, first_sum, both, c_o, w_in, w_out, vectors, inner_bias[None]
    )
    block_out = own_rows(out_rows)
    grad_mixed = split(grad_mixed)
    dcq, dk, dv = cross_backward(
        rank_ref, cross_queries, keys_values, grad_mixed, split(mixed), cross_logs, ranks, heads
    )
    dcq = flat(dcq)
    frames_part = frames_back(rank_ref, dk, dv, c_kv, ranks)
    dcq, frames_part = lax.optimization_barrier((dcq, frames_part))
    frames_sum = lax.psum_scatter(
        frames_part.reshape(ranks * seqs, frames_part.shape[2], width), "tensor", scatter_dimension=0, tiled=True
    )
    frames_grad = frames_sum[:, : frames.shape[1] // ranks].astype(f32)
    back, gain_two, shift_two = normalize_back(first_sum, vectors[2], times_transpose(dcq, c_q))
    grad_first = grad_second + back
    b1 = grad_first.astype(bf16)
    grad_attended = split(times_transpose(b1, w_o).astype(bf16))
    dqkv = flat(
        self_backward(
            rank_ref, qkv, grad_attended, split(attended), self_logs, seg_col, seg_row, stamp_col, ranks, heads
        )
    )

    part_one, first_sums, dqkv_sum = first_back(rank_ref, dqkv, w_qkv, both, ranks)
    grad_one = lax.psum_scatter(split(part_one), "tensor", scatter_dimension=1, tiled=True).astype(f32)
    back, _, _ = normalize_back(
        hidden_in.astype(f32).reshape(-1, width), vectors[0], grad_one.reshape(-1, width)
    )
    input_grad = own_rows(grad_first) + back.reshape(hidden_in.shape)

    def total(values):
        return jnp.sum(values.astype(f32), axis=tuple(range(values.ndim - 1)))

    same = jnp.stack(
        [gain_two, shift_two, sums[0], sums[1], sums[2], sums[3], total(b1), sums[4], sums[5]]
    )
    query_sum = total(dcq).reshape(ranks, SLOT)[:, :side].reshape(1, width)
    even = 1.0 / ranks
    dqkv_sum = dqkv_sum[0]
    own_sums = jnp.stack([dqkv_sum[:side], dqkv_sum[2 * SLOT : 2 * SLOT + side], total(dv)[:side]])
    own_sums = lax.dynamic_update_slice(jnp.zeros((3, width), f32), own_sums, (0, rank * side))
    vector_terms = jnp.concatenate(
        [first_sums, same * even, own_sums[:2], query_sum * even, own_sums[2:], up_sum * even]
    )
    lines = vector_terms.reshape(groups, length)
    owner = place // own_tiles
    if groups == 8:
        bits = owner ^ group
        slot = (bits & 1) * (groups // 2) + (bits >> 1)
        at = jnp.arange(groups, dtype=jnp.int32)
        wanted = group ^ (2 * (at % (groups // 2)) + at // (groups // 2))
        lines = jnp.sum(jnp.where((wanted[:, None] == at[None])[:, :, None], lines[None], 0.0), axis=1)
    else:
        slot = owner
    lines = jnp.pad(lines, ((0, 0), (0, line_rows * LANES - length))).reshape(groups, line_rows, LANES)
    blocks = weight_grads(
        rank_ref, slot, place % own_tiles, side, groups, own_tiles, lines,
        n1, dqkv, n2, dcq, frames, dk, dv, attended, b1, mixed, b2, n3, grad_up, active, b3,
    )
    owned = scatter_blocks(blocks, ranks, groups)
    line = owned[-line_rows:]
    new_first, new_second, new_master, new_stats, new_bases = soap(
        owned, master_tiles[0], tile_first[0], tile_second[0], tile_stats[0], tile_bases[0], *ready
    )
    reach = 1
    while reach < ranks:
        other = lax.ppermute(line, "tensor", [(i, i ^ reach) for i in range(ranks)])
        other, _ = lax.optimization_barrier((other, new_second if reach == 1 else new_bases))
        line = line + other
        reach *= 2
    vector_grad = line.reshape(-1)[:length]
    new_vector_first = beta_one * vector_first + (1.0 - beta_one) * vector_grad
    new_vector_second = beta_two * vector_second + (1.0 - beta_two) * vector_grad * vector_grad
    new_vectors = master_vectors - rate_vectors * (new_vector_first / (1.0 - beta_one**STEP)) / (
        jnp.sqrt(new_vector_second / (1.0 - beta_two**STEP)) + adam_eps
    )
    return (
        block_out, input_grad, frames_grad, new_master[None], new_first[None], new_second[None],
        new_stats[None], new_bases[None], new_vectors, new_vector_first, new_vector_second,
    )


def solution(mesh):
    rows, seqs, tiles, pairs = (
        P("dp", "tensor", None), P("dp", None), P("tensor", "dp", None, None), P("tensor", "dp", None, None, None)
    )
    line = P("dp")
    in_specs = (
        rows, P("dp", None, None), rows, seqs, seqs, P(), tiles, tiles, tiles, pairs, pairs, line, line, line
    )
    out_specs = (rows, rows, rows, tiles, tiles, tiles, pairs, pairs, line, line, line)
    return jax.shard_map(shards, mesh=mesh, in_specs=in_specs, out_specs=out_specs, check_vma=False)
```
